32 devices in a mesh: dp: 16 (over z, x, core), tensor: 2 (over y).
Axes of the slice: x: 2, y: 2, z: 4, core: 2. Of those that a mesh axis runs over, the one named last changes fastest.
Arguments:
- hidden: bfloat16 [8192, 768], P('dp'), may hold values from -6 to 6
- lengths: int32 [16], P('dp'), may hold values from 128 to 512, as said below
- attn_in: bfloat16 [3, 768, 768], P(None, None, 'tensor'), may hold values from -0.21875 to 0.21875
- attn_in_bias: bfloat16 [2, 768], P(None, 'tensor'), may hold values from -0.59765625 to 0.59765625
- rel_table: bfloat16 [320, 64], replicated, may hold values from -6 to 6
- attn_out: bfloat16 [768, 768], P('tensor'), may hold values from -2.5 to 2.5
- attn_out_bias: bfloat16 [768], replicated, may hold values from -1 to 1
- norm1_gain: bfloat16 [768], replicated, may hold values from 0.5 to 1.5
- norm1_bias: bfloat16 [768], replicated, may hold values from -1 to 1
- norm2_gain: bfloat16 [768], replicated, may hold values from 0.5 to 1.5
- norm2_bias: bfloat16 [768], replicated, may hold values from -1 to 1
- ffn_in: bfloat16 [768, 3072], P(None, 'tensor'), may hold values from -0.21875 to 0.21875
- ffn_in_bias: bfloat16 [3072], P('tensor'), may hold values from -3 to 3
- ffn_out: bfloat16 [3072, 768], P('tensor'), may hold values from -0.109375 to 0.109375
- ffn_out_bias: bfloat16 [768], replicated, may hold values from -1 to 1
- cotangent: bfloat16 [8192, 768], P('dp'), may hold values from -6 to 6
Outputs:
- output: bfloat16 [8192, 768], P('dp')
- grad_hidden: bfloat16 [8192, 768], P('dp')
- grad_attn_in: float32 [3, 768, 768], P(None, 'dp', 'tensor')
- grad_attn_in_bias: float32 [2, 768], P(None, 'tensor')
- grad_rel_table: float32 [320, 64], replicated
- grad_attn_out: float32 [768, 768], P('tensor', 'dp')
- grad_attn_out_bias: float32 [768], replicated
- grad_norm1_gain: float32 [768], replicated
- grad_norm1_bias: float32 [768], replicated
- grad_norm2_gain: float32 [768], replicated
- grad_norm2_bias: float32 [768], replicated
- grad_ffn_in: float32 [768, 3072], P('dp', 'tensor')
- grad_ffn_in_bias: float32 [3072], P('tensor')
- grad_ffn_out: float32 [3072, 768], P('tensor', 'dp')
- grad_ffn_out_bias: float32 [768], replicated
The draws below stay inside these ranges and needn't reach their ends.
Inputs may be any that keep to these rules, and one draw needn't show every extreme that they name: Each sequence has 512 slots, the first lengths of them frames and the rest padding; speech sequences and shorter text sequences are mixed unevenly, and at least one sequence fills all its slots.
All inputs are finite; a program needn't handle non-finite values.
Results may differ from the reference program's by a relative error of at most 0.013.
Values sent between devices are 32-bit elements; how exact they have to be, the bound alone decides.
A program may use at most 192 MiB of HBM per device.

```python
import math
import jax
import jax.numpy as jnp
from jax import lax

D = 768
HEADS = 12
HD = 64
FF = 3072
MAXREL = 160
NB = 320
SLOT = 512
SEQS = 16
TOKENS = 8192


def draw_lengths(key, part):
    key = jax.random.fold_in(key, 7)
    kind_key, speech_key, text_key, pick_key = jax.random.split(key, 4)
    kinds = jax.random.randint(kind_key, (SEQS,), 0, 2)
    speech = jax.random.randint(speech_key, (SEQS,), SLOT * 5 // 8, SLOT + 1)
    text = jax.random.randint(text_key, (SEQS,), SLOT // 4, SLOT // 2 + 1)
    drawn = jnp.where(kinds > 0, speech, text)
    chosen = jax.random.randint(pick_key, (), 0, SEQS)
    return jnp.where(jnp.arange(SEQS) == chosen, SLOT, drawn).astype(jnp.int32)


def spiked(entries, rng, source, target, shards_of, factor):
    def block_of(dim):
        return (jnp.arange(entries.shape[dim]) // (entries.shape[dim] // shards_of)).reshape((-1,) + (1,) * (entries.ndim - 1 - dim))

    near = jax.random.permutation(rng, shards_of)[block_of(target)]
    other_side = (block_of(target) + shards_of // 2) % shards_of
    return jnp.where((block_of(source) == near) | (block_of(source) == other_side), factor * entries, entries)


def shard_levels(rng, dims, shards, low, top_value):
    def one(dim, shards_of):
        heights = jax.random.uniform(jax.random.fold_in(jax.random.fold_in(rng, 6), dim), (shards_of,), jnp.float32, low / len(shards), top_value / len(shards))
        return jnp.repeat(jnp.exp(heights), dims[dim] // shards_of).reshape((-1,) + (1,) * (len(dims) - dim - 1))

    factor_of = one(*shards[0])
    for cut in shards[1:]:
        factor_of = factor_of * one(*cut)
    return factor_of


def bell_draw(stream_key, shape, width, bound, cuts=(), dtype=jnp.bfloat16):
    values = jax.random.normal(stream_key, shape, jnp.float32) * width
    if len(cuts) > 0:
        values = shard_levels(stream_key, shape, cuts, -0.22, 0.18) * values
    return jnp.clip(values, min=-bound, max=bound).astype(dtype)


def bell_draw_with(stream_key, extent, scale, bound, cuts, heavy, held_as=jnp.bfloat16):
    values = scale * jax.random.normal(stream_key, extent, jnp.float32)
    if cuts:
        values = values * shard_levels(stream_key, extent, cuts, -0.22, 0.18)
    return jnp.clip(spiked(values, jax.random.fold_in(stream_key, 3), *heavy), -bound, bound).astype(held_as)


def setup_inputs(seed: int = 0) -> dict:
    key_of = jax.random.split(jax.random.key(seed), 17)
    hidden = bell_draw_with(key_of[0], (TOKENS, D), 1.0, 6.0, ((0, 16),), (0, 1, 16, 2.0))
    lengths = draw_lengths(jax.random.fold_in(key_of[16], 71), 0)
    attn_in = bell_draw(key_of[2], (3, D, D), D ** -0.5, 0.21875, ((2, 2),))
    attn_in_bias = bell_draw(key_of[3], (2, D), 0.1, 0.59765625, ((1, 2),))
    rel_table = bell_draw(key_of[4], (NB, HD), 1.0, 6.0)
    attn_out = bell_draw(key_of[5], (D, D), (D // 128) ** -0.5, 2.5, ((0, 2),))
    attn_out_bias = bell_draw(key_of[6], (D,), 0.2, 1.0)
    norm1_gain = jnp.clip(1.0 + 0.1 * jax.random.normal(key_of[7], (D,), jnp.float32), 0.5, 1.5).astype(jnp.bfloat16)
    norm1_bias = bell_draw(key_of[8], (D,), 0.2, 1.0)
    norm2_gain = jnp.clip(1.0 + 0.1 * jax.random.normal(key_of[9], (D,), jnp.float32), 0.5, 1.5).astype(jnp.bfloat16)
    norm2_bias = bell_draw(key_of[10], (D,), 0.2, 1.0)
    ffn_in = bell_draw(key_of[11], (D, FF), D ** -0.5, 0.21875, ((1, 2),))
    ffn_in_bias = bell_draw(key_of[12], (FF,), 0.5, 3.0, ((0, 2),))
    ffn_out = bell_draw(key_of[13], (FF, D), FF ** -0.5, 0.109375, ((0, 2),))
    ffn_out_bias = bell_draw(key_of[14], (D,), 0.2, 1.0)
    cotangent = bell_draw_with(key_of[15], (TOKENS, D), 1.0, 6.0, ((0, 16),), (0, 1, 16, 2.0))
    return dict(hidden=hidden, lengths=lengths, attn_in=attn_in, attn_in_bias=attn_in_bias, rel_table=rel_table, attn_out=attn_out, attn_out_bias=attn_out_bias, norm1_gain=norm1_gain, norm1_bias=norm1_bias, norm2_gain=norm2_gain, norm2_bias=norm2_bias, ffn_in=ffn_in, ffn_in_bias=ffn_in_bias, ffn_out=ffn_out, ffn_out_bias=ffn_out_bias, cotangent=cotangent)


@jax.custom_vjp
def low(v):
    return lax.optimization_barrier(v.astype(jnp.bfloat16)).astype(jnp.float32)

@jax.custom_vjp
def low_back(v):
    return v

def low_keep(v):
    return (low(v), None)

def low_pass(kept, grad):
    return (grad,)

def back_keep(v):
    return (v, None)

def back_low(kept, grad):
    return (low(grad),)
low.defvjp(low_keep, low_pass)
low_back.defvjp(back_keep, back_low)

def both_ways(value_in):
    return low_back(low(value_in))

def layer_norm(value_in, gain_value, offset):
    mean_value = lax.optimization_barrier(jnp.mean(value_in, axis=-1, keepdims=True))
    centred = value_in - mean_value
    inv_scale = lax.rsqrt(lax.optimization_barrier(jnp.mean(centred * centred, axis=-1, keepdims=True)) + 1e-05)
    return centred * inv_scale * gain_value + offset

def matmul(former, latter):
    return jnp.einsum('...i,ij->...j', former, latter, precision=lax.Precision.HIGHEST)

def attention(query, keys_in, values_in, valid_keys, position_table, bucket):
    highest = lax.Precision.HIGHEST
    position = low_back(jnp.einsum('gshd,bd->ghsb', query, position_table, precision=highest))
    bucket_map = jnp.broadcast_to(bucket, position.shape[:2] + bucket.shape)
    bias_term = jnp.take_along_axis(position, bucket_map, axis=3)
    scores = jnp.einsum('gshd,gthd->ghst', query, keys_in, precision=highest) + bias_term
    scores = low_back(jnp.where(valid_keys[:, None, None, :] > 0, scores, -1e+30))
    shares = low(jax.nn.softmax(scores, axis=-1))
    return jnp.einsum('ghst,gthd->gshd', shares, values_in, precision=highest)

def layer_group(params, pieces, bucket):
    attn_in, attn_in_bias, rel_table, attn_out, attn_out_bias, norm1_gain, norm1_bias, norm2_gain, norm2_bias, ffn_in, ffn_in_bias, ffn_out, ffn_out_bias = params
    inputs, valid_rows = pieces
    group_count = inputs.shape[0]
    head_shape = (group_count, SLOT, HEADS, HD)
    normed = low(layer_norm(inputs, norm1_gain, norm1_bias))
    query = both_ways((matmul(normed, attn_in[0]) + attn_in_bias[0]) * HD ** (-0.5))
    keys_in = both_ways(matmul(normed, attn_in[1]))
    values_in = both_ways(matmul(normed, attn_in[2]) + attn_in_bias[1])
    context = attention(query.reshape(head_shape), keys_in.reshape(head_shape), values_in.reshape(head_shape), valid_rows, rel_table, bucket)
    context = both_ways(context.reshape(group_count, SLOT, D))
    attended = low_back(matmul(context, attn_out) + attn_out_bias)
    middle = inputs + attended
    normed2 = low(layer_norm(middle, norm2_gain, norm2_bias))
    preact = low_back(matmul(normed2, ffn_in) + ffn_in_bias)
    active = low(jax.nn.gelu(preact, approximate=False))
    branch2 = low_back(matmul(active, ffn_out) + ffn_out_bias)
    return (middle + branch2) * valid_rows[..., None]

def reference(hidden, lengths, attn_in, attn_in_bias, rel_table, attn_out, attn_out_bias, norm1_gain, norm1_bias, norm2_gain, norm2_bias, ffn_in, ffn_in_bias, ffn_out, ffn_out_bias, cotangent):
    slot_iota = lax.broadcasted_iota(jnp.int32, (SEQS, SLOT), 1)
    valid = (slot_iota < lengths[:, None].astype(jnp.int32)).astype(jnp.float32)
    distance = lax.broadcasted_iota(jnp.int32, (SLOT, SLOT), 0) - lax.broadcasted_iota(jnp.int32, (SLOT, SLOT), 1)
    bucket = (jnp.clip(distance, -MAXREL, MAXREL - 1) + MAXREL).astype(jnp.int32)
    group_size = math.gcd(SEQS, max(1, 4096 // SLOT))
    group_total = SEQS // group_size
    params = tuple((item.astype(jnp.float32) for item in (attn_in, attn_in_bias, rel_table, attn_out, attn_out_bias, norm1_gain, norm1_bias, norm2_gain, norm2_bias, ffn_in, ffn_in_bias, ffn_out, ffn_out_bias)))
    valid_groups = valid.reshape(group_total, group_size, SLOT)

    def forward(inputs, *weights):
        grouped = inputs.reshape(group_total, group_size, SLOT, D)
        step_fn = jax.checkpoint(lambda pieces: layer_group(weights, pieces, bucket))
        result = lax.map(step_fn, (grouped, valid_groups))
        return result.reshape(TOKENS, D)
    output, pullback = jax.vjp(forward, hidden.astype(jnp.float32), *params)
    grads = pullback(cotangent.astype(jnp.float32))
    return (output.astype(jnp.bfloat16), grads[0].astype(jnp.bfloat16), grads[1], grads[2], grads[3], grads[4], grads[5], grads[6], grads[7], grads[8], grads[9], grads[10], grads[11], grads[12], grads[13])
```

```python
from functools import partial

import jax
import jax.numpy as jnp
from jax import lax
from jax.experimental import pallas as pl
from jax.experimental.pallas import tpu as pltpu
from jax.sharding import PartitionSpec as P

HD = 64
EPSILON = 1e-05
NEGATIVE = -1e30
SQRT_HALF = 0.7071067811865476
INV_SQRT_2PI = 0.3989422804014327
RB = 128
RF = 256
CW = 384
SLOTS = 4
MESH = pl.DeviceIdType.MESH
F32 = jnp.float32
BF16 = jnp.bfloat16


def mm(a, b):
    return jnp.dot(a, b, preferred_element_type=F32)


def mm_nt(a, b):
    return lax.dot_general(a, b, (((1,), (1,)), ((), ())), preferred_element_type=F32)


def mm_tn(a, b):
    return lax.dot_general(a, b, (((0,), (0,)), ((), ())), preferred_element_type=F32)


def norm_stats(value):
    mean = jnp.mean(value, axis=-1, keepdims=True)
    centred = value - mean
    scale = lax.rsqrt(jnp.mean(centred * centred, axis=-1, keepdims=True) + EPSILON)
    return centred * scale, scale


def norm_back(grad, unit, scale, gain):
    grad_unit = grad * gain
    inner = (
        grad_unit
        - jnp.mean(grad_unit, axis=-1, keepdims=True)
        - unit * jnp.mean(grad_unit * unit, axis=-1, keepdims=True)
    )
    return inner * scale


def col_sum(value):
    return jnp.sum(value, axis=0, keepdims=True)


def lanes_of(ref3, rows):
    return jnp.concatenate([ref3[p, rows, :] for p in range(ref3.shape[0])], axis=1)


V_N1G, V_N1B, V_REL, V_AOB, V_N2G, V_N2B, V_FOB, V_FIB, V_AIB = 0, 6, 16, 176, 182, 188, 194, 200, 212
YROWS, VROWS = 176, 224


def body(
    ring,
    hidden, lengths, attn_in, rel_table, attn_out, vectors_in, ffn_in, ffn_out, cotangent,
    output, grad_hidden, g_attn_in, g_attn_out, g_ffn_in, g_ffn_out, g_vec,
    *scratch,
):
    names = SCRATCH_RING if ring else SCRATCH_PLAIN + ("g_full",)
    s = dict(zip(names, scratch))
    slots, width = hidden.shape
    local = attn_out.shape[0]
    pairs = local // 128
    units = ffn_in.shape[1]
    table_rows = rel_table.shape[0]
    reach = table_rows // 2
    blocks = slots // RB
    ext = slots + RB
    head_scale = HD ** (-0.5)

    dp = lax.axis_index("dp")
    ten = lax.axis_index("tensor")
    y_peer = (dp, 1 - ten)
    if ring:
        core = lax.rem(dp, 2)
        x_at = lax.rem(lax.div(dp, 2), 2)
        z_at = lax.div(dp, 4)
        core_peer = (dp + 1 - 2 * core, ten)
        x_peer = (dp + 2 - 4 * x_at, ten)
        z_peers = [(lax.rem(dp + 4 * d, 16), ten) for d in (1, 2, 3)]
        greet = [y_peer, core_peer, x_peer] + z_peers
    else:
        greet = [y_peer]

    barrier = pltpu.get_barrier_semaphore()
    for peer in greet:
        pl.semaphore_signal(barrier, inc=1, device_id=peer, device_id_type=MESH)
    pl.semaphore_wait(barrier, len(greet))

    def remote(src, dst, name, at, peer):
        return pltpu.make_async_remote_copy(
            src_ref=src, dst_ref=dst, send_sem=s[name + "_s"].at[at], recv_sem=s[name + "_r"].at[at],
            device_id=peer, device_id_type=MESH,
        )

    if ring:
        piece = local // 4
        mine = 2 * x_at + core
        s["wo_stage"][...] = attn_out[pl.ds(pl.multiple_of(mine * piece, 16), piece), :].astype(F32)
        wo_y = remote(s["wo_stage"], s["wo_recv"].at[mine], "wo", 0, y_peer)
        wo_x = remote(s["wo_recv"].at[mine], s["wo_recv"].at[mine], "wo", 1, x_peer)
        other = 2 * (1 - x_at) + core
        wo_c0 = remote(s["wo_recv"].at[mine], s["wo_recv"].at[mine], "wo", 2, core_peer)
        wo_c1 = remote(s["wo_recv"].at[other], s["wo_recv"].at[other], "wo", 3, core_peer)
    else:
        s["wo_stage"][...] = attn_out[...].astype(F32)
        wo_y = remote(s["wo_stage"], s["wo_recv"], "wo", 0, y_peer)
    wo_y.start()

    bias_q = vectors_in[8:9, 0:local]
    bias_v = vectors_in[8:9, local : 2 * local]
    attn_out_bias = vectors_in[0:1, :]
    gain1, offset1 = vectors_in[1:2, :], vectors_in[2:3, :]
    gain2, offset2 = vectors_in[3:4, :], vectors_in[4:5, :]
    ffn_out_bias = vectors_in[5:6, :]
    seq_len = lengths[0]

    ext_rows = 2 * slots
    distance = slots - 1 - lax.broadcasted_iota(jnp.int32, (ext_rows, table_rows), 0)
    bucket = jnp.clip(distance, -reach, reach - 1) + reach
    pick = (bucket == lax.broadcasted_iota(jnp.int32, (ext_rows, table_rows), 1)).astype(BF16)
    rel = rel_table[...]
    s["table"][...] = mm(pick, jnp.concatenate([rel, rel], axis=1)).astype(BF16)

    def project(i, carry):
        rows = pl.ds(pl.multiple_of(i * RF, RF), RF)
        unit, unused = norm_stats(hidden[rows, :].astype(F32))
        normed = (unit * gain1 + offset1).astype(BF16)
        s["normed_t"][i] = normed.T
        q = ((mm(normed, attn_in[0]) + bias_q) * head_scale).astype(BF16)
        k = mm(normed, attn_in[1]).astype(BF16)
        v = (mm(normed, attn_in[2]) + bias_v).astype(BF16)
        for p in range(pairs):
            s["q"][p, rows, :] = q[:, p * 128 : (p + 1) * 128]
            s["k"][p, rows, :] = k[:, p * 128 : (p + 1) * 128]
            s["v"][p, rows, :] = v[:, p * 128 : (p + 1) * 128]
        return carry

    lax.fori_loop(0, slots // RF, project, 0)

    low_lanes = lax.broadcasted_iota(jnp.int32, (RB, 128), 1) < HD
    key_ok = lax.broadcasted_iota(jnp.int32, (1, slots), 1) < seq_len

    def stack(both):
        zero = jnp.zeros_like(both)
        return jnp.concatenate([jnp.where(low_lanes, both, zero), jnp.where(low_lanes, zero, both)], axis=0)

    def unstack(tall):
        return jnp.where(low_lanes, tall[:RB], tall[RB:])

    def table_rows_of(i):
        return pl.ds(pl.multiple_of(slots - RB - i * RB, RB), ext)

    def ctx_copy(i):
        rows = pl.ds(pl.multiple_of(i * RB, RB), RB)
        return remote(s["ctx_send"].at[:, rows], s["ctx_recv"].at[:, rows], "ctx", i, y_peer)

    def attend(i, carry):
        rows = pl.ds(pl.multiple_of(i * RB, RB), RB)

        def pair_step(p, carry):
            qs = stack(s["q"][p, rows, :])
            spread = mm_nt(qs, s["table"][table_rows_of(i), :])
            shift = ext - RB + 1
            bias = jnp.concatenate(
                [
                    pltpu.roll(spread[:RB], shift, 1, stride=1, stride_axis=0)[:, :slots],
                    pltpu.roll(spread[RB:], shift, 1, stride=1, stride_axis=0)[:, :slots],
                ],
                axis=0,
            )
            scores = jnp.where(key_ok, mm_nt(qs, s["k"][p]) + bias, NEGATIVE)
            expon = jnp.exp(scores - jnp.max(scores, axis=-1, keepdims=True))
            shares = (expon * (1.0 / jnp.sum(expon, axis=-1, keepdims=True))).astype(BF16)
            s["probs"][p, i] = shares
            context = unstack(mm(shares, s["v"][p])).astype(BF16)
            s["ctx"][ten * pairs + p, rows, :] = context
            s["ctx_send"][p, rows, :] = context.astype(F32)
            return carry

        lax.fori_loop(0, pairs, pair_step, 0)
        ctx_copy(i).start()
        return carry

    lax.fori_loop(0, blocks, attend, 0)

    half = pl.ds(pl.multiple_of(ten * local, 128), local)
    far_half = pl.ds(pl.multiple_of((1 - ten) * local, 128), local)
    s["wo"][half, :] = attn_out[...]
    wo_y.wait_recv()
    if ring:
        wo_x.start()
        wo_c0.start()
        wo_x.wait_recv()
        wo_c1.start()
        wo_c0.wait_recv()
        wo_c1.wait_recv()
        for k in range(4):
            rows = pl.ds(pl.multiple_of((1 - ten) * local + k * piece, 16), piece)
            s["wo"][rows, :] = s["wo_recv"][k].astype(BF16)
    else:
        s["wo"][far_half, :] = s["wo_recv"][...].astype(BF16)

    def valid_rows(start, count):
        return (lax.broadcasted_iota(jnp.int32, (count, 1), 0) + start < seq_len).astype(F32)

    def sum_copy(name, i):
        rows = pl.ds(pl.multiple_of(i * RB, RB), RB)
        return remote(s[name + "_send"].at[rows], s[name + "_recv"].at[rows], name, i, y_peer)

    g_vec_acc = s["vec"]
    g_vec_acc[...] = jnp.zeros_like(g_vec_acc)
    s["fib"][...] = jnp.zeros_like(s["fib"])
    s["fob"][...] = jnp.zeros_like(s["fob"])
    s["aob"][...] = jnp.zeros_like(s["aob"])
    s["n1"][...] = jnp.zeros_like(s["n1"])
    s["n2"][...] = jnp.zeros_like(s["n2"])

    step_units = 512

    def feed(b, carry):
        start = pl.multiple_of(b * RF, RF)
        rows = pl.ds(start, RF)
        for j in range(RF // RB):
            ctx_copy(b * (RF // RB) + j).wait_recv()
        for p in range(pairs):
            s["ctx"][(1 - ten) * pairs + p, rows, :] = s["ctx_recv"][p, rows, :].astype(BF16)
        attended = mm(lanes_of(s["ctx"], rows), s["wo"][...]) + attn_out_bias
        middle = hidden[rows, :].astype(F32) + attended
        s["middle"][rows, :] = middle
        unit, unused = norm_stats(middle)
        normed = (unit * gain2 + offset2).astype(BF16)
        s["normed2_t"][b] = normed.T
        top = cotangent[rows, :].astype(F32) * valid_rows(start, RF)
        s["fob"][...] += col_sum(top)
        top = top.astype(BF16)
        s["top_t"][b] = top.T
        for c in range(units // step_units):
            cols = slice(c * step_units, (c + 1) * step_units)
            pre = mm(normed, ffn_in[:, cols]) + s["ffn_in_bias"][:, cols]
            share = 0.5 + 0.5 * lax.erf(pre * SQRT_HALF)
            active = (pre * share).astype(BF16)
            s["active"][rows, cols] = active
            slope = share + pre * (jnp.exp(-0.5 * pre * pre) * INV_SQRT_2PI)
            grad_pre = (mm_nt(top, ffn_out[cols, :]) * slope).astype(BF16)
            s["grad_pre"][rows, cols] = grad_pre
            s["fib"][:, cols] += col_sum(grad_pre.astype(F32))
            back = mm_nt(grad_pre, ffn_in[:, cols])
            onward = mm(active, ffn_out[cols, :])
            if c == 0:
                s["gn2_send"][rows, :] = back
                s["out_send"][rows, :] = onward
            else:
                s["gn2_send"][rows, :] += back
                s["out_send"][rows, :] += onward
        for j in range(RF // RB):
            sum_copy("gn2", b * (RF // RB) + j).start()
        return carry

    s["ffn_in_bias"][:, 0:width] = vectors_in[6:7, :]
    s["ffn_in_bias"][:, width : 2 * width] = vectors_in[7:8, :]
    lax.fori_loop(0, slots // RF, feed, 0)

    def grad_chunk(left_t, right):
        total = mm(left_t[0], right[0:RF])
        for b in range(1, slots // RF):
            total += mm(left_t[b], right[b * RF : (b + 1) * RF])
        return total

    ffn_chunks = 2 * units // CW
    attn_chunks = 4

    def keep(total, chunk, slot):
        if ring:
            parts = total.reshape(8, 2, 48, CW)
            even, odd = parts[:, 0], parts[:, 1]
            s["g_own"][chunk] = jnp.where(core == 0, even, odd).reshape(4, 2, 48, CW)
            s["g_send"][slot] = jnp.where(core == 0, odd, even).reshape(4, 2, 48, CW)
            core_copy(chunk, slot).start()
        else:
            s["g_full"][chunk] = total

    def core_copy(chunk, slot):
        return remote(s["g_send"].at[slot], s["core_recv"].at[slot], "gc", chunk, core_peer)

    def x_copy(chunk):
        return remote(s["g_own"].at[chunk, :, 1 - x_at], s["x_recv"].at[chunk], "gx", chunk, x_peer)

    def z_copies(chunk):
        return [
            remote(
                s["g_own"].at[chunk, lax.rem(z_at + d, 4), x_at], s["z_recv"].at[chunk, 3 - d],
                "gz", 3 * chunk + 3 - d, z_peers[d - 1],
            )
            for d in (1, 2, 3)
        ]

    def core_done(chunk, slot):
        core_copy(chunk, slot).wait_recv()
        s["g_own"][chunk] = s["g_own"][chunk] + s["core_recv"][slot]
        x_copy(chunk).start()

    def x_done(chunk):
        x_copy(chunk).wait_recv()
        for z in range(4):
            s["g_own"][chunk, z, x_at] = s["g_own"][chunk, z, x_at] + s["x_recv"][chunk, z]
        for copy in z_copies(chunk):
            copy.start()

    def z_done(chunk):
        for copy in z_copies(chunk):
            copy.wait_recv()
        part = s["g_own"][chunk, z_at, x_at]
        for d in range(3):
            part += s["z_recv"][chunk, d]
        return part

    def out_grad(c, carry):
        cols = pl.ds(pl.multiple_of(c * CW, CW), CW)
        keep(grad_chunk(s["top_t"], s["active"].at[:, cols]), c, c)
        return carry

    def in_grad(c, carry):
        cols = pl.ds(pl.multiple_of(c * CW, CW), CW)
        keep(grad_chunk(s["normed2_t"], s["grad_pre"].at[:, cols]), c + units // CW, c)
        return carry

    def group_done(first):
        lax.fori_loop(0, SLOTS, lambda c, carry: (core_done(first + c, c), carry)[1], 0)

    def next_group(first):
        pl.semaphore_signal(s["free"].at[0], inc=1, device_id=core_peer, device_id_type=MESH)
        lax.fori_loop(0, SLOTS, lambda c, carry: (core_copy(first + c, c).wait_send(), carry)[1], 0)
        pl.semaphore_wait(s["free"].at[0], 1)

    lax.fori_loop(0, units // CW, out_grad, 0)
    if ring:
        group_done(0)
        next_group(0)
    lax.fori_loop(0, units // CW, in_grad, 0)
    if ring:
        group_done(SLOTS)

    s["grad_k"][...] = jnp.zeros_like(s["grad_k"])
    s["grad_v"][...] = jnp.zeros_like(s["grad_v"])
    s["grad_table"][...] = jnp.zeros_like(s["grad_table"])
    flip_row = lax.broadcasted_iota(jnp.int32, (2 * RB, 2 * RB), 0)
    flip_col = lax.broadcasted_iota(jnp.int32, (2 * RB, 2 * RB), 1)
    same_half = (flip_row < RB) == (flip_col < RB)
    local_row = lax.rem(flip_row, RB)
    local_col = lax.rem(flip_col, RB)
    flip = (same_half & (local_row + local_col == RB - 1)).astype(BF16)

    def attend_back(i, carry):
        start = pl.multiple_of(i * RB, RB)
        rows = pl.ds(start, RB)
        sum_copy("gn2", i).wait_recv()
        grad_normed = s["gn2_send"][rows, :] + s["gn2_recv"][rows, :]
        unit, scale = norm_stats(s["middle"][rows, :])
        s["n2"][0:1, :] += col_sum(grad_normed * unit)
        s["n2"][1:2, :] += col_sum(grad_normed)
        top = cotangent[rows, :].astype(F32) * valid_rows(start, RB)
        grad_middle = top + norm_back(grad_normed, unit, scale, gain2)
        s["grad_middle"][rows, :] = grad_middle
        grad_attended = grad_middle.astype(BF16)
        s["aob"][...] += col_sum(grad_attended.astype(F32))
        s["wo"][:, pl.ds(start, RB)] = grad_attended.T
        grad_context = mm_nt(grad_attended, attn_out[...]).astype(BF16)
        for p in range(pairs):
            s["grad_ctx"][p] = grad_context[:, p * 128 : (p + 1) * 128]

        def pair_step(p, carry):
            qs = stack(s["q"][p, rows, :])
            gs = stack(s["grad_ctx"][p])
            low = s["probs"][p, i]
            s["grad_v"][p] += mm_tn(low, gs)
            shares = low.astype(F32)
            grad_shares = mm_nt(gs, s["v"][p])
            inner = jnp.sum(grad_shares * shares, axis=-1, keepdims=True)
            grad_scores = (shares * (grad_shares - inner)).astype(BF16)
            s["grad_k"][p] += mm_tn(grad_scores, qs)
            grad_q = mm(grad_scores, s["k"][p])
            flipped = mm(flip, grad_scores)
            wide = jnp.concatenate([flipped, jnp.zeros((2 * RB, RB), F32)], axis=1)
            spread = jnp.concatenate(
                [
                    pltpu.roll(wide[:RB], 0, 1, stride=1, stride_axis=0),
                    pltpu.roll(wide[RB:], 0, 1, stride=1, stride_axis=0),
                ],
                axis=0,
            ).astype(BF16)
            q_flipped = mm(flip, qs).astype(BF16)
            s["grad_table"][table_rows_of(i), :] += mm_tn(spread, q_flipped)
            turned = mm(spread, s["table"][table_rows_of(i), :])
            high = turned.astype(BF16)
            rest = (turned - high.astype(F32)).astype(BF16)
            grad_q = unstack(grad_q + (mm(flip, high) + mm(flip, rest))).astype(BF16)
            cols = pl.ds(pl.multiple_of(p * 128, 128), 128)
            s["grad_pre"][rows, cols] = (grad_q.astype(F32) * head_scale).astype(BF16)
            return carry

        lax.fori_loop(0, pairs, pair_step, 0)
        if ring:
            x_done(i)
        return carry

    lax.fori_loop(0, blocks, attend_back, 0)
    pl.semaphore_signal(s["free"].at[1], inc=1, device_id=y_peer, device_id_type=MESH)

    def send_out(i, carry):
        sum_copy("out", i).start()
        return carry

    lax.fori_loop(0, blocks, send_out, 0)

    for p in range(pairs):
        at = local + p * 128
        s["grad_pre"][:, at : at + 128] = s["grad_k"][p].astype(BF16)
        at += local
        s["grad_pre"][:, at : at + 128] = s["grad_v"][p].astype(BF16)
    for i in range(blocks):
        sum_copy("gn2", i).wait_send()
    pl.semaphore_wait(s["free"].at[1], 1)

    def back_copy(i):
        rows = pl.ds(pl.multiple_of(i * RB, RB), RB)
        return remote(s["gn2_send"].at[rows], s["gn2_recv"].at[rows], "gn1", i, y_peer)

    def project_back(b, carry):
        start = pl.multiple_of(b * RF, RF)
        rows = pl.ds(start, RF)
        total = (
            mm_nt(s["grad_pre"][rows, 0:local], attn_in[0])
            + mm_nt(s["grad_pre"][rows, local : 2 * local], attn_in[1])
            + mm_nt(s["grad_pre"][rows, 2 * local : 3 * local], attn_in[2])
        )
        s["gn2_send"][rows, :] = total
        for j in range(RF // RB):
            back_copy(b * (RF // RB) + j).start()
        unit, unused = norm_stats(hidden[rows, :].astype(F32))
        s["n1"][0:1, :] += col_sum(total * unit)
        s["n1"][1:2, :] += col_sum(total)
        return carry

    lax.fori_loop(0, slots // RF, project_back, 0)

    if ring:
        next_group(SLOTS)

    def attn_grad(which, carry):
        cols = pl.ds(pl.multiple_of(which * local, 128), local)
        keep(grad_chunk(s["normed_t"], s["grad_pre"].at[:, cols]), ffn_chunks + which, which)
        return carry

    lax.fori_loop(0, 3, attn_grad, 0)
    context = jnp.concatenate([s["ctx"][ten * pairs + p] for p in range(pairs)], axis=1)
    keep(mm(s["wo"][:, 0:slots], context), ffn_chunks + 3, 3)

    def put(at, row):
        for j in range(row.shape[1] // 128):
            g_vec_acc[at + j : at + j + 1, :] = row[:, j * 128 : (j + 1) * 128]

    put(V_N1G, s["n1"][0:1, :])
    put(V_N1B, s["n1"][1:2, :])
    put(V_N2G, s["n2"][0:1, :])
    put(V_N2B, s["n2"][1:2, :])
    put(V_AOB, s["aob"][...])
    put(V_FOB, s["fob"][...])
    put(V_FIB, s["fib"][...])
    put(V_AIB, col_sum(s["grad_pre"][:, 0:local].astype(F32)))
    put(V_AIB + pairs, col_sum(s["grad_pre"][:, 2 * local : 3 * local].astype(F32)))
    grad_rel = lax.dot_general(
        pick.astype(F32), s["grad_table"][...], (((0,), (0,)), ((), ())),
        preferred_element_type=F32, precision=lax.Precision.HIGHEST,
    )
    grad_rel = grad_rel + pltpu.roll(grad_rel, HD, 1)
    fold = lax.broadcasted_iota(jnp.int32, (reach, 128), 1) < HD
    g_vec_acc[V_REL : V_REL + reach, :] = jnp.where(fold, grad_rel[:reach], grad_rel[reach:])

    def vec_step(step, peer, count):
        rows = pl.ds(0, count)
        return remote(s["vec_send"].at[step, rows], s["vec_recv"].at[step, rows], "vec", step, peer)

    def share(step, peer, count):
        s["vec_send"][step, 0:count] = g_vec_acc[0:count, :]
        vec_step(step, peer, count).start()

    def merge(step, peer, count):
        vec_step(step, peer, count).wait_recv()
        g_vec_acc[0:count, :] = s["vec_send"][step, 0:count] + s["vec_recv"][step, 0:count]

    if ring:
        z_low = (dp + 4 - 8 * lax.rem(z_at, 2), ten)
        z_high = (lax.rem(dp + 8, 16), ten)
        vec_peers = [core_peer, x_peer, z_low, z_high]
        share(1, core_peer, VROWS)
        group_done(ffn_chunks)
        merge(1, core_peer, VROWS)
        for step in (2, 3, 4):
            share(step, vec_peers[step - 1], VROWS)
            merge(step, vec_peers[step - 1], VROWS)
        lax.fori_loop(blocks, ffn_chunks, lambda c, carry: (x_done(c), carry)[1], 0)
    share(0, y_peer, YROWS)

    def finish_out(i, carry):
        start = pl.multiple_of(i * RB, RB)
        rows = pl.ds(start, RB)
        sum_copy("out", i).wait_recv()
        branch = s["out_send"][rows, :] + s["out_recv"][rows, :]
        total = s["middle"][rows, :] + (branch + ffn_out_bias)
        output[rows, :] = (total * valid_rows(start, RB)).astype(BF16)
        return carry

    def finish_hidden(i, carry):
        rows = pl.ds(pl.multiple_of(i * RB, RB), RB)
        back_copy(i).wait_recv()
        grad_normed = s["gn2_send"][rows, :] + s["gn2_recv"][rows, :]
        unit, scale = norm_stats(hidden[rows, :].astype(F32))
        total = s["grad_middle"][rows, :] + norm_back(grad_normed, unit, scale, gain1)
        grad_hidden[rows, :] = total.astype(BF16)
        return carry

    lax.fori_loop(0, blocks, finish_out, 0)
    if ring:
        for c in range(units // CW):
            g_ffn_out[c * CW : (c + 1) * CW, :] = z_done(c).T
        for c in range(units // CW):
            g_ffn_in[:, c * CW : (c + 1) * CW] = z_done(c + units // CW)
        lax.fori_loop(ffn_chunks, ffn_chunks + attn_chunks, lambda c, carry: (x_done(c), carry)[1], 0)
    lax.fori_loop(0, blocks, finish_hidden, 0)
    if ring:
        for c in range(3):
            g_attn_in[c] = z_done(ffn_chunks + c)
        g_attn_out[...] = z_done(ffn_chunks + 3).T
    merge(0, y_peer, YROWS)
    g_vec[...] = g_vec_acc[...]

    wo_y.wait_send()
    if ring:
        wo_x.wait_send()
        wo_c0.wait_send()
        wo_c1.wait_send()

    def sent(i, carry):
        ctx_copy(i).wait_send()
        sum_copy("out", i).wait_send()
        back_copy(i).wait_send()
        return carry

    lax.fori_loop(0, blocks, sent, 0)
    vec_step(0, y_peer, YROWS).wait_send()
    if ring:
        for step in (1, 2, 3, 4):
            vec_step(step, vec_peers[step - 1], VROWS).wait_send()

        def grads_sent(c, carry):
            x_copy(c).wait_send()
            for copy in z_copies(c):
                copy.wait_send()
            return carry

        lax.fori_loop(0, ffn_chunks + attn_chunks, grads_sent, 0)
        for c in range(SLOTS):
            core_copy(ffn_chunks + c, c).wait_send()


def scratch_of(ring, slots, width, local, units, chunks, ffn_chunks):
    pairs = local // 128
    blocks = slots // RB
    halves = slots // RF
    vm, dma = pltpu.VMEM, pltpu.SemaphoreType.DMA
    shapes = dict(
        normed_t=vm((halves, width, RF), BF16),
        q=vm((pairs, slots, 128), BF16),
        k=vm((pairs, slots, 128), BF16),
        v=vm((pairs, slots, 128), BF16),
        table=vm((2 * slots, 128), BF16),
        probs=vm((pairs, blocks, 2 * RB, slots), BF16),
        ctx=vm((2 * pairs, slots, 128), BF16),
        ctx_send=vm((pairs, slots, 128), F32),
        ctx_recv=vm((pairs, slots, 128), F32),
        wo=vm((2 * local, width), BF16),
        wo_stage=vm((local // 4 if ring else local, width), F32),
        wo_recv=vm((4, local // 4, width) if ring else (local, width), F32),
        middle=vm((slots, width), F32),
        normed2_t=vm((halves, width, RF), BF16),
        top_t=vm((halves, width, RF), BF16),
        active=vm((slots, units), BF16),
        grad_pre=vm((slots, units), BF16),
        gn2_send=vm((slots, width), F32),
        gn2_recv=vm((slots, width), F32),
        out_send=vm((slots, width), F32),
        out_recv=vm((slots, width), F32),
        grad_middle=vm((slots, width), F32),
        grad_ctx=vm((pairs, RB, 128), BF16),
        grad_k=vm((pairs, slots, 128), F32),
        grad_v=vm((pairs, slots, 128), F32),
        grad_table=vm((2 * slots, 128), F32),
        vec=vm((VROWS, 128), F32),
        vec_send=vm((5 if ring else 1, VROWS, 128), F32),
        vec_recv=vm((5 if ring else 1, VROWS, 128), F32),
        fib=vm((1, units), F32),
        fob=vm((1, width), F32),
        aob=vm((1, width), F32),
        n1=vm((2, width), F32),
        n2=vm((2, width), F32),
        ffn_in_bias=vm((1, units), F32),
        free=pltpu.SemaphoreType.REGULAR((2,)),
        wo_s=dma((4,)), wo_r=dma((4,)),
        ctx_s=dma((blocks,)), ctx_r=dma((blocks,)),
        gn2_s=dma((blocks,)), gn2_r=dma((blocks,)),
        gn1_s=dma((blocks,)), gn1_r=dma((blocks,)),
        out_s=dma((blocks,)), out_r=dma((blocks,)),
        vec_s=dma((5,)), vec_r=dma((5,)),
    )
    if ring:
        shapes.update(
            g_own=vm((chunks, 4, 2, 48, CW), F32),
            g_send=vm((SLOTS, 4, 2, 48, CW), F32),
            core_recv=vm((SLOTS, 4, 2, 48, CW), F32),
            x_recv=vm((chunks, 4, 48, CW), F32),
            z_recv=vm((chunks, 3, 48, CW), F32),
            gc_s=dma((chunks,)), gc_r=dma((chunks,)),
            gx_s=dma((chunks,)), gx_r=dma((chunks,)),
            gz_s=dma((3 * chunks,)), gz_r=dma((3 * chunks,)),
        )
    return shapes


SCRATCH_PLAIN = tuple(scratch_of(False, 512, 768, 384, 1536, 12, 8))
SCRATCH_RING = tuple(scratch_of(True, 512, 768, 384, 1536, 12, 8))


def on_device(
    ring,
    hidden, lengths, attn_in, attn_in_bias, rel_table, attn_out, attn_out_bias,
    norm1_gain, norm1_bias, norm2_gain, norm2_bias,
    ffn_in, ffn_in_bias, ffn_out, ffn_out_bias, cotangent,
):
    slots, width = hidden.shape
    local = attn_out.shape[0]
    units = ffn_in.shape[1]
    ffn_chunks = 2 * units // CW
    chunks = ffn_chunks + 4
    vectors_in = jnp.concatenate(
        [
            attn_out_bias, norm1_gain, norm1_bias, norm2_gain, norm2_bias, ffn_out_bias,
            ffn_in_bias, attn_in_bias.reshape(2 * local),
        ]
    ).astype(F32).reshape(9, width)
    rows = width // 16
    outs = [
        jax.ShapeDtypeStruct((slots, width), BF16),
        jax.ShapeDtypeStruct((slots, width), BF16),
        jax.ShapeDtypeStruct((3, rows, local), F32),
        jax.ShapeDtypeStruct((local, rows), F32),
        jax.ShapeDtypeStruct((rows, units), F32),
        jax.ShapeDtypeStruct((units, rows), F32),
        jax.ShapeDtypeStruct((VROWS, 128), F32),
    ]
    shapes = scratch_of(ring, slots, width, local, units, chunks, ffn_chunks)
    if not ring:
        outs.append(jax.ShapeDtypeStruct((chunks, width, CW), F32))
    vmem = pl.BlockSpec(memory_space=pltpu.VMEM)

    def kernel(*refs):
        if ring:
            body(ring, *refs)
        else:
            fixed = refs[:16]
            body_plain(refs[16], fixed, refs[17:])

    def body_plain(full, fixed, scratch):
        body(ring, *fixed, *scratch, full)

    results = pl.pallas_call(
        kernel,
        out_shape=outs,
        in_specs=[vmem, pl.BlockSpec(memory_space=pltpu.SMEM)] + [vmem] * 7,
        out_specs=[vmem] * len(outs),
        scratch_shapes=list(shapes.values()),
        compiler_params=pltpu.CompilerParams(
            collective_id=0, has_side_effects=True, vmem_limit_bytes=64 * 1024 * 1024
        ),
    )(hidden, lengths, attn_in, rel_table, attn_out, vectors_in, ffn_in, ffn_out, cotangent)
    output, grad_hidden, g_attn_in, g_attn_out, g_ffn_in, g_ffn_out, vec = results[:7]
    if not ring:
        full = results[7]
        per = units // CW
        wide = jnp.swapaxes(full[: 2 * per].reshape(2, per, width, CW), 1, 2).reshape(2, width, units)

        def scatter(value, dim):
            return lax.psum_scatter(value, "dp", scatter_dimension=dim, tiled=True)

        g_ffn_out = scatter(wide[0].T, 1)
        g_ffn_in = scatter(wide[1], 0)
        g_attn_in = scatter(full[2 * per : 2 * per + 3], 1)
        g_attn_out = scatter(full[2 * per + 3].T, 1)
        vec = lax.psum(vec, "dp")

    def row(at, count=width):
        return vec[at : at + count // 128].reshape(count)

    rel_pairs = vec[V_REL : V_REL + 160]
    grad_rel = jnp.concatenate([rel_pairs[:, :HD], rel_pairs[:, HD:]], axis=0)
    return (
        output, grad_hidden, g_attn_in,
        row(V_AIB).reshape(2, local), grad_rel, g_attn_out, row(V_AOB),
        row(V_N1G), row(V_N1B), row(V_N2G), row(V_N2B),
        g_ffn_in, row(V_FIB, units), g_ffn_out, row(V_FOB),
    )


def solution(mesh):
    ring = mesh.shape["dp"] == 16
    return jax.shard_map(
        partial(on_device, ring),
        mesh=mesh,
        in_specs=(
            P("dp", None), P("dp"), P(None, None, "tensor"), P(None, "tensor"), P(),
            P("tensor", None), P(), P(), P(), P(), P(),
            P(None, "tensor"), P("tensor"), P("tensor", None), P(), P("dp", None),
        ),
        out_specs=(
            P("dp", None), P("dp", None), P(None, "dp", "tensor"), P(None, "tensor"), P(),
            P("tensor", "dp"), P(), P(), P(), P(), P(),
            P("dp", "tensor"), P("tensor"), P("tensor", "dp"), P(),
        ),
        check_vma=False,
    )
```

```python
from functools import partial

import jax
import jax.numpy as jnp
from jax import lax
from jax.experimental import pallas as pl
from jax.experimental.pallas import tpu as pltpu
from jax.sharding import PartitionSpec as P

HD = 64
EPSILON = 1e-05
NEGATIVE = -1e30
SQRT_HALF = 0.7071067811865476
INV_SQRT_2PI = 0.3989422804014327
RB = 128
RF = 256
CW = 384
SLOTS = 4
MESH = pl.DeviceIdType.MESH
F32 = jnp.float32
BF16 = jnp.bfloat16


def mm(a, b):
    return jnp.dot(a, b, preferred_element_type=F32)


def mm_nt(a, b):
    return lax.dot_general(a, b, (((1,), (1,)), ((), ())), preferred_element_type=F32)


def mm_tn(a, b):
    return lax.dot_general(a, b, (((0,), (0,)), ((), ())), preferred_element_type=F32)


def norm_stats(value):
    mean = jnp.mean(value, axis=-1, keepdims=True)
    centred = value - mean
    scale = lax.rsqrt(jnp.mean(centred * centred, axis=-1, keepdims=True) + EPSILON)
    return centred * scale, scale


def norm_back(grad, unit, scale, gain):
    grad_unit = grad * gain
    inner = (
        grad_unit
        - jnp.mean(grad_unit, axis=-1, keepdims=True)
        - unit * jnp.mean(grad_unit * unit, axis=-1, keepdims=True)
    )
    return inner * scale


def col_sum(value):
    return jnp.sum(value, axis=0, keepdims=True)


def lanes_of(ref3, rows):
    return jnp.concatenate([ref3[p, rows, :] for p in range(ref3.shape[0])], axis=1)


V_N1G, V_N1B, V_REL, V_AOB, V_N2G, V_N2B, V_FOB, V_FIB, V_AIB = 0, 6, 16, 176, 182, 188, 194, 200, 212
YROWS, VROWS = 176, 224


def body(
    ring, names,
    lengths, attn_in_bias, rel_table_t, attn_out_bias, norm1_gain, norm1_bias, norm2_gain, norm2_bias,
    ffn_in_bias, ffn_out_bias, far_hidden, far_attn_in, far_attn_out, far_ffn_in, far_ffn_out, far_cotangent,
    far_output, far_grad_hidden, far_grads, far_vec,
    *scratch,
):
    s = dict(zip(names, scratch))

    def bring(at, name, far):
        copy = pltpu.make_async_copy(far, s[name], s["in_s"].at[at])
        copy.start()
        return copy

    bring_attn_out = bring(0, "attn_out", far_attn_out)
    bring_hidden = bring(1, "hidden", far_hidden)
    bring_attn_in = bring(2, "attn_in", far_attn_in)
    bring_cotangent = bring(3, "cotangent", far_cotangent)
    bring_ffn_in = bring(4, "ffn_in", far_ffn_in)
    bring_ffn_out = bring(5, "ffn_out", far_ffn_out)
    hidden, attn_in, attn_out = s["hidden"], s["attn_in"], s["attn_out"]
    cotangent, ffn_in, ffn_out = s["cotangent"], s["ffn_in"], s["ffn_out"]
    output, grad_hidden = s["output"], s["grad_hidden"]
    slots, width = hidden.shape
    local = attn_out.shape[0]
    pairs = local // 128
    units = ffn_in.shape[1]
    table_rows = rel_table_t.shape[1]
    reach = table_rows // 2
    blocks = slots // RB
    ext = slots + RB
    head_scale = HD ** (-0.5)

    dp = lax.axis_index("dp")
    ten = lax.axis_index("tensor")
    y_peer = (dp, 1 - ten)
    if ring:
        core = lax.rem(dp, 2)
        x_at = lax.rem(lax.div(dp, 2), 2)
        z_at = lax.div(dp, 4)
        core_peer = (dp + 1 - 2 * core, ten)
        x_peer = (dp + 2 - 4 * x_at, ten)
        z_peers = [(lax.rem(dp + 4 * d, 16), ten) for d in (1, 2, 3)]
        greet = [y_peer, core_peer, x_peer] + z_peers
    else:
        greet = [y_peer]

    barrier = pltpu.get_barrier_semaphore()
    for peer in greet:
        pl.semaphore_signal(barrier, inc=1, device_id=peer, device_id_type=MESH)

    def remote(src, dst, name, at, peer):
        return pltpu.make_async_remote_copy(
            src_ref=src, dst_ref=dst, send_sem=s[name + "_s"].at[at], recv_sem=s[name + "_r"].at[at],
            device_id=peer, device_id_type=MESH,
        )

    bring_attn_out.wait()
    if ring:
        piece = local // 8
        mine, other = 2 * x_at + core, 2 * (1 - x_at) + core
        for h in range(2):
            at = pl.multiple_of((4 * h + mine) * piece, 16)
            s["wo_stage"][h] = attn_out[pl.ds(at, piece), :].astype(F32)

        def wo_y(h):
            return remote(s["wo_stage"].at[h], s["wo_recv"].at[4 * h + mine], "wo", h, y_peer)

        def wo_pass(h, which, at, peer):
            part = s["wo_recv"].at[4 * h + which]
            return remote(part, part, "wo", at + h, peer)

        def wo_x(h):
            return wo_pass(h, mine, 2, x_peer)

        def wo_core(h):
            return wo_pass(h, mine, 4, core_peer)

        def wo_core_far(h):
            return wo_pass(h, other, 6, core_peer)
    else:
        s["wo_stage"][...] = attn_out[...].astype(F32)

        def wo_y(h):
            return remote(s["wo_stage"], s["wo_recv"], "wo", h, y_peer)

    pl.semaphore_wait(barrier, len(greet))
    wo_y(0).start()
    if ring:
        wo_y(1).start()

    def flat(ref):
        value = ref[...].astype(F32)
        return jnp.concatenate([value[j : j + 1] for j in range(value.shape[0])], axis=1)

    bias_q = attn_in_bias[0:1, :].astype(F32)
    bias_v = attn_in_bias[1:2, :].astype(F32)
    gain1, offset1 = flat(norm1_gain), flat(norm1_bias)
    gain2, offset2 = flat(norm2_gain), flat(norm2_bias)
    out_bias1, out_bias2 = flat(attn_out_bias), flat(ffn_out_bias)
    s["ffn_in_bias"][...] = flat(ffn_in_bias)
    seq_len = lengths[0]

    ext_rows = 2 * slots
    distance = slots - 1 - lax.broadcasted_iota(jnp.int32, (ext_rows, table_rows), 0)
    bucket = jnp.clip(distance, -reach, reach - 1) + reach
    pick = (bucket == lax.broadcasted_iota(jnp.int32, (ext_rows, table_rows), 1)).astype(BF16)
    rel_t = rel_table_t[...]
    s["table"][...] = mm_nt(pick, jnp.concatenate([rel_t, rel_t], axis=0)).astype(BF16)

    def project(i, carry):
        rows = pl.ds(pl.multiple_of(i * RF, RF), RF)
        unit, unused = norm_stats(hidden[rows, :].astype(F32))
        normed = (unit * gain1 + offset1).astype(BF16)
        s["normed_t"][i] = normed.T
        q = ((mm(normed, attn_in[0]) + bias_q) * head_scale).astype(BF16)
        k = mm(normed, attn_in[1]).astype(BF16)
        v = (mm(normed, attn_in[2]) + bias_v).astype(BF16)
        for p in range(pairs):
            s["q"][p, rows, :] = q[:, p * 128 : (p + 1) * 128]
            s["k"][p, rows, :] = k[:, p * 128 : (p + 1) * 128]
            s["v"][p, rows, :] = v[:, p * 128 : (p + 1) * 128]
        return carry

    bring_hidden.wait()
    bring_attn_in.wait()
    lax.fori_loop(0, slots // RF, project, 0)

    low_lanes = lax.broadcasted_iota(jnp.int32, (RB, 128), 1) < HD
    key_ok = lax.broadcasted_iota(jnp.int32, (1, slots), 1) < seq_len

    def stack(both):
        zero = jnp.zeros_like(both)
        return jnp.concatenate([jnp.where(low_lanes, both, zero), jnp.where(low_lanes, zero, both)], axis=0)

    def unstack(tall):
        return jnp.where(low_lanes, tall[:RB], tall[RB:])

    def table_rows_of(i):
        return pl.ds(pl.multiple_of(slots - RB - i * RB, RB), ext)

    def ctx_copy(i):
        rows = pl.ds(pl.multiple_of(i * RB, RB), RB)
        return remote(s["ctx_send"].at[:, rows], s["ctx_recv"].at[:, rows], "ctx", i, y_peer)

    def attend(i, carry):
        rows = pl.ds(pl.multiple_of(i * RB, RB), RB)

        def pair_step(p, carry):
            qs = stack(s["q"][p, rows, :])
            spread = mm_nt(qs, s["table"][table_rows_of(i), :])
            shift = ext - RB + 1
            bias = jnp.concatenate(
                [
                    pltpu.roll(spread[:RB], shift, 1, stride=1, stride_axis=0)[:, :slots],
                    pltpu.roll(spread[RB:], shift, 1, stride=1, stride_axis=0)[:, :slots],
                ],
                axis=0,
            )
            scores = jnp.where(key_ok, mm_nt(qs, s["k"][p]) + bias, NEGATIVE)
            expon = jnp.exp(scores - jnp.max(scores, axis=-1, keepdims=True))
            shares = (expon * (1.0 / jnp.sum(expon, axis=-1, keepdims=True))).astype(BF16)
            s["probs"][p, i] = shares
            context = unstack(mm(shares, s["v"][p])).astype(BF16)
            s["ctx"][ten * pairs + p, rows, :] = context
            s["ctx_send"][p, rows, :] = context.astype(F32)
            return carry

        lax.fori_loop(0, pairs, pair_step, 0)
        ctx_copy(i).start()
        return carry

    half = pl.ds(pl.multiple_of(ten * local, 128), local)
    far_half = pl.ds(pl.multiple_of((1 - ten) * local, 128), local)
    s["wo"][half, :] = attn_out[...]
    attend(0, 0)
    if ring:
        wo_y(0).wait_recv()
        wo_x(0).start()
        wo_core(0).start()
    attend(1, 0)
    if ring:
        wo_y(1).wait_recv()
        wo_x(1).start()
        wo_core(1).start()
        wo_x(0).wait_recv()
        wo_core_far(0).start()
    attend(2, 0)
    if ring:
        wo_x(1).wait_recv()
        wo_core_far(1).start()
    attend(3, 0)

    if ring:
        for h in range(2):
            wo_core(h).wait_recv()
            wo_core_far(h).wait_recv()
        for k in range(8):
            rows = pl.ds(pl.multiple_of((1 - ten) * local + k * piece, 16), piece)
            s["wo"][rows, :] = s["wo_recv"][k].astype(BF16)
    else:
        wo_y(0).wait_recv()
        s["wo"][far_half, :] = s["wo_recv"][...].astype(BF16)
    bring_cotangent.wait()
    bring_ffn_in.wait()
    bring_ffn_out.wait()

    def valid_rows(start, count):
        return (lax.broadcasted_iota(jnp.int32, (count, 1), 0) + start < seq_len).astype(F32)

    def sum_copy(name, i):
        rows = pl.ds(pl.multiple_of(i * RB, RB), RB)
        return remote(s[name + "_send"].at[rows], s[name + "_recv"].at[rows], name, i, y_peer)

    g_vec_acc = s["vec"]
    g_vec_acc[...] = jnp.zeros_like(g_vec_acc)
    s["fib"][...] = jnp.zeros_like(s["fib"])
    s["fob"][...] = jnp.zeros_like(s["fob"])
    s["aob"][...] = jnp.zeros_like(s["aob"])
    s["n1"][...] = jnp.zeros_like(s["n1"])
    s["n2"][...] = jnp.zeros_like(s["n2"])

    step_units = 512

    def feed(b, carry):
        start = pl.multiple_of(b * RF, RF)
        rows = pl.ds(start, RF)
        for j in range(RF // RB):
            ctx_copy(b * (RF // RB) + j).wait_recv()
        for p in range(pairs):
            s["ctx"][(1 - ten) * pairs + p, rows, :] = s["ctx_recv"][p, rows, :].astype(BF16)
        attended = mm(lanes_of(s["ctx"], rows), s["wo"][...]) + out_bias1
        middle = hidden[rows, :].astype(F32) + attended
        s["middle"][rows, :] = middle
        unit, unused = norm_stats(middle)
        normed = (unit * gain2 + offset2).astype(BF16)
        s["normed2_t"][b] = normed.T
        top = cotangent[rows, :].astype(F32) * valid_rows(start, RF)
        s["fob"][...] += col_sum(top)
        top = top.astype(BF16)
        s["top_t"][b] = top.T
        for c in range(units // step_units):
            cols = slice(c * step_units, (c + 1) * step_units)
            pre = mm(normed, ffn_in[:, cols]) + s["ffn_in_bias"][:, cols]
            share = 0.5 + 0.5 * lax.erf(pre * SQRT_HALF)
            active = (pre * share).astype(BF16)
            s["active"][rows, cols] = active
            slope = share + pre * (jnp.exp(-0.5 * pre * pre) * INV_SQRT_2PI)
            grad_pre = (mm_nt(top, ffn_out[cols, :]) * slope).astype(BF16)
            s["grad_pre"][rows, cols] = grad_pre
            s["fib"][:, cols] += col_sum(grad_pre.astype(F32))
            back = mm_nt(grad_pre, ffn_in[:, cols])
            onward = mm(active, ffn_out[cols, :])
            if c == 0:
                s["gn2_send"][rows, :] = back
                s["out_send"][rows, :] = onward
            else:
                s["gn2_send"][rows, :] += back
                s["out_send"][rows, :] += onward
        for j in range(RF // RB):
            sum_copy("gn2", b * (RF // RB) + j).start()
        return carry

    lax.fori_loop(0, slots // RF, feed, 0)

    def grad_chunk(left_t, right):
        total = mm(left_t[0], right[0:RF])
        for b in range(1, slots // RF):
            total += mm(left_t[b], right[b * RF : (b + 1) * RF])
        return total

    ffn_chunks = 2 * units // CW
    attn_chunks = 4

    def keep(total, chunk, slot):
        if ring:
            parts = total.reshape(8, 2, 48, CW)
            even, odd = parts[:, 0], parts[:, 1]
            s["g_own"][chunk] = jnp.where(core == 0, even, odd).reshape(4, 2, 48, CW)
            s["g_send"][slot] = jnp.where(core == 0, odd, even).reshape(4, 2, 48, CW)
            core_copy(chunk, slot).start()
        else:
            s["g_full"][chunk] = total

    def core_copy(chunk, slot):
        return remote(s["g_send"].at[slot], s["core_recv"].at[slot], "gc", chunk, core_peer)

    def x_copy(chunk):
        return remote(s["g_own"].at[chunk, :, 1 - x_at], s["x_recv"].at[chunk], "gx", chunk, x_peer)

    def z_copies(chunk):
        return [
            remote(
                s["g_own"].at[chunk, lax.rem(z_at + d, 4), x_at], s["z_recv"].at[chunk, 3 - d],
                "gz", 3 * chunk + 3 - d, z_peers[d - 1],
            )
            for d in (1, 2, 3)
        ]

    def core_done(chunk, slot):
        core_copy(chunk, slot).wait_recv()
        s["g_own"][chunk] = s["g_own"][chunk] + s["core_recv"][slot]
        x_copy(chunk).start()

    def x_done(chunk):
        x_copy(chunk).wait_recv()
        for z in range(4):
            s["g_own"][chunk, z, x_at] = s["g_own"][chunk, z, x_at] + s["x_recv"][chunk, z]
        for copy in z_copies(chunk):
            copy.start()

    def z_done(chunk):
        for copy in z_copies(chunk):
            copy.wait_recv()
        part = s["g_own"][chunk, z_at, x_at]
        for d in range(3):
            part += s["z_recv"][chunk, d]
        return part

    def out_grad(c, carry):
        cols = pl.ds(pl.multiple_of(c * CW, CW), CW)
        keep(grad_chunk(s["top_t"], s["active"].at[:, cols]), c, c)
        return carry

    def in_grad(c, carry):
        cols = pl.ds(pl.multiple_of(c * CW, CW), CW)
        keep(grad_chunk(s["normed2_t"], s["grad_pre"].at[:, cols]), c + units // CW, c)
        return carry

    def group_done(first):
        lax.fori_loop(0, SLOTS, lambda c, carry: (core_done(first + c, c), carry)[1], 0)

    def next_group(first):
        pl.semaphore_signal(s["free"].at[0], inc=1, device_id=core_peer, device_id_type=MESH)
        lax.fori_loop(0, SLOTS, lambda c, carry: (core_copy(first + c, c).wait_send(), carry)[1], 0)
        pl.semaphore_wait(s["free"].at[0], 1)

    lax.fori_loop(0, units // CW, out_grad, 0)
    if ring:
        group_done(0)
        next_group(0)
    lax.fori_loop(0, units // CW, in_grad, 0)
    if ring:
        group_done(SLOTS)

    s["grad_k"][...] = jnp.zeros_like(s["grad_k"])
    s["grad_v"][...] = jnp.zeros_like(s["grad_v"])
    s["grad_table"][...] = jnp.zeros_like(s["grad_table"])
    flip_row = lax.broadcasted_iota(jnp.int32, (2 * RB, 2 * RB), 0)
    flip_col = lax.broadcasted_iota(jnp.int32, (2 * RB, 2 * RB), 1)
    same_half = (flip_row < RB) == (flip_col < RB)
    local_row = lax.rem(flip_row, RB)
    local_col = lax.rem(flip_col, RB)
    flip = (same_half & (local_row + local_col == RB - 1)).astype(BF16)

    def attend_back(i, carry):
        start = pl.multiple_of(i * RB, RB)
        rows = pl.ds(start, RB)
        sum_copy("gn2", i).wait_recv()
        grad_normed = s["gn2_send"][rows, :] + s["gn2_recv"][rows, :]
        unit, scale = norm_stats(s["middle"][rows, :])
        s["n2"][0:1, :] += col_sum(grad_normed * unit)
        s["n2"][1:2, :] += col_sum(grad_normed)

        @pl.when(i == blocks - 1)
        def send_out():
            for j in range(blocks):
                sum_copy("out", j).start()

        top = cotangent[rows, :].astype(F32) * valid_rows(start, RB)
        grad_middle = top + norm_back(grad_normed, unit, scale, gain2)
        s["grad_middle"][rows, :] = grad_middle
        grad_attended = grad_middle.astype(BF16)
        s["aob"][...] += col_sum(grad_attended.astype(F32))
        s["wo"][:, pl.ds(start, RB)] = grad_attended.T
        grad_context = mm_nt(grad_attended, attn_out[...]).astype(BF16)
        for p in range(pairs):
            s["grad_ctx"][p] = grad_context[:, p * 128 : (p + 1) * 128]

        def pair_step(p, carry):
            qs = stack(s["q"][p, rows, :])
            gs = stack(s["grad_ctx"][p])
            low = s["probs"][p, i]
            s["grad_v"][p] += mm_tn(low, gs)
            shares = low.astype(F32)
            grad_shares = mm_nt(gs, s["v"][p])
            inner = jnp.sum(grad_shares * shares, axis=-1, keepdims=True)
            grad_scores = (shares * (grad_shares - inner)).astype(BF16)
            s["grad_k"][p] += mm_tn(grad_scores, qs)
            grad_q = mm(grad_scores, s["k"][p])
            flipped = mm(flip, grad_scores)
            wide = jnp.concatenate([flipped, jnp.zeros((2 * RB, RB), F32)], axis=1)
            spread = jnp.concatenate(
                [
                    pltpu.roll(wide[:RB], 0, 1, stride=1, stride_axis=0),
                    pltpu.roll(wide[RB:], 0, 1, stride=1, stride_axis=0),
                ],
                axis=0,
            ).astype(BF16)
            q_flipped = mm(flip, qs).astype(BF16)
            s["grad_table"][table_rows_of(i), :] += mm_tn(spread, q_flipped)
            turned = mm(spread, s["table"][table_rows_of(i), :])
            high = turned.astype(BF16)
            rest = (turned - high.astype(F32)).astype(BF16)
            grad_q = unstack(grad_q + (mm(flip, high) + mm(flip, rest))).astype(BF16)
            cols = pl.ds(pl.multiple_of(p * 128, 128), 128)
            s["grad_pre"][rows, cols] = (grad_q.astype(F32) * head_scale).astype(BF16)
            return carry

        lax.fori_loop(0, pairs, pair_step, 0)
        if ring:
            x_done(i)
        return carry

    lax.fori_loop(0, blocks, attend_back, 0)
    pl.semaphore_signal(s["free"].at[1], inc=1, device_id=y_peer, device_id_type=MESH)

    for p in range(pairs):
        at = local + p * 128
        s["grad_pre"][:, at : at + 128] = s["grad_k"][p].astype(BF16)
        at += local
        s["grad_pre"][:, at : at + 128] = s["grad_v"][p].astype(BF16)
    for i in range(blocks):
        sum_copy("gn2", i).wait_send()
    pl.semaphore_wait(s["free"].at[1], 1)

    def back_copy(i):
        rows = pl.ds(pl.multiple_of(i * RB, RB), RB)
        return remote(s["gn2_send"].at[rows], s["gn2_recv"].at[rows], "gn1", i, y_peer)

    def project_back(b, carry):
        start = pl.multiple_of(b * RF, RF)
        rows = pl.ds(start, RF)
        total = (
            mm_nt(s["grad_pre"][rows, 0:local], attn_in[0])
            + mm_nt(s["grad_pre"][rows, local : 2 * local], attn_in[1])
            + mm_nt(s["grad_pre"][rows, 2 * local : 3 * local], attn_in[2])
        )
        s["gn2_send"][rows, :] = total
        for j in range(RF // RB):
            back_copy(b * (RF // RB) + j).start()
        unit, unused = norm_stats(hidden[rows, :].astype(F32))
        s["n1"][0:1, :] += col_sum(total * unit)
        s["n1"][1:2, :] += col_sum(total)
        return carry

    lax.fori_loop(0, slots // RF, project_back, 0)

    def put(at, row):
        for j in range(row.shape[1] // 128):
            g_vec_acc[at + j : at + j + 1, :] = row[:, j * 128 : (j + 1) * 128]

    put(V_N1G, s["n1"][0:1, :])
    put(V_N1B, s["n1"][1:2, :])
    put(V_N2G, s["n2"][0:1, :])
    put(V_N2B, s["n2"][1:2, :])
    put(V_AOB, s["aob"][...])
    put(V_FOB, s["fob"][...])
    put(V_FIB, s["fib"][...])
    put(V_AIB, col_sum(s["grad_pre"][:, 0:local].astype(F32)))
    put(V_AIB + pairs, col_sum(s["grad_pre"][:, 2 * local : 3 * local].astype(F32)))
    grad_rel = None
    rest = s["grad_table"][...]
    for part in range(3):
        piece16 = rest.astype(BF16)
        term = mm_tn(pick, piece16)
        grad_rel = term if part == 0 else grad_rel + term
        rest = rest - piece16.astype(F32)
    grad_rel = grad_rel + pltpu.roll(grad_rel, HD, 1)
    fold = lax.broadcasted_iota(jnp.int32, (reach, 128), 1) < HD
    g_vec_acc[V_REL : V_REL + reach, :] = jnp.where(fold, grad_rel[:reach], grad_rel[reach:])

    def vec_step(step, peer, count):
        rows = pl.ds(0, count)
        return remote(s["vec_send"].at[step, rows], s["vec_recv"].at[step, rows], "vec", step, peer)

    def share(step, peer, count):
        s["vec_send"][step, 0:count] = g_vec_acc[0:count, :]
        vec_step(step, peer, count).start()

    def merge(step, peer, count):
        vec_step(step, peer, count).wait_recv()
        g_vec_acc[0:count, :] = s["vec_send"][step, 0:count] + s["vec_recv"][step, 0:count]

    if ring:
        z_low = (dp + 4 - 8 * lax.rem(z_at, 2), ten)
        z_high = (lax.rem(dp + 8, 16), ten)
        vec_peers = [y_peer, core_peer, x_peer, z_low, z_high]
        share(1, core_peer, VROWS)

    if ring:
        next_group(SLOTS)

    def attn_grad(which, carry):
        cols = pl.ds(pl.multiple_of(which * local, 128), local)
        keep(grad_chunk(s["normed_t"], s["grad_pre"].at[:, cols]), ffn_chunks + which, which)
        return carry

    lax.fori_loop(0, 3, attn_grad, 0)
    context = jnp.concatenate([s["ctx"][ten * pairs + p] for p in range(pairs)], axis=1)
    keep(mm(s["wo"][:, 0:slots], context), ffn_chunks + 3, 3)

    def results(at, near, far):
        return pltpu.make_async_copy(near, far, s["out_dma"].at[at])

    def finish_out(i, carry):
        start = pl.multiple_of(i * RB, RB)
        rows = pl.ds(start, RB)
        sum_copy("out", i).wait_recv()
        branch = s["out_send"][rows, :] + s["out_recv"][rows, :]
        total = s["middle"][rows, :] + (branch + out_bias2)
        output[rows, :] = (total * valid_rows(start, RB)).astype(BF16)
        results(i, output.at[rows], far_output.at[rows]).start()
        return carry

    def finish_hidden(i, carry):
        rows = pl.ds(pl.multiple_of(i * RB, RB), RB)
        back_copy(i).wait_recv()
        grad_normed = s["gn2_send"][rows, :] + s["gn2_recv"][rows, :]
        unit, scale = norm_stats(hidden[rows, :].astype(F32))
        total = s["grad_middle"][rows, :] + norm_back(grad_normed, unit, scale, gain1)
        grad_hidden[rows, :] = total.astype(BF16)
        results(blocks + i, grad_hidden.at[rows], far_grad_hidden.at[rows]).start()
        return carry

    def finish_grad(c, carry):
        s["grads"][c] = z_done(c)
        results(2 * blocks + 1 + c, s["grads"].at[c], far_grads.at[c]).start()
        return carry

    def x_range(first, last):
        lax.fori_loop(first, last, lambda c, carry: (x_done(c), carry)[1], 0)

    vec_out = results(2 * blocks, g_vec_acc, far_vec)
    chunks = ffn_chunks + attn_chunks
    if ring:
        merge(1, core_peer, VROWS)
        share(2, x_peer, VROWS)
        group_done(ffn_chunks)
        x_range(blocks, ffn_chunks)
        merge(2, x_peer, VROWS)
        share(3, z_low, VROWS)
        x_done(ffn_chunks)
        merge(3, z_low, VROWS)
        share(4, z_high, VROWS)
        x_done(ffn_chunks + 1)
        merge(4, z_high, VROWS)
        share(0, y_peer, YROWS)
        lax.fori_loop(0, blocks, finish_out, 0)
        x_range(ffn_chunks + 2, chunks)
        lax.fori_loop(0, ffn_chunks, finish_grad, 0)
        lax.fori_loop(0, blocks - 1, finish_hidden, 0)
        lax.fori_loop(ffn_chunks, chunks, finish_grad, 0)
        merge(0, y_peer, YROWS)
        vec_out.start()
        finish_hidden(blocks - 1, 0)
    else:
        share(0, y_peer, YROWS)
        lax.fori_loop(0, blocks, finish_out, 0)
        merge(0, y_peer, YROWS)
        vec_out.start()
        lax.fori_loop(0, blocks, finish_hidden, 0)

    wo_y(0).wait_send()
    if ring:
        wo_y(1).wait_send()
        for h in range(2):
            wo_x(h).wait_send()
            wo_core(h).wait_send()
            wo_core_far(h).wait_send()

    def sent(i, carry):
        ctx_copy(i).wait_send()
        sum_copy("out", i).wait_send()
        back_copy(i).wait_send()
        return carry

    lax.fori_loop(0, blocks, sent, 0)
    vec_step(0, y_peer, YROWS).wait_send()
    if ring:
        for step in (1, 2, 3, 4):
            vec_step(step, vec_peers[step], VROWS).wait_send()

        def grads_sent(c, carry):
            x_copy(c).wait_send()
            for copy in z_copies(c):
                copy.wait_send()
            return carry

        lax.fori_loop(0, chunks, grads_sent, 0)
        for c in range(SLOTS):
            core_copy(ffn_chunks + c, c).wait_send()
        lax.fori_loop(
            0, chunks,
            lambda c, carry: (results(2 * blocks + 1 + c, s["grads"].at[c], far_grads.at[c]).wait(), carry)[1], 0,
        )
    for i in range(blocks):
        rows = slice(i * RB, (i + 1) * RB)
        results(i, output.at[rows], far_output.at[rows]).wait()
        results(blocks + i, grad_hidden.at[rows], far_grad_hidden.at[rows]).wait()
    vec_out.wait()


def scratch_of(ring, slots, width, local, units, chunks, ffn_chunks):
    pairs = local // 128
    blocks = slots // RB
    halves = slots // RF
    vm, dma = pltpu.VMEM, pltpu.SemaphoreType.DMA
    shapes = dict(
        hidden=vm((slots, width), BF16),
        attn_in=vm((3, width, local), BF16),
        attn_out=vm((local, width), BF16),
        ffn_in=vm((width, units), BF16),
        ffn_out=vm((units, width), BF16),
        cotangent=vm((slots, width), BF16),
        output=vm((slots, width), BF16),
        grad_hidden=vm((slots, width), BF16),
        in_s=dma((6,)),
        out_dma=dma((2 * blocks + 1 + chunks,)),
        normed_t=vm((halves, width, RF), BF16),
        q=vm((pairs, slots, 128), BF16),
        k=vm((pairs, slots, 128), BF16),
        v=vm((pairs, slots, 128), BF16),
        table=vm((2 * slots, 128), BF16),
        probs=vm((pairs, blocks, 2 * RB, slots), BF16),
        ctx=vm((2 * pairs, slots, 128), BF16),
        ctx_send=vm((pairs, slots, 128), F32),
        ctx_recv=vm((pairs, slots, 128), F32),
        wo=vm((2 * local, width), BF16),
        wo_stage=vm((2, local // 8, width) if ring else (local, width), F32),
        wo_recv=vm((8, local // 8, width) if ring else (local, width), F32),
        middle=vm((slots, width), F32),
        normed2_t=vm((halves, width, RF), BF16),
        top_t=vm((halves, width, RF), BF16),
        active=vm((slots, units), BF16),
        grad_pre=vm((slots, units), BF16),
        gn2_send=vm((slots, width), F32),
        gn2_recv=vm((slots, width), F32),
        out_send=vm((slots, width), F32),
        out_recv=vm((slots, width), F32),
        grad_middle=vm((slots, width), F32),
        grad_ctx=vm((pairs, RB, 128), BF16),
        grad_k=vm((pairs, slots, 128), F32),
        grad_v=vm((pairs, slots, 128), F32),
        grad_table=vm((2 * slots, 128), F32),
        vec=vm((VROWS, 128), F32),
        vec_send=vm((5 if ring else 1, VROWS, 128), F32),
        vec_recv=vm((5 if ring else 1, VROWS, 128), F32),
        fib=vm((1, units), F32),
        fob=vm((1, width), F32),
        aob=vm((1, width), F32),
        n1=vm((2, width), F32),
        n2=vm((2, width), F32),
        ffn_in_bias=vm((1, units), F32),
        free=pltpu.SemaphoreType.REGULAR((2,)),
        wo_s=dma((8,)), wo_r=dma((8,)),
        ctx_s=dma((blocks,)), ctx_r=dma((blocks,)),
        gn2_s=dma((blocks,)), gn2_r=dma((blocks,)),
        gn1_s=dma((blocks,)), gn1_r=dma((blocks,)),
        out_s=dma((blocks,)), out_r=dma((blocks,)),
        vec_s=dma((5,)), vec_r=dma((5,)),
    )
    if ring:
        shapes.update(
            g_own=vm((chunks, 4, 2, 48, CW), F32),
            g_send=vm((SLOTS, 4, 2, 48, CW), F32),
            core_recv=vm((SLOTS, 4, 2, 48, CW), F32),
            x_recv=vm((chunks, 4, 48, CW), F32),
            z_recv=vm((chunks, 3, 48, CW), F32),
            grads=vm((chunks, 48, CW), F32),
            gc_s=dma((chunks,)), gc_r=dma((chunks,)),
            gx_s=dma((chunks,)), gx_r=dma((chunks,)),
            gz_s=dma((3 * chunks,)), gz_r=dma((3 * chunks,)),
        )
    return shapes


def place(
    output_in, grad_hidden_in, grads_in, vec,
    output, grad_hidden, g_attn_in, g_attn_in_bias, g_rel_t, g_attn_out_t, g_attn_out_bias,
    g_norm1_gain, g_norm1_bias, g_norm2_gain, g_norm2_bias, g_ffn_in, g_ffn_in_bias, g_ffn_out_t, g_ffn_out_bias,
):
    per = g_ffn_in.shape[1] // CW
    output[...] = output_in[...]
    grad_hidden[...] = grad_hidden_in[...]
    g_attn_in[...] = grads_in[2 * per : 2 * per + 3]
    g_attn_out_t[...] = grads_in[2 * per + 3]
    for c in range(per):
        cols = slice(c * CW, (c + 1) * CW)
        g_ffn_out_t[:, cols] = grads_in[c]
        g_ffn_in[:, cols] = grads_in[per + c]
    for ref, at in (
        (g_attn_out_bias, V_AOB), (g_norm1_gain, V_N1G), (g_norm1_bias, V_N1B), (g_norm2_gain, V_N2G),
        (g_norm2_bias, V_N2B), (g_ffn_in_bias, V_FIB), (g_ffn_out_bias, V_FOB),
    ):
        ref[...] = vec[at : at + ref.shape[0], :]
    local = g_attn_in_bias.shape[1]
    for k in range(2):
        at = V_AIB + k * (local // 128)
        g_attn_in_bias[k : k + 1, :] = jnp.concatenate(
            [vec[at + j : at + j + 1, :] for j in range(local // 128)], axis=1
        )
    reach = g_rel_t.shape[1] // 2
    turned = vec[V_REL : V_REL + reach, :].T
    g_rel_t[...] = jnp.concatenate([turned[:HD], turned[HD:]], axis=1)


def on_device(
    ring,
    hidden, lengths, attn_in, attn_in_bias, rel_table, attn_out, attn_out_bias,
    norm1_gain, norm1_bias, norm2_gain, norm2_bias,
    ffn_in, ffn_in_bias, ffn_out, ffn_out_bias, cotangent,
):
    slots, width = hidden.shape
    local = attn_out.shape[0]
    units = ffn_in.shape[1]
    table_rows = rel_table.shape[0]
    ffn_chunks = 2 * units // CW
    chunks = ffn_chunks + 4
    rows = width // 16
    shape = jax.ShapeDtypeStruct
    shapes = scratch_of(ring, slots, width, local, units, chunks, ffn_chunks)
    names = tuple(shapes)
    outs = [shape((slots, width), BF16), shape((slots, width), BF16), shape((chunks, rows, CW), F32), shape((VROWS, 128), F32)]
    far = pl.BlockSpec(memory_space=pl.ANY)
    near = pl.BlockSpec(memory_space=pltpu.VMEM)
    out_specs = [far] * 4
    if not ring:
        names = ("g_full",) + names
        outs.append(shape((chunks, width, CW), F32))
        out_specs.append(near)

    def lanes(vector):
        return vector.reshape(vector.shape[0] // 128, 128)

    def unlanes(array):
        return array.reshape(array.shape[0] * 128)

    results = pl.pallas_call(
        partial(body, ring, names),
        out_shape=outs,
        in_specs=[pl.BlockSpec(memory_space=pltpu.SMEM)] + [near] * 9 + [far] * 6,
        out_specs=out_specs,
        scratch_shapes=list(shapes.values()),
        compiler_params=pltpu.CompilerParams(
            collective_id=0, has_side_effects=True, vmem_limit_bytes=64 * 1024 * 1024
        ),
    )(
        lengths, attn_in_bias, rel_table.T, lanes(attn_out_bias), lanes(norm1_gain), lanes(norm1_bias),
        lanes(norm2_gain), lanes(norm2_bias), lanes(ffn_in_bias), lanes(ffn_out_bias),
        hidden, attn_in, attn_out, ffn_in, ffn_out, cotangent,
    )
    if ring:
        vector = shape((width // 128, 128), F32)
        placed = pl.pallas_call(
            place,
            out_shape=[
                outs[0], outs[1], shape((3, rows, local), F32), shape((2, local), F32), shape((HD, table_rows), F32),
                shape((rows, local), F32), vector, vector, vector, vector, vector,
                shape((rows, units), F32), shape((units // 128, 128), F32), shape((rows, units), F32), vector,
            ],
            in_specs=[near] * 4,
            out_specs=[near] * 15,
        )(*results)
        (
            output, grad_hidden, g_attn_in, g_attn_in_bias, g_rel_t, g_attn_out_t, g_attn_out_bias, n1g, n1b, n2g, n2b,
            g_ffn_in, g_ffn_in_bias, g_ffn_out_t, g_ffn_out_bias,
        ) = placed
        return (
            output, grad_hidden, g_attn_in, g_attn_in_bias, g_rel_t.T, g_attn_out_t.T, unlanes(g_attn_out_bias),
            unlanes(n1g), unlanes(n1b), unlanes(n2g), unlanes(n2b),
            g_ffn_in, unlanes(g_ffn_in_bias), g_ffn_out_t.T, unlanes(g_ffn_out_bias),
        )
    output, grad_hidden, unused, vec, full = results
    per = units // CW
    wide = jnp.swapaxes(full[: 2 * per].reshape(2, per, width, CW), 1, 2).reshape(2, width, units)

    def scatter(value, dim):
        return lax.psum_scatter(value, "dp", scatter_dimension=dim, tiled=True)

    g_ffn_out = scatter(wide[0].T, 1)
    g_ffn_in = scatter(wide[1], 0)
    g_attn_in = scatter(full[2 * per : 2 * per + 3], 1)
    g_attn_out = scatter(full[2 * per + 3].T, 1)
    vec = lax.psum(vec, "dp")

    def row(at, count=width):
        return unlanes(vec[at : at + count // 128])

    rel_pairs = vec[V_REL : V_REL + table_rows // 2]
    grad_rel = jnp.concatenate([rel_pairs[:, :HD], rel_pairs[:, HD:]], axis=0)
    return (
        output, grad_hidden, g_attn_in,
        row(V_AIB, 2 * local).reshape(2, local), grad_rel, g_attn_out, row(V_AOB),
        row(V_N1G), row(V_N1B), row(V_N2G), row(V_N2B),
        g_ffn_in, row(V_FIB, units), g_ffn_out, row(V_FOB),
    )


def solution(mesh):
    ring = mesh.shape["dp"] == 16
    return jax.shard_map(
        partial(on_device, ring),
        mesh=mesh,
        in_specs=(
            P("dp", None), P("dp"), P(None, None, "tensor"), P(None, "tensor"), P(),
            P("tensor", None), P(), P(), P(), P(), P(),
            P(None, "tensor"), P("tensor"), P("tensor", None), P(), P("dp", None),
        ),
        out_specs=(
            P("dp", None), P("dp", None), P(None, "dp", "tensor"), P(None, "tensor"), P(),
            P("tensor", "dp"), P(), P(), P(), P(), P(),
            P("dp", "tensor"), P("tensor"), P("tensor", "dp"), P(),
        ),
        check_vma=False,
    )
```

```python
from functools import partial
from types import SimpleNamespace

import jax
import jax.numpy as jnp
from jax import lax
from jax.experimental import pallas as pl
from jax.experimental.pallas import tpu as pltpu
from jax.sharding import PartitionSpec as P

HD = 64
EPSILON = 1e-05
NEGATIVE = -1e30
SQRT_HALF = 0.7071067811865476
INV_SQRT_2PI = 0.3989422804014327
RB = 128
RF = 256
CW = 384
FULL = "g_full"
Z_FIRST = (1, 4)
SLOTS = 4
MESH = pl.DeviceIdType.MESH
F32 = jnp.float32
BF16 = jnp.bfloat16


def mm(a, b):
    return jnp.dot(a, b, preferred_element_type=F32)


def mm_nt(a, b):
    return lax.dot_general(a, b, (((1,), (1,)), ((), ())), preferred_element_type=F32)


def mm_tn(a, b):
    return lax.dot_general(a, b, (((0,), (0,)), ((), ())), preferred_element_type=F32)


def norm_stats(value):
    mean = jnp.mean(value, axis=-1, keepdims=True)
    centred = value - mean
    scale = lax.rsqrt(jnp.mean(centred * centred, axis=-1, keepdims=True) + EPSILON)
    return centred * scale, scale


def norm_back(grad, unit, scale, gain):
    grad_unit = grad * gain
    inner = (
        grad_unit
        - jnp.mean(grad_unit, axis=-1, keepdims=True)
        - unit * jnp.mean(grad_unit * unit, axis=-1, keepdims=True)
    )
    return inner * scale


def col_sum(value):
    return jnp.sum(value, axis=0, keepdims=True)


def lanes_of(ref3, rows):
    return jnp.concatenate([ref3[p, rows, :] for p in range(ref3.shape[0])], axis=1)


V_N1G, V_N1B, V_AOB, V_N2G, V_N2B, V_REL, V_FOB, V_FIB, V_AIB = 0, 6, 12, 18, 24, 32, 192, 198, 210
YROWS, VROWS = 192, 216


def body(
    ring, names,
    lengths, attn_in_bias, rel_table_t, attn_out_bias, norm1_gain, norm1_bias, norm2_gain, norm2_bias,
    ffn_in_bias, ffn_out_bias, far_hidden, far_attn_in, far_attn_out, far_ffn_in, far_ffn_out, far_cotangent,
    far_output, far_grad_hidden, far_attn_in_grad, far_attn_out_grad, far_ffn_in_grad, far_ffn_out_grad, far_vec,
    *scratch,
):
    s = SimpleNamespace(**dict(zip(names, scratch)))

    def bring(at, near, far):
        copy = pltpu.make_async_copy(far, near, s.in_s.at[at])
        copy.start()
        return copy

    bring_attn_out = bring(0, s.attn_out, far_attn_out)
    bring_hidden = bring(1, s.hidden, far_hidden)
    bring_attn_in = bring(2, s.attn_in, far_attn_in)
    hidden, attn_in, attn_out = s.hidden, s.attn_in, s.attn_out
    cotangent, ffn_in, ffn_out = s.cotangent, s.ffn_in, s.ffn_out
    output, grad_hidden = s.output, s.grad_hidden
    slots, width = hidden.shape
    local = attn_out.shape[0]
    pairs = local // 128
    units = ffn_in.shape[1]
    table_rows = rel_table_t.shape[1]
    reach = table_rows // 2
    blocks = slots // RB
    ext = slots + RB
    head_scale = HD ** (-0.5)

    dp = lax.axis_index("dp")
    ten = lax.axis_index("tensor")
    y_peer = (dp, 1 - ten)
    if ring:
        core = lax.rem(dp, 2)
        x_at = lax.rem(lax.div(dp, 2), 2)
        z_low_at = lax.rem(lax.div(dp, 4), 2)
        z_high_at = lax.div(dp, 8)
        core_peer = (dp + 1 - 2 * core, ten)
        x_peer = (dp + 2 - 4 * x_at, ten)
        z_low = (dp + 4 - 8 * z_low_at, ten)
        z_high = (dp + 8 - 16 * z_high_at, ten)
        greet = [y_peer, core_peer, x_peer, z_low, z_high]
    else:
        greet = [y_peer]

    barrier = pltpu.get_barrier_semaphore()
    for peer in greet:
        pl.semaphore_signal(barrier, inc=1, device_id=peer, device_id_type=MESH)

    def remote(src, dst, sems, at, peer):
        return pltpu.make_async_remote_copy(
            src_ref=src, dst_ref=dst, send_sem=sems.at[0, at], recv_sem=sems.at[1, at],
            device_id=peer, device_id_type=MESH,
        )

    bring_attn_out.wait()
    if ring:
        piece = local // 8
        mine = (2 * z_low_at + x_at) * 2 + core
        s.wo_stage[...] = attn_out[pl.ds(pl.multiple_of(mine * piece, 16), piece), :].astype(F32)

        def wo_y():
            return remote(s.wo_stage, s.wo_recv.at[z_low_at, x_at, core], s.wo_sem, 0, y_peer)

        def wo_pass(part, at, peer):
            return remote(part, part, s.wo_sem, at, peer)

        def wo_x():
            return wo_pass(s.wo_recv.at[z_low_at, x_at, core], 1, x_peer)

        def wo_z():
            return wo_pass(s.wo_recv.at[z_low_at, x_at, core], 2, z_low)

        def wo_xz():
            return wo_pass(s.wo_recv.at[z_low_at, 1 - x_at, core], 3, z_low)

        def wo_core(near):
            return wo_pass(s.wo_recv.at[z_low_at if near else 1 - z_low_at, :, core], 4 if near else 5, core_peer)
    else:
        s.wo_stage[...] = attn_out[...].astype(F32)

        def wo_y():
            return remote(s.wo_stage, s.wo_recv, s.wo_sem, 0, y_peer)

    pl.semaphore_wait(barrier, len(greet))
    wo_y().start()

    def flat(ref):
        value = ref[...].astype(F32)
        return jnp.concatenate([value[j : j + 1] for j in range(value.shape[0])], axis=1)

    bias_q = attn_in_bias[0:1, :].astype(F32)
    bias_v = attn_in_bias[1:2, :].astype(F32)
    gain1, offset1 = flat(norm1_gain), flat(norm1_bias)
    gain2, offset2 = flat(norm2_gain), flat(norm2_bias)
    out_bias1, out_bias2 = flat(attn_out_bias), flat(ffn_out_bias)
    s.ffn_in_bias[...] = flat(ffn_in_bias)
    seq_len = lengths[0]

    ext_rows = 2 * slots
    distance = slots - 1 - lax.broadcasted_iota(jnp.int32, (ext_rows, table_rows), 0)
    bucket = jnp.clip(distance, -reach, reach - 1) + reach
    pick = (bucket == lax.broadcasted_iota(jnp.int32, (ext_rows, table_rows), 1)).astype(BF16)
    rel_t = rel_table_t[...]
    s.table[...] = mm_nt(pick, jnp.concatenate([rel_t, rel_t], axis=0)).astype(BF16)

    def project(i, carry):
        rows = pl.ds(pl.multiple_of(i * RF, RF), RF)
        unit, unused = norm_stats(hidden[rows, :].astype(F32))
        normed = (unit * gain1 + offset1).astype(BF16)
        s.normed_t[i] = normed.T
        q = ((mm(normed, attn_in[0]) + bias_q) * head_scale).astype(BF16)
        k = mm(normed, attn_in[1]).astype(BF16)
        v = (mm(normed, attn_in[2]) + bias_v).astype(BF16)
        for p in range(pairs):
            s.q[p, rows, :] = q[:, p * 128 : (p + 1) * 128]
            s.k[p, rows, :] = k[:, p * 128 : (p + 1) * 128]
            s.v[p, rows, :] = v[:, p * 128 : (p + 1) * 128]
        return carry

    bring_hidden.wait()
    bring_attn_in.wait()
    bring_cotangent = bring(3, s.cotangent, far_cotangent)
    bring_ffn_in = bring(4, s.ffn_in, far_ffn_in)
    bring_ffn_out = bring(5, s.ffn_out, far_ffn_out)
    lax.fori_loop(0, slots // RF, project, 0)

    low_lanes = lax.broadcasted_iota(jnp.int32, (RB, 128), 1) < HD
    key_ok = lax.broadcasted_iota(jnp.int32, (1, slots), 1) < seq_len

    def stack(both):
        zero = jnp.zeros_like(both)
        return jnp.concatenate([jnp.where(low_lanes, both, zero), jnp.where(low_lanes, zero, both)], axis=0)

    def unstack(tall):
        return jnp.where(low_lanes, tall[:RB], tall[RB:])

    def table_rows_of(i):
        return pl.ds(pl.multiple_of(slots - RB - i * RB, RB), ext)

    def ctx_copy(i, p):
        rows = pl.ds(pl.multiple_of(i * RB, RB), RB)
        return remote(s.ctx_send.at[p, rows], s.ctx_recv.at[p, rows], s.ctx_sem, i * pairs + p, y_peer)

    def attend(i):
        rows = pl.ds(pl.multiple_of(i * RB, RB), RB)

        def pair_step(p, carry):
            qs = stack(s.q[p, rows, :])
            spread = mm_nt(qs, s.table[table_rows_of(i), :])
            shift = ext - RB + 1
            bias = jnp.concatenate(
                [
                    pltpu.roll(spread[:RB], shift, 1, stride=1, stride_axis=0)[:, :slots],
                    pltpu.roll(spread[RB:], shift, 1, stride=1, stride_axis=0)[:, :slots],
                ],
                axis=0,
            )
            scores = jnp.where(key_ok, mm_nt(qs, s.k[p]) + bias, NEGATIVE)
            expon = jnp.exp(scores - jnp.max(scores, axis=-1, keepdims=True))
            shares = (expon * (1.0 / jnp.sum(expon, axis=-1, keepdims=True))).astype(BF16)
            s.probs[p, i] = shares
            context = unstack(mm(shares, s.v[p])).astype(BF16)
            s.ctx[ten * pairs + p, rows, :] = context
            s.ctx_send[p, rows, :] = context.astype(F32)
            ctx_copy(i, p).start()
            return carry

        lax.fori_loop(0, pairs, pair_step, 0)

    half = pl.ds(pl.multiple_of(ten * local, 128), local)
    far_half = pl.ds(pl.multiple_of((1 - ten) * local, 128), local)
    s.wo[half, :] = attn_out[...]
    attend(0)
    if ring:
        wo_y().wait_recv()
        wo_x().start()
        wo_z().start()
    attend(1)
    if ring:
        wo_x().wait_recv()
        wo_xz().start()
        wo_core(True).start()
    attend(2)
    attend(3)

    if ring:
        wo_z().wait_recv()
        wo_xz().wait_recv()
        wo_core(False).start()
        wo_core(True).wait_recv()
        wo_core(False).wait_recv()
        s.wo[far_half, :] = s.wo_recv[...].reshape(local, width).astype(BF16)
    else:
        wo_y().wait_recv()
        s.wo[far_half, :] = s.wo_recv[...].astype(BF16)
    bring_cotangent.wait()
    bring_ffn_in.wait()
    bring_ffn_out.wait()

    def valid_rows(start, count):
        return (lax.broadcasted_iota(jnp.int32, (count, 1), 0) + start < seq_len).astype(F32)

    def gn2_copy(j):
        rows = pl.ds(pl.multiple_of((2 * j + 1 - ten) * RB, RB), RB)
        return remote(s.gn2_send.at[rows], s.gn2_recv.at[j], s.gn2_sem, j, y_peer)

    def grad_ctx_copy(j):
        return remote(s.grad_ctx_send.at[j], s.grad_ctx_recv.at[j], s.grad_ctx_sem, j, y_peer)

    def out_copy(i):
        rows = pl.ds(pl.multiple_of(i * RB, RB), RB)
        return remote(s.out_send.at[rows], s.out_recv.at[rows], s.out_sem, i, y_peer)

    g_vec_acc = s.vec
    g_vec_acc[...] = jnp.zeros_like(g_vec_acc)
    s.fib[...] = jnp.zeros_like(s.fib)
    s.fob[...] = jnp.zeros_like(s.fob)
    s.aob[...] = jnp.zeros_like(s.aob)
    s.n1[...] = jnp.zeros_like(s.n1)
    s.n2[...] = jnp.zeros_like(s.n2)

    step_units = 512

    def feed(b):
        start = b * RF
        rows = slice(start, start + RF)
        for j in range(RF // RB):
            for p in range(pairs):
                ctx_copy(b * (RF // RB) + j, p).wait_recv()
        for p in range(pairs):
            s.ctx[(1 - ten) * pairs + p, rows, :] = s.ctx_recv[p, rows, :].astype(BF16)
        attended = mm(lanes_of(s.ctx, rows), s.wo[...]) + out_bias1
        middle = hidden[rows, :].astype(F32) + attended
        s.middle[rows, :] = middle
        unit, unused = norm_stats(middle)
        normed = (unit * gain2 + offset2).astype(BF16)
        s.normed2_t[b] = normed.T
        top = cotangent[rows, :].astype(F32) * valid_rows(start, RF)
        s.fob[...] += col_sum(top)
        top = top.astype(BF16)
        s.top_t[b] = top.T
        for c in range(units // step_units):
            cols = slice(c * step_units, (c + 1) * step_units)
            pre = mm(normed, ffn_in[:, cols]) + s.ffn_in_bias[:, cols]
            share = 0.5 + 0.5 * lax.erf(pre * SQRT_HALF)
            active = (pre * share).astype(BF16)
            s.active[rows, cols] = active
            slope = share + pre * (jnp.exp(-0.5 * pre * pre) * INV_SQRT_2PI)
            grad_pre = (mm_nt(top, ffn_out[cols, :]) * slope).astype(BF16)
            s.grad_pre[rows, cols] = grad_pre
            s.fib[:, cols] += col_sum(grad_pre.astype(F32))
            back = mm_nt(grad_pre, ffn_in[:, cols])
            onward = mm(active, ffn_out[cols, :])
            if c == 0:
                s.gn2_send[rows, :] = back
                s.out_send[rows, :] = onward
            else:
                s.gn2_send[rows, :] += back
                s.out_send[rows, :] += onward
        gn2_copy(b).start()

    feed(0)

    def grad_chunk(left_t, right):
        total = mm(left_t[0], right[0:RF])
        for b in range(1, slots // RF):
            total += mm(left_t[b], right[b * RF : (b + 1) * RF])
        return total

    per = units // CW
    first_wo, first_in = 2 * per, 2 * per + 2
    chunks = first_in + 3

    def hold(total, chunk, begun=False):
        if not ring:
            s.g_full[chunk] = s.g_full[chunk] + total if begun else total
            return
        slot = chunk % SLOTS
        parts = total.reshape(8, 2, 48, CW)
        even, odd = parts[:, 0], parts[:, 1]
        near = jnp.where(core == 0, even, odd).reshape(2, 2, 2, 48, CW)
        far = jnp.where(core == 0, odd, even).reshape(2, 2, 2, 48, CW)
        s.g_own[chunk] = s.g_own[chunk] + near if begun else near
        s.g_send[slot] = s.g_send[slot] + far if begun else far

    def keep(total, chunk, begun=False):
        if ring and chunk >= SLOTS:
            core_copy(chunk - SLOTS).wait_send()
            pl.semaphore_wait(s.free.at[chunk % SLOTS], 1)
        hold(total, chunk, begun)
        if ring:
            core_copy(chunk).start()

    def core_copy(chunk):
        slot = chunk % SLOTS
        return remote(s.g_send.at[slot], s.core_recv.at[slot], s.gc_sem, chunk, core_peer)

    def first_copy(chunk):
        own = s.g_own.at[chunk]
        if chunk in Z_FIRST:
            return remote(own.at[:, 1 - z_low_at], s.first_recv.at[chunk], s.g1_sem, chunk, z_low)
        return remote(own.at[:, :, 1 - x_at], s.first_recv.at[chunk], s.g1_sem, chunk, x_peer)

    def second_copy(chunk):
        own = s.g_own.at[chunk]
        into = s.late_recv.at[chunk, 0:2]
        if chunk in Z_FIRST:
            return remote(own.at[1 - z_high_at, z_low_at], into, s.g2_sem, chunk, z_high)
        return remote(own.at[:, 1 - z_low_at, x_at], into, s.g2_sem, chunk, z_low)

    def third_copy(chunk):
        own = s.g_own.at[chunk]
        into = s.late_recv.at[chunk, 2]
        if chunk in Z_FIRST:
            return remote(own.at[z_high_at, z_low_at, 1 - x_at], into, s.g3_sem, chunk, x_peer)
        return remote(own.at[1 - z_high_at, z_low_at, x_at], into, s.g3_sem, chunk, z_high)

    def core_done(*which):
        for chunk in which if ring else ():
            core_copy(chunk).wait_recv()
            s.g_own[chunk] = s.g_own[chunk] + s.core_recv[chunk % SLOTS]
            if chunk + SLOTS < chunks:
                pl.semaphore_signal(s.free.at[chunk % SLOTS], inc=1, device_id=core_peer, device_id_type=MESH)
            first_copy(chunk).start()

    def first_done(*which):
        for chunk in which if ring else ():
            first_copy(chunk).wait_recv()
            if chunk in Z_FIRST:
                s.g_own[chunk, :, z_low_at] = s.g_own[chunk, :, z_low_at] + s.first_recv[chunk]
            else:
                s.g_own[chunk, :, :, x_at] = s.g_own[chunk, :, :, x_at] + s.first_recv[chunk]
            second_copy(chunk).start()

    def second_done(*which):
        for chunk in which if ring else ():
            second_copy(chunk).wait_recv()
            if chunk in Z_FIRST:
                s.g_own[chunk, z_high_at, z_low_at] = s.g_own[chunk, z_high_at, z_low_at] + s.late_recv[chunk, 0:2]
            else:
                s.g_own[chunk, :, z_low_at, x_at] = s.g_own[chunk, :, z_low_at, x_at] + s.late_recv[chunk, 0:2]
            third_copy(chunk).start()

    def results(at, near, far):
        return pltpu.make_async_copy(near, far, s.out_dma.at[at])

    def grad_result(chunk):
        if chunk < per:
            far = far_ffn_out_grad.at[:, chunk * CW : (chunk + 1) * CW]
        elif chunk < 2 * per:
            far = far_ffn_in_grad.at[:, (chunk - per) * CW : (chunk - per + 1) * CW]
        else:
            far = far_attn_in_grad.at[chunk - first_in]
        return results(2 * blocks + 1 + chunk, s.grads.at[chunk], far)

    def third_done(*which):
        for chunk in which if ring else ():
            third_copy(chunk).wait_recv()
            s.grads[chunk] = s.g_own[chunk, z_high_at, z_low_at, x_at] + s.late_recv[chunk, 2]
            if not first_wo <= chunk < first_in:
                grad_result(chunk).start()

    def wo_grad_copy():
        return remote(s.grads.at[first_wo + 1 - ten], s.wo_grad_recv, s.wo_grad_sem, 0, y_peer)

    def wo_grad_done():
        wo_grad_copy().wait_recv()
        s.wo_grad[...] = s.grads[first_wo + ten] + s.wo_grad_recv[...]
        wo_grad_result().start()

    def wo_grad_result():
        return results(2 * blocks + 1 + first_wo, s.wo_grad, far_attn_out_grad)

    def own_rows(j):
        start = pl.multiple_of((2 * j + ten) * RB, RB)
        rows = pl.ds(start, RB)
        gn2_copy(j).wait_recv()
        grad_normed = s.gn2_send[rows, :] + s.gn2_recv[j]
        unit, scale = norm_stats(s.middle[rows, :])
        s.n2[0:1, :] += col_sum(grad_normed * unit)
        s.n2[1:2, :] += col_sum(grad_normed)
        top = cotangent[rows, :].astype(F32) * valid_rows(start, RB)
        grad_middle = top + norm_back(grad_normed, unit, scale, gain2)
        s.grad_middle[j] = grad_middle
        grad_attended = grad_middle.astype(BF16)
        s.grad_ctx_send[j] = mm_nt(grad_attended, s.wo[far_half, :]).astype(BF16).astype(F32)
        grad_ctx_copy(j).start()
        s.aob[...] += col_sum(grad_attended.astype(F32))
        s.grad_att_t[j] = grad_attended.T
        grad_context = mm_nt(grad_attended, attn_out[...]).astype(BF16)
        for p in range(pairs):
            s.grad_ctx[j, p] = grad_context[:, p * 128 : (p + 1) * 128]

    def far_rows(j):
        grad_ctx_copy(j).wait_recv()
        for p in range(pairs):
            s.grad_ctx[2 + j, p] = s.grad_ctx_recv[j, :, p * 128 : (p + 1) * 128].astype(BF16)

    def out_grad(c, b):
        return mm(s.top_t[b], s.active[b * RF : (b + 1) * RF, c * CW : (c + 1) * CW])

    def keep_in(c):
        keep(grad_chunk(s.normed2_t, s.grad_pre.at[:, c * CW : (c + 1) * CW]), per + c)

    def keep_wo(h):
        total = None
        for j in range(2):
            rows = pl.ds(pl.multiple_of((2 * j + ten) * RB, RB), RB)
            context = jnp.concatenate([s.ctx[h * pairs + p, rows, :] for p in range(pairs)], axis=1)
            term = mm(s.grad_att_t[j], context)
            total = term if total is None else total + term
        keep(total, first_wo + h)

    for c in range(per):
        hold(out_grad(c, 0), c)
    feed(1)
    for c in range(per):
        keep(out_grad(c, 1), c, True)
        if c >= 2:
            core_done(c - 2)
    own_rows(0)
    for c in range(2):
        keep_in(c)
        core_done(2 + c)
    own_rows(1)
    for i in range(blocks):
        out_copy(i).start()
    for c in range(2, per):
        keep_in(c)
        core_done(2 + c)
    for h in range(2):
        keep_wo(h)
        core_done(per + 2 + h)

    s.grad_k[...] = jnp.zeros_like(s.grad_k)
    s.grad_v[...] = jnp.zeros_like(s.grad_v)
    s.grad_table[...] = jnp.zeros_like(s.grad_table)
    flip_row = lax.broadcasted_iota(jnp.int32, (2 * RB, 2 * RB), 0)
    flip_col = lax.broadcasted_iota(jnp.int32, (2 * RB, 2 * RB), 1)
    same_half = (flip_row < RB) == (flip_col < RB)
    local_row = lax.rem(flip_row, RB)
    local_col = lax.rem(flip_col, RB)
    flip = (same_half & (local_row + local_col == RB - 1)).astype(BF16)

    def attend_back(step, i):
        start = pl.multiple_of(i * RB, RB)
        rows = pl.ds(start, RB)

        def pair_step(p, carry):
            qs = stack(s.q[p, rows, :])
            gs = stack(s.grad_ctx[step, p])
            low = s.probs[p, i]
            s.grad_v[p] += mm_tn(low, gs)
            shares = low.astype(F32)
            grad_shares = mm_nt(gs, s.v[p])
            inner = jnp.sum(grad_shares * shares, axis=-1, keepdims=True)
            grad_scores = (shares * (grad_shares - inner)).astype(BF16)
            s.grad_k[p] += mm_tn(grad_scores, qs)
            grad_q = mm(grad_scores, s.k[p])
            flipped = mm(flip, grad_scores)
            wide = jnp.concatenate([flipped, jnp.zeros((2 * RB, RB), F32)], axis=1)
            spread = jnp.concatenate(
                [
                    pltpu.roll(wide[:RB], 0, 1, stride=1, stride_axis=0),
                    pltpu.roll(wide[RB:], 0, 1, stride=1, stride_axis=0),
                ],
                axis=0,
            ).astype(BF16)
            q_flipped = mm(flip, qs).astype(BF16)
            s.grad_table[table_rows_of(i), :] += mm_tn(spread, q_flipped)
            turned = mm(spread, s.table[table_rows_of(i), :])
            high = turned.astype(BF16)
            rest = (turned - high.astype(F32)).astype(BF16)
            grad_q = unstack(grad_q + (mm(flip, high) + mm(flip, rest))).astype(BF16)
            cols = pl.ds(pl.multiple_of(p * 128, 128), 128)
            s.grad_pre[rows, cols] = (grad_q.astype(F32) * head_scale).astype(BF16)
            return carry

        lax.fori_loop(0, pairs, pair_step, 0)

    attend_back(0, ten)
    core_done(first_wo, first_wo + 1)
    first_done(0, 1)
    attend_back(1, 2 + ten)
    first_done(2)
    far_rows(0)
    attend_back(2, 1 - ten)
    first_done(4, 3)
    second_done(0, 1, 2)
    far_rows(1)
    attend_back(3, 3 - ten)
    first_done(5)
    second_done(4, 3)
    third_done(0)

    for p in range(pairs):
        at = local + p * 128
        s.grad_pre[:, at : at + 128] = s.grad_k[p].astype(BF16)
        at += local
        s.grad_pre[:, at : at + 128] = s.grad_v[p].astype(BF16)
    for j in range(2):
        gn2_copy(j).wait_send()

    def back_copy(i):
        rows = pl.ds(pl.multiple_of(i * RB, RB), RB)
        return remote(s.gn2_send.at[rows], s.gn1_recv.at[rows], s.gn1_sem, i, y_peer)

    def project_back(b, carry):
        start = pl.multiple_of(b * RF, RF)
        rows = pl.ds(start, RF)
        total = (
            mm_nt(s.grad_pre[rows, 0:local], attn_in[0])
            + mm_nt(s.grad_pre[rows, local : 2 * local], attn_in[1])
            + mm_nt(s.grad_pre[rows, 2 * local : 3 * local], attn_in[2])
        )
        unit, scale = norm_stats(hidden[rows, :].astype(F32))
        s.gn2_send[rows, :] = norm_back(total, unit, scale, gain1)
        own = pl.ds(pl.multiple_of(start + ten * RB, RB), RB)
        s.gn2_send[own, :] += s.grad_middle[b]
        for j in range(RF // RB):
            back_copy(b * (RF // RB) + j).start()
        s.n1[0:1, :] += col_sum(total * unit)
        s.n1[1:2, :] += col_sum(total)
        return carry

    lax.fori_loop(0, slots // RF, project_back, 0)

    def put(at, row):
        for j in range(row.shape[1] // 128):
            g_vec_acc[at + j : at + j + 1, :] = row[:, j * 128 : (j + 1) * 128]

    put(V_N1G, s.n1[0:1, :])
    put(V_N1B, s.n1[1:2, :])
    put(V_N2G, s.n2[0:1, :])
    put(V_N2B, s.n2[1:2, :])
    put(V_AOB, s.aob[...])
    put(V_FOB, s.fob[...])
    put(V_FIB, s.fib[...])
    put(V_AIB, col_sum(s.grad_pre[:, 0:local].astype(F32)))
    put(V_AIB + pairs, col_sum(s.grad_pre[:, 2 * local : 3 * local].astype(F32)))
    grad_rel = None
    rest = s.grad_table[...]
    for part in range(3):
        piece16 = rest.astype(BF16)
        term = mm_tn(pick, piece16)
        grad_rel = term if part == 0 else grad_rel + term
        rest = rest - piece16.astype(F32)
    grad_rel = grad_rel + pltpu.roll(grad_rel, HD, 1)
    fold = lax.broadcasted_iota(jnp.int32, (reach, 128), 1) < HD
    g_vec_acc[V_REL : V_REL + reach, :] = jnp.where(fold, grad_rel[:reach], grad_rel[reach:])

    def vec_step(step, peer, count):
        rows = pl.ds(0, count)
        return remote(s.vec_send.at[step, rows], s.vec_recv.at[step, rows], s.vec_sem, step, peer)

    def share(step, peer, count):
        s.vec_send[step, 0:count] = g_vec_acc[0:count, :]
        vec_step(step, peer, count).start()

    def merge(step, peer, count):
        vec_step(step, peer, count).wait_recv()
        g_vec_acc[0:count, :] = s.vec_send[step, 0:count] + s.vec_recv[step, 0:count]

    if ring:
        share(1, core_peer, VROWS)

    for c in range(3):
        keep(grad_chunk(s.normed_t, s.grad_pre.at[:, c * local : (c + 1) * local]), first_in + c)

    def finish_out(i, carry):
        start = pl.multiple_of(i * RB, RB)
        rows = pl.ds(start, RB)
        out_copy(i).wait_recv()
        branch = s.out_send[rows, :] + s.out_recv[rows, :]
        total = s.middle[rows, :] + (branch + out_bias2)
        output[rows, :] = (total * valid_rows(start, RB)).astype(BF16)
        results(i, output.at[rows], far_output.at[rows]).start()
        return carry

    def finish_hidden(i, carry):
        rows = pl.ds(pl.multiple_of(i * RB, RB), RB)
        back_copy(i).wait_recv()
        grad_hidden[rows, :] = (s.gn2_send[rows, :] + s.gn1_recv[rows, :]).astype(BF16)
        results(blocks + i, grad_hidden.at[rows], far_grad_hidden.at[rows]).start()
        return carry

    vec_out = results(2 * blocks, g_vec_acc, far_vec)
    if ring:
        second_done(5)
        first_done(6)
        core_done(first_in, first_in + 1, first_in + 2)
        merge(1, core_peer, VROWS)
        share(2, z_low, VROWS)
        first_done(7)
        second_done(6)
        third_done(2, 3)
        merge(2, z_low, VROWS)
        share(3, z_high, VROWS)
        lax.fori_loop(0, blocks, finish_out, 0)
        first_done(8)
        second_done(7)
        third_done(5)
        merge(3, z_high, VROWS)
        share(4, x_peer, VROWS)
        first_done(9)
        second_done(8)
        third_done(6, 7)
        first_done(10)
        second_done(9)
        third_done(8, 1, 4)
        first_done(11)
        second_done(10)
        third_done(9)
        wo_grad_copy().start()
        first_done(12)
        second_done(11)
        third_done(10)
        merge(4, x_peer, VROWS)
        share(0, y_peer, YROWS)
        second_done(12)
        third_done(11)
        lax.fori_loop(0, blocks - 1, finish_hidden, 0)
        third_done(12)
        finish_hidden(blocks - 1, 0)
        wo_grad_done()
        merge(0, y_peer, YROWS)
        vec_out.start()
    else:
        share(0, y_peer, YROWS)
        lax.fori_loop(0, blocks, finish_out, 0)
        lax.fori_loop(0, blocks, finish_hidden, 0)
        merge(0, y_peer, YROWS)
        vec_out.start()

    wo_y().wait_send()
    if ring:
        wo_x().wait_send()
        wo_z().wait_send()
        wo_xz().wait_send()
        wo_core(True).wait_send()
        wo_core(False).wait_send()

    def sent(i, carry):
        for p in range(pairs):
            ctx_copy(i, p).wait_send()
        out_copy(i).wait_send()
        back_copy(i).wait_send()
        return carry

    lax.fori_loop(0, blocks, sent, 0)
    vec_step(0, y_peer, YROWS).wait_send()
    if ring:
        for step, peer in enumerate((core_peer, z_low, z_high, x_peer)):
            vec_step(step + 1, peer, VROWS).wait_send()
        for c in range(chunks):
            if c >= chunks - SLOTS:
                core_copy(c).wait_send()
            first_copy(c).wait_send()
            second_copy(c).wait_send()
            third_copy(c).wait_send()
            if not first_wo <= c < first_in:
                grad_result(c).wait()
        wo_grad_copy().wait_send()
        wo_grad_result().wait()
    for j in range(2):
        grad_ctx_copy(j).wait_send()
    for i in range(blocks):
        rows = slice(i * RB, (i + 1) * RB)
        results(i, output.at[rows], far_output.at[rows]).wait()
        results(blocks + i, grad_hidden.at[rows], far_grad_hidden.at[rows]).wait()
    vec_out.wait()


def scratch_of(ring, slots, width, local, units, chunks):
    pairs = local // 128
    blocks = slots // RB
    halves = slots // RF
    vm, dma = pltpu.VMEM, pltpu.SemaphoreType.DMA
    shapes = dict(
        hidden=vm((slots, width), BF16),
        attn_in=vm((3, width, local), BF16),
        attn_out=vm((local, width), BF16),
        ffn_in=vm((width, units), BF16),
        ffn_out=vm((units, width), BF16),
        cotangent=vm((slots, width), BF16),
        output=vm((slots, width), BF16),
        grad_hidden=vm((slots, width), BF16),
        in_s=dma((6,)),
        out_dma=dma((2 * blocks + 1 + chunks,)),
        normed_t=vm((halves, width, RF), BF16),
        q=vm((pairs, slots, 128), BF16),
        k=vm((pairs, slots, 128), BF16),
        v=vm((pairs, slots, 128), BF16),
        table=vm((2 * slots, 128), BF16),
        probs=vm((pairs, blocks, 2 * RB, slots), BF16),
        ctx=vm((2 * pairs, slots, 128), BF16),
        ctx_send=vm((pairs, slots, 128), F32),
        ctx_recv=vm((pairs, slots, 128), F32),
        wo=vm((2 * local, width), BF16),
        wo_stage=vm((local // 8, width) if ring else (local, width), F32),
        wo_recv=vm((2, 2, 2, local // 8, width) if ring else (local, width), F32),
        middle=vm((slots, width), F32),
        normed2_t=vm((halves, width, RF), BF16),
        top_t=vm((halves, width, RF), BF16),
        active=vm((slots, units), BF16),
        grad_pre=vm((slots, units), BF16),
        gn2_send=vm((slots, width), F32),
        gn2_recv=vm((blocks // 2, RB, width), F32),
        gn1_recv=vm((slots, width), F32),
        out_send=vm((slots, width), F32),
        out_recv=vm((slots, width), F32),
        grad_middle=vm((blocks // 2, RB, width), F32),
        grad_att_t=vm((blocks // 2, width, RB), BF16),
        grad_ctx_send=vm((blocks // 2, RB, local), F32),
        grad_ctx_recv=vm((blocks // 2, RB, local), F32),
        grad_ctx=vm((blocks, pairs, RB, 128), BF16),
        grad_k=vm((pairs, slots, 128), F32),
        grad_v=vm((pairs, slots, 128), F32),
        grad_table=vm((2 * slots, 128), F32),
        vec=vm((VROWS, 128), F32),
        vec_send=vm((5 if ring else 1, VROWS, 128), F32),
        vec_recv=vm((5 if ring else 1, VROWS, 128), F32),
        fib=vm((1, units), F32),
        fob=vm((1, width), F32),
        aob=vm((1, width), F32),
        n1=vm((2, width), F32),
        n2=vm((2, width), F32),
        ffn_in_bias=vm((1, units), F32),
        free=pltpu.SemaphoreType.REGULAR((SLOTS,)),
        wo_sem=dma((2, 8)),
        ctx_sem=dma((2, blocks * pairs)),
        gn2_sem=dma((2, blocks // 2)),
        grad_ctx_sem=dma((2, blocks // 2)),
        gn1_sem=dma((2, blocks)),
        out_sem=dma((2, blocks)),
        vec_sem=dma((2, 5)),
    )
    if ring:
        shapes.update(
            g_own=vm((chunks, 2, 2, 2, 48, CW), F32),
            g_send=vm((SLOTS, 2, 2, 2, 48, CW), F32),
            core_recv=vm((SLOTS, 2, 2, 2, 48, CW), F32),
            first_recv=vm((chunks, 2, 2, 48, CW), F32),
            late_recv=vm((chunks, 3, 48, CW), F32),
            grads=vm((chunks, 48, CW), F32),
            wo_grad=vm((48, CW), F32),
            wo_grad_recv=vm((48, CW), F32),
            gc_sem=dma((2, chunks)),
            g1_sem=dma((2, chunks)),
            g2_sem=dma((2, chunks)),
            g3_sem=dma((2, chunks)),
            wo_grad_sem=dma((2, 1)),
        )
    return shapes


def place(
    output_in, grad_hidden_in, attn_in_in, attn_out_in, ffn_in_in, ffn_out_in, vec,
    output, grad_hidden, g_attn_in, g_attn_out_t, g_ffn_in, g_ffn_out_t,
    g_attn_in_bias, g_rel_t, g_attn_out_bias, g_norm1_gain, g_norm1_bias, g_norm2_gain, g_norm2_bias,
    g_ffn_in_bias, g_ffn_out_bias,
):
    for ref, source in (
        (output, output_in), (grad_hidden, grad_hidden_in), (g_attn_in, attn_in_in), (g_attn_out_t, attn_out_in),
        (g_ffn_in, ffn_in_in), (g_ffn_out_t, ffn_out_in),
    ):
        ref[...] = source[...]
    for ref, at in (
        (g_attn_out_bias, V_AOB), (g_norm1_gain, V_N1G), (g_norm1_bias, V_N1B), (g_norm2_gain, V_N2G),
        (g_norm2_bias, V_N2B), (g_ffn_in_bias, V_FIB), (g_ffn_out_bias, V_FOB),
    ):
        ref[...] = vec[at : at + ref.shape[0], :]
    local = g_attn_in_bias.shape[1]
    for k in range(2):
        at = V_AIB + k * (local // 128)
        g_attn_in_bias[k : k + 1, :] = jnp.concatenate(
            [vec[at + j : at + j + 1, :] for j in range(local // 128)], axis=1
        )
    reach = g_rel_t.shape[1] // 2
    turned = vec[V_REL : V_REL + reach, :].T
    g_rel_t[...] = jnp.concatenate([turned[:HD], turned[HD:]], axis=1)


def on_device(
    ring,
    hidden, lengths, attn_in, attn_in_bias, rel_table, attn_out, attn_out_bias,
    norm1_gain, norm1_bias, norm2_gain, norm2_bias,
    ffn_in, ffn_in_bias, ffn_out, ffn_out_bias, cotangent,
):
    slots, width = hidden.shape
    local = attn_out.shape[0]
    units = ffn_in.shape[1]
    table_rows = rel_table.shape[0]
    chunks = 2 * units // CW + 5
    rows = width // 16
    shape = jax.ShapeDtypeStruct
    shapes = scratch_of(ring, slots, width, local, units, chunks)
    names = tuple(shapes)
    outs = [
        shape((slots, width), BF16), shape((slots, width), BF16), shape((3, rows, local), F32), shape((rows, local), F32),
        shape((rows, units), F32), shape((rows, units), F32), shape((VROWS, 128), F32),
    ]
    far = pl.BlockSpec(memory_space=pl.ANY)
    near = pl.BlockSpec(memory_space=pltpu.VMEM)
    out_specs = [far] * 7
    if not ring:
        names = (FULL,) + names
        outs.append(shape((chunks, width, CW), F32))
        out_specs.append(near)

    def lanes(vector):
        return vector.reshape(vector.shape[0] // 128, 128)

    def unlanes(array):
        return array.reshape(array.shape[0] * 128)

    results = pl.pallas_call(
        partial(body, ring, names),
        out_shape=outs,
        in_specs=[pl.BlockSpec(memory_space=pltpu.SMEM)] + [near] * 9 + [far] * 6,
        out_specs=out_specs,
        scratch_shapes=list(shapes.values()),
        compiler_params=pltpu.CompilerParams(
            collective_id=0, has_side_effects=True, vmem_limit_bytes=64 * 1024 * 1024
        ),
    )(
        lengths, attn_in_bias, rel_table.T, lanes(attn_out_bias), lanes(norm1_gain), lanes(norm1_bias),
        lanes(norm2_gain), lanes(norm2_bias), lanes(ffn_in_bias), lanes(ffn_out_bias),
        hidden, attn_in, attn_out, ffn_in, ffn_out, cotangent,
    )
    if ring:
        vector = shape((width // 128, 128), F32)
        placed = pl.pallas_call(
            place,
            out_shape=outs[:6] + [
                shape((2, local), F32), shape((HD, table_rows), F32), vector, vector, vector, vector, vector,
                shape((units // 128, 128), F32), vector,
            ],
            in_specs=[near] * 7,
            out_specs=[near] * 15,
        )(*results)
        (
            output, grad_hidden, g_attn_in, g_attn_out_t, g_ffn_in, g_ffn_out_t, g_attn_in_bias, g_rel_t,
            g_attn_out_bias, n1g, n1b, n2g, n2b, g_ffn_in_bias, g_ffn_out_bias,
        ) = placed
        return (
            output, grad_hidden, g_attn_in, g_attn_in_bias, g_rel_t.T, g_attn_out_t.T, unlanes(g_attn_out_bias),
            unlanes(n1g), unlanes(n1b), unlanes(n2g), unlanes(n2b),
            g_ffn_in, unlanes(g_ffn_in_bias), g_ffn_out_t.T, unlanes(g_ffn_out_bias),
        )
    output, grad_hidden, vec, full = results[0], results[1], results[6], results[7]
    per = units // CW
    wide = jnp.swapaxes(full[: 2 * per].reshape(2, per, width, CW), 1, 2).reshape(2, width, units)

    def scatter(value, dim, axis="dp"):
        return lax.psum_scatter(value, axis, scatter_dimension=dim, tiled=True)

    g_ffn_out = scatter(wide[0].T, 1)
    g_ffn_in = scatter(wide[1], 0)
    g_attn_out = scatter(scatter(full[2 * per : 2 * per + 2], 0, "tensor")[0].T, 1)
    g_attn_in = scatter(full[2 * per + 2 : 2 * per + 5], 1)
    vec = lax.psum(vec, "dp")

    def row(at, count=width):
        return unlanes(vec[at : at + count // 128])

    rel_pairs = vec[V_REL : V_REL + table_rows // 2]
    grad_rel = jnp.concatenate([rel_pairs[:, :HD], rel_pairs[:, HD:]], axis=0)
    return (
        output, grad_hidden, g_attn_in,
        row(V_AIB, 2 * local).reshape(2, local), grad_rel, g_attn_out, row(V_AOB),
        row(V_N1G), row(V_N1B), row(V_N2G), row(V_N2B),
        g_ffn_in, row(V_FIB, units), g_ffn_out, row(V_FOB),
    )


def solution(mesh):
    ring = mesh.shape["dp"] == 16
    return jax.shard_map(
        partial(on_device, ring),
        mesh=mesh,
        in_specs=(
            P("dp", None), P("dp"), P(None, None, "tensor"), P(None, "tensor"), P(),
            P("tensor", None), P(), P(), P(), P(), P(),
            P(None, "tensor"), P("tensor"), P("tensor", None), P(), P("dp", None),
        ),
        out_specs=(
            P("dp", None), P("dp", None), P(None, "dp", "tensor"), P(None, "tensor"), P(),
            P("tensor", "dp"), P(), P(), P(), P(), P(),
            P("dp", "tensor"), P("tensor"), P("tensor", "dp"), P(),
        ),
        check_vma=False,
    )
```

```python
from functools import partial
from types import SimpleNamespace

import jax
import jax.numpy as jnp
from jax import lax
from jax.experimental import pallas as pl
from jax.experimental.pallas import tpu as pltpu
from jax.sharding import PartitionSpec as P

HD = 64
EPSILON = 1e-05
NEGATIVE = -1e30
SQRT_HALF = 0.7071067811865476
INV_SQRT_2PI = 0.3989422804014327
RB = 128
RF = 256
CW = 384
FULL = "g_full"
OUT_AT, IN_AT, WO_AT, QKV_AT = (0, 1, 2, 3), (4, 5, 8, 9), (6, 7), (10, 11, 12)
Z_FIRST = (1, 4)
SLOTS = 4
MESH = pl.DeviceIdType.MESH
F32 = jnp.float32
BF16 = jnp.bfloat16


def mm(a, b):
    return jnp.dot(a, b, preferred_element_type=F32)


def mm_nt(a, b):
    return lax.dot_general(a, b, (((1,), (1,)), ((), ())), preferred_element_type=F32)


def mm_tn(a, b):
    return lax.dot_general(a, b, (((0,), (0,)), ((), ())), preferred_element_type=F32)


def norm_stats(value):
    mean = jnp.mean(value, axis=-1, keepdims=True)
    centred = value - mean
    scale = lax.rsqrt(jnp.mean(centred * centred, axis=-1, keepdims=True) + EPSILON)
    return centred * scale, scale


def norm_back(grad, unit, scale, gain):
    grad_unit = grad * gain
    inner = (
        grad_unit
        - jnp.mean(grad_unit, axis=-1, keepdims=True)
        - unit * jnp.mean(grad_unit * unit, axis=-1, keepdims=True)
    )
    return inner * scale


def col_sum(value):
    return jnp.sum(value, axis=0, keepdims=True)


def lanes_of(ref3, rows):
    return jnp.concatenate([ref3[p, rows, :] for p in range(ref3.shape[0])], axis=1)


V_N1G, V_N1B, V_AOB, V_N2G, V_N2B, V_REL, V_FOB, V_FIB, V_AIB = 0, 6, 12, 18, 24, 32, 192, 198, 210
YROWS, VROWS = 192, 216


def vec_place(row):
    part, at = (row // 24, row % 24) if row < YROWS else ((row - YROWS) // 3, 24 + (row - YROWS) % 3)
    return part // 4, part // 2 % 2, part % 2, at


def vec_rows(vec, first, count):
    found = []
    for row in range(first, first + count):
        a, b, c, at = vec_place(row)
        found.append(vec[a, b, c, at : at + 1, :])
    return found


def body(
    ring, names,
    lengths, far_attn_in_bias, far_rel_table_t, far_attn_out_bias, far_norm1_gain, far_norm1_bias, far_norm2_gain,
    far_norm2_bias, far_ffn_in_bias, far_ffn_out_bias, far_hidden, far_attn_in, far_attn_out, far_ffn_in, far_ffn_out, far_cotangent,
    far_output, far_grad_hidden, far_attn_in_grad, far_attn_out_grad, far_ffn_in_grad, far_ffn_out_grad, far_vec,
    *scratch,
):
    s = SimpleNamespace(**dict(zip(names, scratch)))

    def bring(at, near, far):
        copy = pltpu.make_async_copy(far, near, s.in_s.at[at])
        copy.start()
        return copy

    bring_attn_out = bring(0, s.attn_out, far_attn_out)
    bring_hidden = bring(1, s.hidden, far_hidden)
    bring_attn_in = bring(2, s.attn_in, far_attn_in)
    small = (
        (s.attn_in_bias, far_attn_in_bias), (s.rel_table_t, far_rel_table_t), (s.attn_out_bias, far_attn_out_bias),
        (s.norm1_gain, far_norm1_gain), (s.norm1_bias, far_norm1_bias), (s.norm2_gain, far_norm2_gain),
        (s.norm2_bias, far_norm2_bias), (s.ffn_in_bias16, far_ffn_in_bias), (s.ffn_out_bias, far_ffn_out_bias),
    )
    bring_small = [bring(6 + k, near, far) for k, (near, far) in enumerate(small)]
    hidden, attn_in, attn_out = s.hidden, s.attn_in, s.attn_out
    cotangent, ffn_in, ffn_out = s.cotangent, s.ffn_in, s.ffn_out
    output, grad_hidden = s.output, s.grad_hidden
    slots, width = hidden.shape
    local = attn_out.shape[0]
    pairs = local // 128
    units = ffn_in.shape[1]
    table_rows = s.rel_table_t.shape[1]
    reach = table_rows // 2
    blocks = slots // RB
    ext = slots + RB
    head_scale = HD ** (-0.5)

    dp = lax.axis_index("dp")
    ten = lax.axis_index("tensor")
    y_peer = (dp, 1 - ten)
    if ring:
        core = lax.rem(dp, 2)
        x_at = lax.rem(lax.div(dp, 2), 2)
        z_low_at = lax.rem(lax.div(dp, 4), 2)
        z_high_at = lax.div(dp, 8)
        core_peer = (dp + 1 - 2 * core, ten)
        x_peer = (dp + 2 - 4 * x_at, ten)
        z_low = (dp + 4 - 8 * z_low_at, ten)
        z_high = (dp + 8 - 16 * z_high_at, ten)
        greet = [y_peer, core_peer, x_peer, z_low, z_high]
    else:
        greet = [y_peer]

    barrier = pltpu.get_barrier_semaphore()
    for peer in greet:
        pl.semaphore_signal(barrier, inc=1, device_id=peer, device_id_type=MESH)

    def remote(src, dst, sems, at, peer):
        return pltpu.make_async_remote_copy(
            src_ref=src, dst_ref=dst, send_sem=sems.at[0, at], recv_sem=sems.at[1, at],
            device_id=peer, device_id_type=MESH,
        )

    bring_attn_out.wait()
    if ring:
        piece = local // 8
        mine = (2 * z_low_at + x_at) * 2 + core
        s.wo_stage[...] = attn_out[pl.ds(pl.multiple_of(mine * piece, 16), piece), :].astype(F32)

        def wo_y():
            return remote(s.wo_stage, s.wo_recv.at[z_low_at, x_at, core], s.wo_sem, 0, y_peer)

        def wo_pass(part, at, peer):
            return remote(part, part, s.wo_sem, at, peer)

        def wo_x():
            return wo_pass(s.wo_recv.at[z_low_at, x_at, core], 1, x_peer)

        def wo_z():
            return wo_pass(s.wo_recv.at[z_low_at, x_at, core], 2, z_low)

        def wo_xz():
            return wo_pass(s.wo_recv.at[z_low_at, 1 - x_at, core], 3, z_low)

        def wo_core(near):
            return wo_pass(s.wo_recv.at[z_low_at if near else 1 - z_low_at, :, core], 4 if near else 5, core_peer)
    else:
        s.wo_stage[...] = attn_out[...].astype(F32)

        def wo_y():
            return remote(s.wo_stage, s.wo_recv, s.wo_sem, 0, y_peer)

    pl.semaphore_wait(barrier, len(greet))
    wo_y().start()

    def flat(ref):
        value = ref[...].astype(F32)
        return jnp.concatenate([value[j : j + 1] for j in range(value.shape[0])], axis=1)

    for copy in bring_small:
        copy.wait()
    bias_q = s.attn_in_bias[0:1, :].astype(F32)
    bias_v = s.attn_in_bias[1:2, :].astype(F32)
    gain1, offset1 = flat(s.norm1_gain), flat(s.norm1_bias)
    gain2, offset2 = flat(s.norm2_gain), flat(s.norm2_bias)
    out_bias1, out_bias2 = flat(s.attn_out_bias), flat(s.ffn_out_bias)
    s.ffn_in_bias[...] = flat(s.ffn_in_bias16)
    seq_len = lengths[0]

    ext_rows = 2 * slots
    distance = slots - 1 - lax.broadcasted_iota(jnp.int32, (ext_rows, table_rows), 0)
    bucket = jnp.clip(distance, -reach, reach - 1) + reach
    pick = (bucket == lax.broadcasted_iota(jnp.int32, (ext_rows, table_rows), 1)).astype(BF16)
    rel_t = s.rel_table_t[...]
    s.table[...] = mm_nt(pick, jnp.concatenate([rel_t, rel_t], axis=0)).astype(BF16)

    def project(i, carry):
        rows = pl.ds(pl.multiple_of(i * RF, RF), RF)
        unit, unused = norm_stats(hidden[rows, :].astype(F32))
        normed = (unit * gain1 + offset1).astype(BF16)
        s.normed_t[i] = normed.T
        q = ((mm(normed, attn_in[0]) + bias_q) * head_scale).astype(BF16)
        k = mm(normed, attn_in[1]).astype(BF16)
        v = (mm(normed, attn_in[2]) + bias_v).astype(BF16)
        for p in range(pairs):
            s.q[p, rows, :] = q[:, p * 128 : (p + 1) * 128]
            s.k[p, rows, :] = k[:, p * 128 : (p + 1) * 128]
            s.v[p, rows, :] = v[:, p * 128 : (p + 1) * 128]
        return carry

    bring_hidden.wait()
    bring_attn_in.wait()
    bring_cotangent = bring(3, s.cotangent, far_cotangent)
    bring_ffn_in = bring(4, s.ffn_in, far_ffn_in)
    bring_ffn_out = bring(5, s.ffn_out, far_ffn_out)
    lax.fori_loop(0, slots // RF, project, 0)

    low_lanes = lax.broadcasted_iota(jnp.int32, (RB, 128), 1) < HD
    key_ok = lax.broadcasted_iota(jnp.int32, (1, slots), 1) < seq_len

    def stack(both):
        zero = jnp.zeros_like(both)
        return jnp.concatenate([jnp.where(low_lanes, both, zero), jnp.where(low_lanes, zero, both)], axis=0)

    def unstack(tall):
        return jnp.where(low_lanes, tall[:RB], tall[RB:])

    def table_rows_of(i):
        return pl.ds(pl.multiple_of(slots - RB - i * RB, RB), ext)

    def ctx_copy(i, p):
        rows = pl.ds(pl.multiple_of(i * RB, RB), RB)
        return remote(s.ctx_send.at[p, rows], s.ctx_recv.at[p, rows], s.ctx_sem, i * pairs + p, y_peer)

    def attend(i):
        rows = pl.ds(pl.multiple_of(i * RB, RB), RB)

        def pair_step(p, carry):
            qs = stack(s.q[p, rows, :])
            spread = mm_nt(qs, s.table[table_rows_of(i), :])
            shift = ext - RB + 1
            bias = jnp.concatenate(
                [
                    pltpu.roll(spread[:RB], shift, 1, stride=1, stride_axis=0)[:, :slots],
                    pltpu.roll(spread[RB:], shift, 1, stride=1, stride_axis=0)[:, :slots],
                ],
                axis=0,
            )
            scores = jnp.where(key_ok, mm_nt(qs, s.k[p]) + bias, NEGATIVE)
            expon = jnp.exp(scores - jnp.max(scores, axis=-1, keepdims=True))
            shares = (expon * (1.0 / jnp.sum(expon, axis=-1, keepdims=True))).astype(BF16)
            s.probs[p, i] = shares
            context = unstack(mm(shares, s.v[p])).astype(BF16)
            s.ctx[ten * pairs + p, rows, :] = context
            s.ctx_send[p, rows, :] = context.astype(F32)
            ctx_copy(i, p).start()
            return carry

        lax.fori_loop(0, pairs, pair_step, 0)

    half = pl.ds(pl.multiple_of(ten * local, 128), local)
    far_half = pl.ds(pl.multiple_of((1 - ten) * local, 128), local)
    s.wo[half, :] = attn_out[...]
    attend(0)
    if ring:
        wo_y().wait_recv()
        wo_x().start()
        wo_z().start()
    attend(1)
    if ring:
        wo_x().wait_recv()
        wo_xz().start()
        wo_core(True).start()
    attend(2)
    attend(3)

    if ring:
        wo_z().wait_recv()
        wo_xz().wait_recv()
        wo_core(False).start()
        wo_core(True).wait_recv()
        wo_core(False).wait_recv()
        s.wo[far_half, :] = s.wo_recv[...].reshape(local, width).astype(BF16)
    else:
        wo_y().wait_recv()
        s.wo[far_half, :] = s.wo_recv[...].astype(BF16)
    bring_cotangent.wait()
    bring_ffn_in.wait()
    bring_ffn_out.wait()

    def valid_rows(start, count):
        return (lax.broadcasted_iota(jnp.int32, (count, 1), 0) + start < seq_len).astype(F32)

    def gn2_copy(j):
        rows = pl.ds(pl.multiple_of((2 * j + 1 - ten) * RB, RB), RB)
        return remote(s.gn2_send.at[rows], s.gn2_recv.at[j], s.gn2_sem, j, y_peer)

    def grad_ctx_copy(j):
        return remote(s.grad_ctx_send.at[j], s.grad_ctx_recv.at[j], s.grad_ctx_sem, j, y_peer)

    def out_copy(i):
        rows = pl.ds(pl.multiple_of(i * RB, RB), RB)
        return remote(s.out_send.at[rows], s.out_recv.at[rows], s.out_sem, i, y_peer)

    s.vec[...] = jnp.zeros_like(s.vec)
    s.fib[...] = jnp.zeros_like(s.fib)
    s.fob[...] = jnp.zeros_like(s.fob)
    s.aob[...] = jnp.zeros_like(s.aob)
    s.n1[...] = jnp.zeros_like(s.n1)
    s.n2[...] = jnp.zeros_like(s.n2)

    step_units = 512

    def feed(b):
        start = b * RF
        rows = slice(start, start + RF)
        for j in range(RF // RB):
            for p in range(pairs):
                ctx_copy(b * (RF // RB) + j, p).wait_recv()
        for p in range(pairs):
            s.ctx[(1 - ten) * pairs + p, rows, :] = s.ctx_recv[p, rows, :].astype(BF16)
        attended = mm(lanes_of(s.ctx, rows), s.wo[...]) + out_bias1
        middle = hidden[rows, :].astype(F32) + attended
        s.middle[rows, :] = middle
        unit, unused = norm_stats(middle)
        normed = (unit * gain2 + offset2).astype(BF16)
        s.normed2_t[b] = normed.T
        top = cotangent[rows, :].astype(F32) * valid_rows(start, RF)
        s.fob[...] += col_sum(top)
        top = top.astype(BF16)
        s.top_t[b] = top.T
        for c in range(units // step_units):
            cols = slice(c * step_units, (c + 1) * step_units)
            pre = mm(normed, ffn_in[:, cols]) + s.ffn_in_bias[:, cols]
            share = 0.5 + 0.5 * lax.erf(pre * SQRT_HALF)
            active = (pre * share).astype(BF16)
            s.active[rows, cols] = active
            slope = share + pre * (jnp.exp(-0.5 * pre * pre) * INV_SQRT_2PI)
            grad_pre = (mm_nt(top, ffn_out[cols, :]) * slope).astype(BF16)
            s.grad_pre[rows, cols] = grad_pre
            s.fib[:, cols] += col_sum(grad_pre.astype(F32))
            back = mm_nt(grad_pre, ffn_in[:, cols])
            onward = mm(active, ffn_out[cols, :])
            if c == 0:
                s.gn2_send[rows, :] = back
                s.out_send[rows, :] = onward
            else:
                s.gn2_send[rows, :] += back
                s.out_send[rows, :] += onward
        gn2_copy(b).start()

    feed(0)

    def grad_chunk(left_t, right):
        total = mm(left_t[0], right[0:RF])
        for b in range(1, slots // RF):
            total += mm(left_t[b], right[b * RF : (b + 1) * RF])
        return total

    per = units // CW
    chunks = 2 * per + 5

    def hold(total, chunk, begun=False):
        if not ring:
            s.g_full[chunk] = s.g_full[chunk] + total if begun else total
            return
        slot = chunk % SLOTS
        parts = total.reshape(8, 2, 48, CW)
        even, odd = parts[:, 0], parts[:, 1]
        near = jnp.where(core == 0, even, odd).reshape(2, 2, 2, 48, CW)
        far = jnp.where(core == 0, odd, even).reshape(2, 2, 2, 48, CW)
        s.g_own[chunk] = s.g_own[chunk] + near if begun else near
        s.g_send[slot] = s.g_send[slot] + far if begun else far

    def keep(total, chunk, begun=False):
        if ring and chunk >= SLOTS:
            core_copy(chunk - SLOTS).wait_send()
            pl.semaphore_wait(s.free.at[chunk % SLOTS], 1)
        hold(total, chunk, begun)
        if ring:
            core_copy(chunk).start()

    def core_copy(chunk):
        slot = chunk % SLOTS
        return remote(s.g_send.at[slot], s.core_recv.at[slot], s.gc_sem, chunk, core_peer)

    def first_copy(chunk):
        own = s.g_own.at[chunk]
        if chunk in Z_FIRST:
            return remote(own.at[:, 1 - z_low_at], s.first_recv.at[chunk], s.g1_sem, chunk, z_low)
        return remote(own.at[:, :, 1 - x_at], s.first_recv.at[chunk], s.g1_sem, chunk, x_peer)

    def second_copy(chunk):
        own = s.g_own.at[chunk]
        into = s.late_recv.at[chunk, 0:2]
        if chunk in Z_FIRST:
            return remote(own.at[1 - z_high_at, z_low_at], into, s.g2_sem, chunk, z_high)
        return remote(own.at[:, 1 - z_low_at, x_at], into, s.g2_sem, chunk, z_low)

    def third_copy(chunk):
        own = s.g_own.at[chunk]
        into = s.late_recv.at[chunk, 2]
        if chunk in Z_FIRST:
            return remote(own.at[z_high_at, z_low_at, 1 - x_at], into, s.g3_sem, chunk, x_peer)
        return remote(own.at[1 - z_high_at, z_low_at, x_at], into, s.g3_sem, chunk, z_high)

    def core_done(*which):
        for chunk in which if ring else ():
            core_copy(chunk).wait_recv()
            s.g_own[chunk] = s.g_own[chunk] + s.core_recv[chunk % SLOTS]
            if chunk + SLOTS < chunks:
                pl.semaphore_signal(s.free.at[chunk % SLOTS], inc=1, device_id=core_peer, device_id_type=MESH)
            first_copy(chunk).start()

    def first_done(*which):
        for chunk in which if ring else ():
            first_copy(chunk).wait_recv()
            if chunk in Z_FIRST:
                s.g_own[chunk, :, z_low_at] = s.g_own[chunk, :, z_low_at] + s.first_recv[chunk]
            else:
                s.g_own[chunk, :, :, x_at] = s.g_own[chunk, :, :, x_at] + s.first_recv[chunk]
            second_copy(chunk).start()

    def second_done(*which):
        for chunk in which if ring else ():
            second_copy(chunk).wait_recv()
            if chunk in Z_FIRST:
                s.g_own[chunk, z_high_at, z_low_at] = s.g_own[chunk, z_high_at, z_low_at] + s.late_recv[chunk, 0:2]
            else:
                s.g_own[chunk, :, z_low_at, x_at] = s.g_own[chunk, :, z_low_at, x_at] + s.late_recv[chunk, 0:2]
            third_copy(chunk).start()

    def results(at, near, far):
        return pltpu.make_async_copy(near, far, s.out_dma.at[at])

    def grad_result(chunk):
        if chunk in OUT_AT:
            c = OUT_AT.index(chunk)
            far = far_ffn_out_grad.at[:, c * CW : (c + 1) * CW]
        elif chunk in IN_AT:
            c = IN_AT.index(chunk)
            far = far_ffn_in_grad.at[:, c * CW : (c + 1) * CW]
        else:
            far = far_attn_in_grad.at[QKV_AT.index(chunk)]
        return results(2 * blocks + 1 + chunk, s.grads.at[chunk], far)

    def third_done(*which):
        for chunk in which if ring else ():
            third_copy(chunk).wait_recv()
            s.grads[chunk] = s.g_own[chunk, z_high_at, z_low_at, x_at] + s.late_recv[chunk, 2]
            if chunk not in WO_AT:
                grad_result(chunk).start()

    def wo_grad_copy():
        return remote(s.grads.at[WO_AT[0] + 1 - ten], s.wo_grad_recv, s.wo_grad_sem, 0, y_peer)

    def wo_grad_done():
        wo_grad_copy().wait_recv()
        s.wo_grad[...] = s.grads[WO_AT[0] + ten] + s.wo_grad_recv[...]
        wo_grad_result().start()

    def wo_grad_result():
        return results(2 * blocks + 1 + WO_AT[0], s.wo_grad, far_attn_out_grad)

    def own_rows(j):
        start = pl.multiple_of((2 * j + ten) * RB, RB)
        rows = pl.ds(start, RB)
        gn2_copy(j).wait_recv()
        grad_normed = s.gn2_send[rows, :] + s.gn2_recv[j]
        unit, scale = norm_stats(s.middle[rows, :])
        s.n2[0:1, :] += col_sum(grad_normed * unit)
        s.n2[1:2, :] += col_sum(grad_normed)
        top = cotangent[rows, :].astype(F32) * valid_rows(start, RB)
        grad_middle = top + norm_back(grad_normed, unit, scale, gain2)
        s.grad_middle[j] = grad_middle
        grad_attended = grad_middle.astype(BF16)
        s.grad_ctx_send[j] = mm_nt(grad_attended, s.wo[far_half, :]).astype(BF16).astype(F32)
        grad_ctx_copy(j).start()
        s.aob[...] += col_sum(grad_attended.astype(F32))
        s.grad_att_t[j] = grad_attended.T
        grad_context = mm_nt(grad_attended, attn_out[...]).astype(BF16)
        for p in range(pairs):
            s.grad_ctx[j, p] = grad_context[:, p * 128 : (p + 1) * 128]

    def far_rows(j):
        grad_ctx_copy(j).wait_recv()
        for p in range(pairs):
            s.grad_ctx[2 + j, p] = s.grad_ctx_recv[j, :, p * 128 : (p + 1) * 128].astype(BF16)

    def out_grad(c, b):
        return mm(s.top_t[b], s.active[b * RF : (b + 1) * RF, c * CW : (c + 1) * CW])

    def keep_in(c):
        keep(grad_chunk(s.normed2_t, s.grad_pre.at[:, c * CW : (c + 1) * CW]), IN_AT[c])

    def keep_wo(h):
        total = None
        for j in range(2):
            rows = pl.ds(pl.multiple_of((2 * j + ten) * RB, RB), RB)
            context = jnp.concatenate([s.ctx[h * pairs + p, rows, :] for p in range(pairs)], axis=1)
            term = mm(s.grad_att_t[j], context)
            total = term if total is None else total + term
        keep(total, WO_AT[h])

    for c in range(per):
        hold(out_grad(c, 0), c)
    feed(1)
    for c in range(per):
        keep(out_grad(c, 1), c, True)
        if c >= 2:
            core_done(c - 2)
    own_rows(0)
    for c in range(2):
        keep_in(c)
        core_done(2 + c)
    own_rows(1)
    for i in range(blocks):
        out_copy(i).start()
    for h in range(2):
        keep_wo(h)
        core_done(4 + h)
    for c in range(2):
        keep_in(2 + c)
        core_done(6 + c)

    s.grad_k[...] = jnp.zeros_like(s.grad_k)
    s.grad_v[...] = jnp.zeros_like(s.grad_v)
    s.grad_table[...] = jnp.zeros_like(s.grad_table)
    flip_row = lax.broadcasted_iota(jnp.int32, (2 * RB, 2 * RB), 0)
    flip_col = lax.broadcasted_iota(jnp.int32, (2 * RB, 2 * RB), 1)
    same_half = (flip_row < RB) == (flip_col < RB)
    local_row = lax.rem(flip_row, RB)
    local_col = lax.rem(flip_col, RB)
    flip = (same_half & (local_row + local_col == RB - 1)).astype(BF16)

    def attend_back(step, i):
        start = pl.multiple_of(i * RB, RB)
        rows = pl.ds(start, RB)

        def pair_step(p, carry):
            qs = stack(s.q[p, rows, :])
            gs = stack(s.grad_ctx[step, p])
            low = s.probs[p, i]
            s.grad_v[p] += mm_tn(low, gs)
            shares = low.astype(F32)
            grad_shares = mm_nt(gs, s.v[p])
            inner = jnp.sum(grad_shares * shares, axis=-1, keepdims=True)
            grad_scores = (shares * (grad_shares - inner)).astype(BF16)
            s.grad_k[p] += mm_tn(grad_scores, qs)
            grad_q = mm(grad_scores, s.k[p])
            flipped = mm(flip, grad_scores)
            wide = jnp.concatenate([flipped, jnp.zeros((2 * RB, RB), F32)], axis=1)
            spread = jnp.concatenate(
                [
                    pltpu.roll(wide[:RB], 0, 1, stride=1, stride_axis=0),
                    pltpu.roll(wide[RB:], 0, 1, stride=1, stride_axis=0),
                ],
                axis=0,
            ).astype(BF16)
            q_flipped = mm(flip, qs).astype(BF16)
            s.grad_table[table_rows_of(i), :] += mm_tn(spread, q_flipped)
            turned = mm(spread, s.table[table_rows_of(i), :])
            high = turned.astype(BF16)
            rest = (turned - high.astype(F32)).astype(BF16)
            grad_q = unstack(grad_q + (mm(flip, high) + mm(flip, rest))).astype(BF16)
            cols = pl.ds(pl.multiple_of(p * 128, 128), 128)
            s.grad_pre[rows, cols] = (grad_q.astype(F32) * head_scale).astype(BF16)
            return carry

        lax.fori_loop(0, pairs, pair_step, 0)

    attend_back(0, ten)
    core_done(8, 9)
    first_done(0, 1)
    attend_back(1, 2 + ten)
    first_done(2)
    far_rows(0)
    attend_back(2, 1 - ten)
    first_done(4, 3)
    second_done(0, 1, 2)
    far_rows(1)
    attend_back(3, 3 - ten)
    first_done(5)
    second_done(4, 3)
    third_done(0)

    for p in range(pairs):
        at = local + p * 128
        s.grad_pre[:, at : at + 128] = s.grad_k[p].astype(BF16)
        at += local
        s.grad_pre[:, at : at + 128] = s.grad_v[p].astype(BF16)
    for j in range(2):
        gn2_copy(j).wait_send()

    def back_copy(i):
        rows = pl.ds(pl.multiple_of(i * RB, RB), RB)
        return remote(s.gn2_send.at[rows], s.gn1_recv.at[rows], s.gn1_sem, i, y_peer)

    def project_back(b, carry):
        start = pl.multiple_of(b * RF, RF)
        rows = pl.ds(start, RF)
        total = (
            mm_nt(s.grad_pre[rows, 0:local], attn_in[0])
            + mm_nt(s.grad_pre[rows, local : 2 * local], attn_in[1])
            + mm_nt(s.grad_pre[rows, 2 * local : 3 * local], attn_in[2])
        )
        unit, scale = norm_stats(hidden[rows, :].astype(F32))
        s.gn2_send[rows, :] = norm_back(total, unit, scale, gain1)
        own = pl.ds(pl.multiple_of(start + ten * RB, RB), RB)
        s.gn2_send[own, :] += s.grad_middle[b]
        s.n1[0:1, :] += col_sum(total * unit)
        s.n1[1:2, :] += col_sum(total)
        return carry

    lax.fori_loop(0, slots // RF, project_back, 0)

    def put(at, row):
        for j in range(row.shape[1] // 128):
            a, b, c, i = vec_place(at + j)
            s.vec[a, b, c, i : i + 1, :] = row[:, j * 128 : (j + 1) * 128]

    put(V_N1G, s.n1[0:1, :])
    put(V_N1B, s.n1[1:2, :])
    put(V_N2G, s.n2[0:1, :])
    put(V_N2B, s.n2[1:2, :])
    put(V_AOB, s.aob[...])
    put(V_FOB, s.fob[...])
    put(V_FIB, s.fib[...])
    put(V_AIB, col_sum(s.grad_pre[:, 0:local].astype(F32)))
    put(V_AIB + pairs, col_sum(s.grad_pre[:, 2 * local : 3 * local].astype(F32)))
    grad_rel = None
    rest = s.grad_table[...]
    for part in range(3):
        piece16 = rest.astype(BF16)
        term = mm_tn(pick, piece16)
        grad_rel = term if part == 0 else grad_rel + term
        rest = rest - piece16.astype(F32)
    grad_rel = grad_rel + pltpu.roll(grad_rel, HD, 1)
    fold = lax.broadcasted_iota(jnp.int32, (reach, 128), 1) < HD
    packed = jnp.where(fold, grad_rel[:reach], grad_rel[reach:])
    done = 0
    while done < reach:
        a, b, c, at = vec_place(V_REL + done)
        count = min(24 - at, reach - done)
        s.vec[a, b, c, at : at + count, :] = packed[done : done + count]
        done += count

    def vec_send(src, dst, at, peer):
        return remote(src, dst, s.vec_sem, at, peer)

    if ring:
        own_vec = s.vec.at[core, z_low_at, z_high_at]
        vec_core = vec_send(s.vec.at[1 - core], s.vec_half, 0, core_peer)
        vec_low = vec_send(s.vec.at[core, 1 - z_low_at], s.vec_quarter, 1, z_low)
        vec_high = vec_send(s.vec.at[core, z_low_at, 1 - z_high_at], s.vec_eighth.at[0], 2, z_high)
        vec_y = vec_send(own_vec.at[0:24], s.vec_eighth.at[1, 0:24], 3, y_peer)
        vec_x = vec_send(own_vec, s.vec_eighth.at[2], 4, x_peer)
        all_high, all_low, all_core = (
            vec_send(part, part, 5 + k, peer)
            for k, (part, peer) in enumerate(
                (
                    (s.vec_all.at[core, z_low_at, z_high_at], z_high),
                    (s.vec_all.at[core, z_low_at], z_low),
                    (s.vec_all.at[core], core_peer),
                )
            )
        )
        vec_core.start()
    else:
        vec_y = vec_send(s.vec.at[:, :, :, 0:24], s.vec_half, 0, y_peer)
        vec_y.start()
    back_copy(0).start()
    back_copy(1).start()

    for c in range(3):
        keep(grad_chunk(s.normed_t, s.grad_pre.at[:, c * local : (c + 1) * local]), QKV_AT[c])

    def finish_out(i, carry):
        start = pl.multiple_of(i * RB, RB)
        rows = pl.ds(start, RB)
        out_copy(i).wait_recv()
        branch = s.out_send[rows, :] + s.out_recv[rows, :]
        total = s.middle[rows, :] + (branch + out_bias2)
        output[rows, :] = (total * valid_rows(start, RB)).astype(BF16)
        results(i, output.at[rows], far_output.at[rows]).start()
        return carry

    def finish_hidden(i, carry):
        rows = pl.ds(pl.multiple_of(i * RB, RB), RB)
        back_copy(i).wait_recv()
        grad_hidden[rows, :] = (s.gn2_send[rows, :] + s.gn1_recv[rows, :]).astype(BF16)
        results(blocks + i, grad_hidden.at[rows], far_grad_hidden.at[rows]).start()
        return carry

    def sent():
        wo_y().wait_send()
        for i in range(blocks):
            for p in range(pairs):
                ctx_copy(i, p).wait_send()
            out_copy(i).wait_send()
            rows = slice(i * RB, (i + 1) * RB)
            results(i, output.at[rows], far_output.at[rows]).wait()
        for j in range(2):
            grad_ctx_copy(j).wait_send()
        if ring:
            for copy in (wo_x(), wo_z(), wo_xz(), wo_core(True), wo_core(False), wo_grad_copy(), vec_core, vec_low, vec_high):
                copy.wait_send()
            wo_grad_result().wait()
            for c in range(chunks):
                if c >= chunks - SLOTS:
                    core_copy(c).wait_send()
                first_copy(c).wait_send()
                second_copy(c).wait_send()
                third_copy(c).wait_send()
                if c not in WO_AT:
                    grad_result(c).wait()

    vec_out = results(2 * blocks, s.vec_all if ring else s.vec, far_vec)
    if ring:
        first_done(6)
        second_done(5)
        vec_core.wait_recv()
        s.vec[core] = s.vec[core] + s.vec_half[...]
        vec_low.start()
        core_done(*QKV_AT)
        first_done(7)
        second_done(6)
        third_done(2, 3)
        first_done(8)
        vec_low.wait_recv()
        s.vec[core, z_low_at] = s.vec[core, z_low_at] + s.vec_quarter[...]
        vec_high.start()
        second_done(7)
        third_done(5, 6)
        first_done(9)
        vec_high.wait_recv()
        own_vec[...] = own_vec[...] + s.vec_eighth[0]
        vec_y.start()
        third_done(7)
        wo_grad_copy().start()
        back_copy(2).start()
        back_copy(3).start()
        second_done(8)
        lax.fori_loop(0, blocks, finish_out, 0)
        first_done(10)
        second_done(9)
        third_done(8)
        vec_y.wait()
        own_vec[0:24] = own_vec[0:24] + s.vec_eighth[1, 0:24]
        vec_x.start()
        first_done(11)
        third_done(9, 1, 4)
        second_done(10)
        wo_grad_done()
        first_done(12)
        second_done(11)
        third_done(10)
        vec_x.wait()
        s.vec_all[core, z_low_at, z_high_at] = own_vec[...] + s.vec_eighth[2]
        all_high.start()
        second_done(12)
        third_done(11)
        all_high.wait_recv()
        all_low.start()
        third_done(12)
        all_low.wait_recv()
        all_core.start()
        sent()
        all_core.wait_recv()
    else:
        back_copy(2).start()
        back_copy(3).start()
        vec_y.wait()
        s.vec[:, :, :, 0:24] = s.vec[:, :, :, 0:24] + s.vec_half[...]
        lax.fori_loop(0, blocks, finish_out, 0)
        sent()
    vec_out.start()
    lax.fori_loop(0, blocks, finish_hidden, 0)
    for i in range(blocks):
        rows = slice(i * RB, (i + 1) * RB)
        back_copy(i).wait_send()
        results(blocks + i, grad_hidden.at[rows], far_grad_hidden.at[rows]).wait()
    vec_out.wait()
    if ring:
        for copy in (all_high, all_low, all_core):
            copy.wait_send()


def scratch_of(ring, slots, width, local, units, table_rows, chunks):
    pairs = local // 128
    blocks = slots // RB
    halves = slots // RF
    vm, dma = pltpu.VMEM, pltpu.SemaphoreType.DMA
    shapes = dict(
        hidden=vm((slots, width), BF16),
        attn_in=vm((3, width, local), BF16),
        attn_out=vm((local, width), BF16),
        ffn_in=vm((width, units), BF16),
        ffn_out=vm((units, width), BF16),
        cotangent=vm((slots, width), BF16),
        output=vm((slots, width), BF16),
        grad_hidden=vm((slots, width), BF16),
        in_s=dma((15,)),
        out_dma=dma((2 * blocks + 1 + chunks,)),
        normed_t=vm((halves, width, RF), BF16),
        q=vm((pairs, slots, 128), BF16),
        k=vm((pairs, slots, 128), BF16),
        v=vm((pairs, slots, 128), BF16),
        table=vm((2 * slots, 128), BF16),
        probs=vm((pairs, blocks, 2 * RB, slots), BF16),
        ctx=vm((2 * pairs, slots, 128), BF16),
        ctx_send=vm((pairs, slots, 128), F32),
        ctx_recv=vm((pairs, slots, 128), F32),
        wo=vm((2 * local, width), BF16),
        wo_stage=vm((local // 8, width) if ring else (local, width), F32),
        wo_recv=vm((2, 2, 2, local // 8, width) if ring else (local, width), F32),
        middle=vm((slots, width), F32),
        normed2_t=vm((halves, width, RF), BF16),
        top_t=vm((halves, width, RF), BF16),
        active=vm((slots, units), BF16),
        grad_pre=vm((slots, units), BF16),
        gn2_send=vm((slots, width), F32),
        gn2_recv=vm((blocks // 2, RB, width), F32),
        gn1_recv=vm((slots, width), F32),
        out_send=vm((slots, width), F32),
        out_recv=vm((slots, width), F32),
        grad_middle=vm((blocks // 2, RB, width), F32),
        grad_att_t=vm((blocks // 2, width, RB), BF16),
        grad_ctx_send=vm((blocks // 2, RB, local), F32),
        grad_ctx_recv=vm((blocks // 2, RB, local), F32),
        grad_ctx=vm((blocks, pairs, RB, 128), BF16),
        grad_k=vm((pairs, slots, 128), F32),
        grad_v=vm((pairs, slots, 128), F32),
        grad_table=vm((2 * slots, 128), F32),
        attn_in_bias=vm((2, local), BF16),
        rel_table_t=vm((HD, table_rows), BF16),
        attn_out_bias=vm((width // 128, 128), BF16),
        norm1_gain=vm((width // 128, 128), BF16),
        norm1_bias=vm((width // 128, 128), BF16),
        norm2_gain=vm((width // 128, 128), BF16),
        norm2_bias=vm((width // 128, 128), BF16),
        ffn_in_bias16=vm((units // 128, 128), BF16),
        ffn_out_bias=vm((width // 128, 128), BF16),
        vec=vm((2, 2, 2, 32, 128), F32),
        vec_half=vm((2, 2, 32, 128) if ring else (2, 2, 2, 24, 128), F32),
        fib=vm((1, units), F32),
        fob=vm((1, width), F32),
        aob=vm((1, width), F32),
        n1=vm((2, width), F32),
        n2=vm((2, width), F32),
        ffn_in_bias=vm((1, units), F32),
        free=pltpu.SemaphoreType.REGULAR((SLOTS,)),
        wo_sem=dma((2, 8)),
        ctx_sem=dma((2, blocks * pairs)),
        gn2_sem=dma((2, blocks // 2)),
        grad_ctx_sem=dma((2, blocks // 2)),
        gn1_sem=dma((2, blocks)),
        out_sem=dma((2, blocks)),
        vec_sem=dma((2, 8)),
    )
    if ring:
        shapes.update(
            g_own=vm((chunks, 2, 2, 2, 48, CW), F32),
            g_send=vm((SLOTS, 2, 2, 2, 48, CW), F32),
            core_recv=vm((SLOTS, 2, 2, 2, 48, CW), F32),
            first_recv=vm((chunks, 2, 2, 48, CW), F32),
            late_recv=vm((chunks, 3, 48, CW), F32),
            grads=vm((chunks, 48, CW), F32),
            vec_quarter=vm((2, 32, 128), F32),
            vec_eighth=vm((3, 32, 128), F32),
            vec_all=vm((2, 2, 2, 32, 128), F32),
            wo_grad=vm((48, CW), F32),
            wo_grad_recv=vm((48, CW), F32),
            gc_sem=dma((2, chunks)),
            g1_sem=dma((2, chunks)),
            g2_sem=dma((2, chunks)),
            g3_sem=dma((2, chunks)),
            wo_grad_sem=dma((2, 1)),
        )
    return shapes


def place(*refs):
    ins, outs, held, small, sems = refs[:7], refs[7:22], refs[22:29], refs[29:38], refs[38]
    bring = [pltpu.make_async_copy(far, near, sems.at[k]) for k, (far, near) in enumerate(zip(ins, held))]
    write = [
        pltpu.make_async_copy(near, far, sems.at[7 + k]) for k, (near, far) in enumerate(zip(held[:6] + small, outs))
    ]
    for copy in bring[::-1]:
        copy.start()
    bring[6].wait()
    vec = held[6]
    g_attn_in_bias, g_rel_t = small[:2]
    for ref, at in zip(small[2:], (V_AOB, V_N1G, V_N1B, V_N2G, V_N2B, V_FIB, V_FOB)):
        ref[...] = jnp.concatenate(vec_rows(vec, at, ref.shape[0]), axis=0)
    count = g_attn_in_bias.shape[1] // 128
    for k in range(2):
        g_attn_in_bias[k : k + 1, :] = jnp.concatenate(vec_rows(vec, V_AIB + k * count, count), axis=1)
    reach = g_rel_t.shape[1] // 2
    turned = jnp.concatenate(vec_rows(vec, V_REL, reach), axis=0).T
    g_rel_t[...] = jnp.concatenate([turned[:HD], turned[HD:]], axis=1)
    for copy in write[6:]:
        copy.start()
    for k in range(6):
        bring[k].wait()
        write[k].start()
    for copy in write:
        copy.wait()


def on_device(
    ring,
    hidden, lengths, attn_in, attn_in_bias, rel_table, attn_out, attn_out_bias,
    norm1_gain, norm1_bias, norm2_gain, norm2_bias,
    ffn_in, ffn_in_bias, ffn_out, ffn_out_bias, cotangent,
):
    slots, width = hidden.shape
    local = attn_out.shape[0]
    units = ffn_in.shape[1]
    table_rows = rel_table.shape[0]
    chunks = 2 * units // CW + 5
    rows = width // 16
    shape = jax.ShapeDtypeStruct
    shapes = scratch_of(ring, slots, width, local, units, table_rows, chunks)
    names = tuple(shapes)
    outs = [
        shape((slots, width), BF16), shape((slots, width), BF16), shape((3, rows, local), F32), shape((rows, local), F32),
        shape((rows, units), F32), shape((rows, units), F32), shape((2, 2, 2, 32, 128), F32),
    ]
    far = pl.BlockSpec(memory_space=pl.ANY)
    near = pl.BlockSpec(memory_space=pltpu.VMEM)
    out_specs = [far] * 7
    if not ring:
        names = (FULL,) + names
        outs.append(shape((chunks, width, CW), F32))
        out_specs.append(near)

    def lanes(vector):
        return vector.reshape(vector.shape[0] // 128, 128)

    def unlanes(array):
        return array.reshape(array.shape[0] * 128)

    results = pl.pallas_call(
        partial(body, ring, names),
        out_shape=outs,
        in_specs=[pl.BlockSpec(memory_space=pltpu.SMEM)] + [far] * 15,
        out_specs=out_specs,
        scratch_shapes=list(shapes.values()),
        compiler_params=pltpu.CompilerParams(
            collective_id=0, has_side_effects=True, vmem_limit_bytes=64 * 1024 * 1024
        ),
    )(
        lengths, attn_in_bias, rel_table.T, lanes(attn_out_bias), lanes(norm1_gain), lanes(norm1_bias),
        lanes(norm2_gain), lanes(norm2_bias), lanes(ffn_in_bias), lanes(ffn_out_bias),
        hidden, attn_in, attn_out, ffn_in, ffn_out, cotangent,
    )
    if ring:
        vector = shape((width // 128, 128), F32)
        small = [
            shape((2, local), F32), shape((HD, table_rows), F32), vector, vector, vector, vector, vector,
            shape((units // 128, 128), F32), vector,
        ]
        placed = pl.pallas_call(
            place,
            out_shape=outs[:6] + small,
            in_specs=[far] * 7,
            out_specs=[far] * 15,
            scratch_shapes=[pltpu.VMEM(array.shape, array.dtype) for array in outs + small]
            + [pltpu.SemaphoreType.DMA((22,))],
        )(*results)
        (
            output, grad_hidden, g_attn_in, g_attn_out_t, g_ffn_in, g_ffn_out_t, g_attn_in_bias, g_rel_t,
            g_attn_out_bias, n1g, n1b, n2g, n2b, g_ffn_in_bias, g_ffn_out_bias,
        ) = placed
        return (
            output, grad_hidden, g_attn_in, g_attn_in_bias, g_rel_t.T, g_attn_out_t.T, unlanes(g_attn_out_bias),
            unlanes(n1g), unlanes(n1b), unlanes(n2g), unlanes(n2b),
            g_ffn_in, unlanes(g_ffn_in_bias), g_ffn_out_t.T, unlanes(g_ffn_out_bias),
        )
    output, grad_hidden, vec, full = results[0], results[1], results[6], results[7]

    def wide(which):
        return jnp.concatenate([full[c] for c in which], axis=1)

    def scatter(value, dim, axis="dp"):
        return lax.psum_scatter(value, axis, scatter_dimension=dim, tiled=True)

    g_ffn_out = scatter(wide(OUT_AT).T, 1)
    g_ffn_in = scatter(wide(IN_AT), 0)
    g_attn_out = scatter(scatter(full[WO_AT[0] : WO_AT[1] + 1], 0, "tensor")[0].T, 1)
    g_attn_in = scatter(full[QKV_AT[0] : QKV_AT[2] + 1], 1)
    vec = lax.psum(vec, "dp")

    def row(at, count=width):
        return unlanes(jnp.concatenate(vec_rows(vec, at, count // 128), axis=0))

    rel_pairs = jnp.concatenate(vec_rows(vec, V_REL, table_rows // 2), axis=0)
    grad_rel = jnp.concatenate([rel_pairs[:, :HD], rel_pairs[:, HD:]], axis=0)
    return (
        output, grad_hidden, g_attn_in,
        row(V_AIB, 2 * local).reshape(2, local), grad_rel, g_attn_out, row(V_AOB),
        row(V_N1G), row(V_N1B), row(V_N2G), row(V_N2B),
        g_ffn_in, row(V_FIB, units), g_ffn_out, row(V_FOB),
    )


def solution(mesh):
    ring = mesh.shape["dp"] == 16
    return jax.shard_map(
        partial(on_device, ring),
        mesh=mesh,
        in_specs=(
            P("dp", None), P("dp"), P(None, None, "tensor"), P(None, "tensor"), P(),
            P("tensor", None), P(), P(), P(), P(), P(),
            P(None, "tensor"), P("tensor"), P("tensor", None), P(), P("dp", None),
        ),
        out_specs=(
            P("dp", None), P("dp", None), P(None, "dp", "tensor"), P(None, "tensor"), P(),
            P("tensor", "dp"), P(), P(), P(), P(), P(),
            P("dp", "tensor"), P("tensor"), P("tensor", "dp"), P(),
        ),
        check_vma=False,
    )
```

```python
from functools import partial
from types import SimpleNamespace

import jax
import jax.numpy as jnp
from jax import lax
from jax.experimental import pallas as pl
from jax.experimental.pallas import tpu as pltpu
from jax.sharding import PartitionSpec as P

HD = 64
EPSILON = 1e-05
NEGATIVE = -1e30
SQRT_HALF = 0.7071067811865476
INV_SQRT_2PI = 0.3989422804014327
RB = 128
RF = 256
CW = 384
FULL = "g_full"
OUT_AT, IN_AT, WO_AT, QKV_AT = (0, 1, 2, 3), (4, 5, 8, 9), (6, 7), (10, 11, 12)
Z_FIRST = (0, 2, 3)
SLOTS = 4
MESH = pl.DeviceIdType.MESH
F32 = jnp.float32
BF16 = jnp.bfloat16


def mm(a, b):
    return jnp.dot(a, b, preferred_element_type=F32)


def mm_nt(a, b):
    return lax.dot_general(a, b, (((1,), (1,)), ((), ())), preferred_element_type=F32)


def mm_tn(a, b):
    return lax.dot_general(a, b, (((0,), (0,)), ((), ())), preferred_element_type=F32)


def norm_stats(value):
    mean = jnp.mean(value, axis=-1, keepdims=True)
    centred = value - mean
    scale = lax.rsqrt(jnp.mean(centred * centred, axis=-1, keepdims=True) + EPSILON)
    return centred * scale, scale


def norm_back(grad, unit, scale, gain):
    grad_unit = grad * gain
    inner = (
        grad_unit
        - jnp.mean(grad_unit, axis=-1, keepdims=True)
        - unit * jnp.mean(grad_unit * unit, axis=-1, keepdims=True)
    )
    return inner * scale


def col_sum(value):
    return jnp.sum(value, axis=0, keepdims=True)


def lanes_of(ref3, rows):
    return jnp.concatenate([ref3[p, rows, :] for p in range(ref3.shape[0])], axis=1)


V_N1G, V_N1B, V_AOB, V_N2G, V_N2B, V_REL, V_FOB, V_FIB, V_AIB = 0, 6, 12, 18, 24, 32, 192, 198, 210
YROWS, VROWS = 192, 216


def vec_place(row):
    part, at = (row // 24, row % 24) if row < YROWS else ((row - YROWS) // 3, 24 + (row - YROWS) % 3)
    return part // 4, part // 2 % 2, part % 2, at


def vec_rows(vec, first, count):
    found = []
    for row in range(first, first + count):
        a, b, c, at = vec_place(row)
        found.append(vec[a, b, c, at : at + 1, :])
    return found


def body(
    ring, names,
    lengths, far_attn_in_bias, far_rel_table_t, far_attn_out_bias, far_norm1_gain, far_norm1_bias, far_norm2_gain,
    far_norm2_bias, far_ffn_in_bias, far_ffn_out_bias, far_hidden, far_attn_in, far_attn_out, far_ffn_in, far_ffn_out, far_cotangent,
    far_output, far_grad_hidden, far_attn_in_grad, far_attn_out_grad, far_ffn_in_grad, far_ffn_out_grad, far_vec,
    *scratch,
):
    s = SimpleNamespace(**dict(zip(names, scratch)))

    def bring(at, near, far):
        copy = pltpu.make_async_copy(far, near, s.in_s.at[at])
        copy.start()
        return copy

    bring_attn_out = bring(0, s.attn_out, far_attn_out)
    bring_hidden = bring(1, s.hidden, far_hidden)
    bring_attn_in = bring(2, s.attn_in, far_attn_in)
    small = (
        (s.attn_in_bias, far_attn_in_bias), (s.rel_table_t, far_rel_table_t), (s.attn_out_bias, far_attn_out_bias),
        (s.norm1_gain, far_norm1_gain), (s.norm1_bias, far_norm1_bias), (s.norm2_gain, far_norm2_gain),
        (s.norm2_bias, far_norm2_bias), (s.ffn_in_bias16, far_ffn_in_bias), (s.ffn_out_bias, far_ffn_out_bias),
    )
    bring_small = [bring(6 + k, near, far) for k, (near, far) in enumerate(small)]
    hidden, attn_in, attn_out = s.hidden, s.attn_in, s.attn_out
    cotangent, ffn_in, ffn_out = s.cotangent, s.ffn_in, s.ffn_out
    output, grad_hidden = s.output, s.grad_hidden
    slots, width = hidden.shape
    local = attn_out.shape[0]
    pairs = local // 128
    units = ffn_in.shape[1]
    table_rows = s.rel_table_t.shape[1]
    reach = table_rows // 2
    blocks = slots // RB
    ext = slots + RB
    head_scale = HD ** (-0.5)

    dp = lax.axis_index("dp")
    ten = lax.axis_index("tensor")
    y_peer = (dp, 1 - ten)
    if ring:
        core = lax.rem(dp, 2)
        x_at = lax.rem(lax.div(dp, 2), 2)
        z_low_at = lax.rem(lax.div(dp, 4), 2)
        z_high_at = lax.div(dp, 8)
        core_peer = (dp + 1 - 2 * core, ten)
        x_peer = (dp + 2 - 4 * x_at, ten)
        z_low = (dp + 4 - 8 * z_low_at, ten)
        z_high = (dp + 8 - 16 * z_high_at, ten)
        greet = [y_peer, core_peer, x_peer, z_low, z_high]
    else:
        greet = [y_peer]

    barrier = pltpu.get_barrier_semaphore()
    for peer in greet:
        pl.semaphore_signal(barrier, inc=1, device_id=peer, device_id_type=MESH)

    def remote(src, dst, sems, at, peer):
        return pltpu.make_async_remote_copy(
            src_ref=src, dst_ref=dst, send_sem=sems.at[0, at], recv_sem=sems.at[1, at],
            device_id=peer, device_id_type=MESH,
        )

    bring_attn_out.wait()
    if ring:
        piece = local // 8
        mine = (2 * z_low_at + x_at) * 2 + core
        s.wo_stage[...] = attn_out[pl.ds(pl.multiple_of(mine * piece, 16), piece), :].astype(F32)

        def wo_y():
            return remote(s.wo_stage, s.wo_recv.at[z_low_at, x_at, core], s.wo_sem, 0, y_peer)

        def wo_pass(part, at, peer):
            return remote(part, part, s.wo_sem, at, peer)

        def wo_x():
            return wo_pass(s.wo_recv.at[z_low_at, x_at, core], 1, x_peer)

        def wo_z():
            return wo_pass(s.wo_recv.at[z_low_at, x_at, core], 2, z_low)

        def wo_xz():
            return wo_pass(s.wo_recv.at[z_low_at, 1 - x_at, core], 3, z_low)

        def wo_core(near):
            return wo_pass(s.wo_recv.at[z_low_at if near else 1 - z_low_at, :, core], 4 if near else 5, core_peer)
    else:
        s.wo_stage[...] = attn_out[...].astype(F32)

        def wo_y():
            return remote(s.wo_stage, s.wo_recv, s.wo_sem, 0, y_peer)

    pl.semaphore_wait(barrier, len(greet))
    wo_y().start()

    def flat(ref):
        value = ref[...].astype(F32)
        return jnp.concatenate([value[j : j + 1] for j in range(value.shape[0])], axis=1)

    for copy in bring_small:
        copy.wait()
    bias_q = s.attn_in_bias[0:1, :].astype(F32)
    bias_v = s.attn_in_bias[1:2, :].astype(F32)
    gain1, offset1 = flat(s.norm1_gain), flat(s.norm1_bias)
    gain2, offset2 = flat(s.norm2_gain), flat(s.norm2_bias)
    out_bias1, out_bias2 = flat(s.attn_out_bias), flat(s.ffn_out_bias)
    s.ffn_in_bias[...] = flat(s.ffn_in_bias16)
    seq_len = lengths[0]

    ext_rows = 2 * slots
    distance = slots - 1 - lax.broadcasted_iota(jnp.int32, (ext_rows, table_rows), 0)
    bucket = jnp.clip(distance, -reach, reach - 1) + reach
    pick = (bucket == lax.broadcasted_iota(jnp.int32, (ext_rows, table_rows), 1)).astype(BF16)
    rel_t = s.rel_table_t[...]
    s.table[...] = mm_nt(pick, jnp.concatenate([rel_t, rel_t], axis=0)).astype(BF16)

    def project(i, carry):
        rows = pl.ds(pl.multiple_of(i * RF, RF), RF)
        unit, unused = norm_stats(hidden[rows, :].astype(F32))
        normed = (unit * gain1 + offset1).astype(BF16)
        s.normed_t[i] = normed.T
        q = ((mm(normed, attn_in[0]) + bias_q) * head_scale).astype(BF16)
        k = mm(normed, attn_in[1]).astype(BF16)
        v = (mm(normed, attn_in[2]) + bias_v).astype(BF16)
        for p in range(pairs):
            s.q[p, rows, :] = q[:, p * 128 : (p + 1) * 128]
            s.k[p, rows, :] = k[:, p * 128 : (p + 1) * 128]
            s.v[p, rows, :] = v[:, p * 128 : (p + 1) * 128]
        return carry

    bring_hidden.wait()
    bring_attn_in.wait()
    bring_cotangent = bring(3, s.cotangent, far_cotangent)
    bring_ffn_in = bring(4, s.ffn_in, far_ffn_in)
    bring_ffn_out = bring(5, s.ffn_out, far_ffn_out)
    lax.fori_loop(0, slots // RF, project, 0)

    low_lanes = lax.broadcasted_iota(jnp.int32, (RB, 128), 1) < HD
    key_ok = lax.broadcasted_iota(jnp.int32, (1, slots), 1) < seq_len

    def stack(both):
        zero = jnp.zeros_like(both)
        return jnp.concatenate([jnp.where(low_lanes, both, zero), jnp.where(low_lanes, zero, both)], axis=0)

    def unstack(tall):
        return jnp.where(low_lanes, tall[:RB], tall[RB:])

    def table_rows_of(i):
        return pl.ds(pl.multiple_of(slots - RB - i * RB, RB), ext)

    def ctx_copy(i, p):
        rows = pl.ds(pl.multiple_of(i * RB, RB), RB)
        return remote(s.ctx_send.at[p, rows], s.ctx_recv.at[p, rows], s.ctx_sem, i * pairs + p, y_peer)

    def attend(i):
        rows = pl.ds(pl.multiple_of(i * RB, RB), RB)

        def pair_step(p, carry):
            qs = stack(s.q[p, rows, :])
            spread = mm_nt(qs, s.table[table_rows_of(i), :])
            shift = ext - RB + 1
            bias = jnp.concatenate(
                [
                    pltpu.roll(spread[:RB], shift, 1, stride=1, stride_axis=0)[:, :slots],
                    pltpu.roll(spread[RB:], shift, 1, stride=1, stride_axis=0)[:, :slots],
                ],
                axis=0,
            )
            scores = jnp.where(key_ok, mm_nt(qs, s.k[p]) + bias, NEGATIVE)
            expon = jnp.exp(scores - jnp.max(scores, axis=-1, keepdims=True))
            shares = (expon * (1.0 / jnp.sum(expon, axis=-1, keepdims=True))).astype(BF16)
            s.probs[p, i] = shares
            context = unstack(mm(shares, s.v[p])).astype(BF16)
            s.ctx[ten * pairs + p, rows, :] = context
            s.ctx_send[p, rows, :] = context.astype(F32)
            ctx_copy(i, p).start()
            return carry

        lax.fori_loop(0, pairs, pair_step, 0)

    half = pl.ds(pl.multiple_of(ten * local, 128), local)
    far_half = pl.ds(pl.multiple_of((1 - ten) * local, 128), local)
    s.wo[half, :] = attn_out[...]
    attend(0)
    if ring:
        wo_y().wait_recv()
        wo_x().start()
        wo_z().start()
    attend(1)
    if ring:
        wo_x().wait_recv()
        wo_xz().start()
        wo_core(True).start()
    attend(2)
    attend(3)

    if ring:
        wo_z().wait_recv()
        wo_xz().wait_recv()
        wo_core(False).start()
        wo_core(True).wait_recv()
        wo_core(False).wait_recv()
        s.wo[far_half, :] = s.wo_recv[...].reshape(local, width).astype(BF16)
    else:
        wo_y().wait_recv()
        s.wo[far_half, :] = s.wo_recv[...].astype(BF16)
    bring_cotangent.wait()
    bring_ffn_in.wait()
    bring_ffn_out.wait()

    def valid_rows(start, count):
        return (lax.broadcasted_iota(jnp.int32, (count, 1), 0) + start < seq_len).astype(F32)

    def grad_ctx_copy(i):
        rows = pl.ds(i * RB, RB)
        return remote(s.grad_ctx_send.at[rows], s.grad_ctx_recv.at[rows], s.grad_ctx_sem, i, y_peer)

    def out_copy(i):
        rows = pl.ds(pl.multiple_of(i * RB, RB), RB)
        return remote(s.out_send.at[rows], s.out_recv.at[rows], s.out_sem, i, y_peer)

    s.vec[...] = jnp.zeros_like(s.vec)
    s.fib[...] = jnp.zeros_like(s.fib)
    s.fob[...] = jnp.zeros_like(s.fob)
    s.aob[...] = jnp.zeros_like(s.aob)
    s.n1[...] = jnp.zeros_like(s.n1)
    s.n2[...] = jnp.zeros_like(s.n2)

    step_units = 512

    def feed(b):
        start = b * RF
        rows = slice(start, start + RF)
        for j in range(RF // RB):
            for p in range(pairs):
                ctx_copy(b * (RF // RB) + j, p).wait_recv()
        for p in range(pairs):
            s.ctx[(1 - ten) * pairs + p, rows, :] = s.ctx_recv[p, rows, :].astype(BF16)
        attended = mm(lanes_of(s.ctx, rows), s.wo[...]) + out_bias1
        middle = hidden[rows, :].astype(F32) + attended
        s.middle[rows, :] = middle
        unit, scale = norm_stats(middle)
        normed = (unit * gain2 + offset2).astype(BF16)
        s.normed2_t[b] = normed.T
        top = cotangent[rows, :].astype(F32) * valid_rows(start, RF)
        s.fob[...] += col_sum(top)
        half_top = 0.5 * top
        top = top.astype(BF16)
        s.top_t[b] = top.T
        for c in range(units // step_units):
            cols = slice(c * step_units, (c + 1) * step_units)
            pre = mm(normed, ffn_in[:, cols]) + s.ffn_in_bias[:, cols]
            share = 0.5 + 0.5 * lax.erf(pre * SQRT_HALF)
            active = (pre * share).astype(BF16)
            s.active[rows, cols] = active
            slope = share + pre * (jnp.exp(-0.5 * pre * pre) * INV_SQRT_2PI)
            grad_pre = (mm_nt(top, ffn_out[cols, :]) * slope).astype(BF16)
            s.grad_pre[rows, cols] = grad_pre
            s.fib[:, cols] += col_sum(grad_pre.astype(F32))
            back = mm_nt(grad_pre, ffn_in[:, cols])
            onward = mm(active, ffn_out[cols, :])
            if c == 0:
                s.gn1_send[rows, :] = back
                s.out_send[rows, :] = onward
            else:
                s.gn1_send[rows, :] += back
                s.out_send[rows, :] += onward
            if b == 1:
                for chunk in range(per):
                    if c * step_units < (chunk + 1) * CW <= (c + 1) * step_units:
                        keep(out_grad(chunk, 1), chunk, True)
                if c > 0:
                    core_done(c - 1)
        back = s.gn1_send[rows, :]
        s.n2[0:1, :] += col_sum(back * unit)
        s.n2[1:2, :] += col_sum(back)
        grad_middle = half_top + norm_back(back, unit, scale, gain2)
        s.grad_middle[rows, :] = grad_middle
        grad_attended = grad_middle.astype(BF16)
        s.grad_ctx_send[rows, :] = mm_nt(grad_attended, s.wo[far_half, :])
        for j in range(RF // RB):
            grad_ctx_copy(b * (RF // RB) + j).start()
        s.grad_ctx_own[rows, :] = mm_nt(grad_attended, attn_out[...])
        s.aob[...] += col_sum(grad_attended.astype(F32))
        s.grad_att_t[b] = grad_attended.T

    feed(0)

    def grad_chunk(left_t, right):
        total = mm(left_t[0], right[0:RF])
        for b in range(1, slots // RF):
            total += mm(left_t[b], right[b * RF : (b + 1) * RF])
        return total

    per = units // CW
    chunks = 2 * per + 5

    def hold(total, chunk, begun=False):
        if not ring:
            s.g_full[chunk] = s.g_full[chunk] + total if begun else total
            return
        slot = chunk % SLOTS
        parts = total.reshape(8, 2, 48, CW)
        even, odd = parts[:, 0], parts[:, 1]
        near = jnp.where(core == 0, even, odd).reshape(2, 2, 2, 48, CW)
        far = jnp.where(core == 0, odd, even).reshape(2, 2, 2, 48, CW)
        s.g_own[chunk] = s.g_own[chunk] + near if begun else near
        s.g_send[slot] = s.g_send[slot] + far if begun else far

    def keep(total, chunk, begun=False):
        if ring and chunk >= SLOTS:
            core_copy(chunk - SLOTS).wait_send()
            pl.semaphore_wait(s.free.at[chunk % SLOTS], 1)
        hold(total, chunk, begun)
        if ring:
            core_copy(chunk).start()

    def core_copy(chunk):
        slot = chunk % SLOTS
        return remote(s.g_send.at[slot], s.core_recv.at[slot], s.gc_sem, chunk, core_peer)

    def first_copy(chunk):
        own = s.g_own.at[chunk]
        if chunk in Z_FIRST:
            return remote(own.at[:, 1 - z_low_at], s.first_recv.at[chunk], s.g1_sem, chunk, z_low)
        return remote(own.at[:, :, 1 - x_at], s.first_recv.at[chunk], s.g1_sem, chunk, x_peer)

    def second_copy(chunk):
        own = s.g_own.at[chunk]
        into = s.late_recv.at[chunk, 0:2]
        if chunk in Z_FIRST:
            return remote(own.at[1 - z_high_at, z_low_at], into, s.g2_sem, chunk, z_high)
        return remote(own.at[:, 1 - z_low_at, x_at], into, s.g2_sem, chunk, z_low)

    def third_copy(chunk):
        own = s.g_own.at[chunk]
        into = s.late_recv.at[chunk, 2]
        if chunk in Z_FIRST:
            return remote(own.at[z_high_at, z_low_at, 1 - x_at], into, s.g3_sem, chunk, x_peer)
        return remote(own.at[1 - z_high_at, z_low_at, x_at], into, s.g3_sem, chunk, z_high)

    def core_done(*which):
        for chunk in which if ring else ():
            core_copy(chunk).wait_recv()
            s.g_own[chunk] = s.g_own[chunk] + s.core_recv[chunk % SLOTS]
            if chunk + SLOTS < chunks:
                pl.semaphore_signal(s.free.at[chunk % SLOTS], inc=1, device_id=core_peer, device_id_type=MESH)
            first_copy(chunk).start()

    def first_done(*which):
        for chunk in which if ring else ():
            first_copy(chunk).wait_recv()
            if chunk in Z_FIRST:
                s.g_own[chunk, :, z_low_at] = s.g_own[chunk, :, z_low_at] + s.first_recv[chunk]
            else:
                s.g_own[chunk, :, :, x_at] = s.g_own[chunk, :, :, x_at] + s.first_recv[chunk]
            second_copy(chunk).start()

    def second_done(*which):
        for chunk in which if ring else ():
            second_copy(chunk).wait_recv()
            if chunk in Z_FIRST:
                s.g_own[chunk, z_high_at, z_low_at] = s.g_own[chunk, z_high_at, z_low_at] + s.late_recv[chunk, 0:2]
            else:
                s.g_own[chunk, :, z_low_at, x_at] = s.g_own[chunk, :, z_low_at, x_at] + s.late_recv[chunk, 0:2]
            third_copy(chunk).start()

    def results(at, near, far):
        return pltpu.make_async_copy(near, far, s.out_dma.at[at])

    def grad_result(chunk):
        if chunk in OUT_AT:
            c = OUT_AT.index(chunk)
            far = far_ffn_out_grad.at[:, c * CW : (c + 1) * CW]
        elif chunk in IN_AT:
            c = IN_AT.index(chunk)
            far = far_ffn_in_grad.at[:, c * CW : (c + 1) * CW]
        else:
            far = far_attn_in_grad.at[QKV_AT.index(chunk)]
        return results(2 * blocks + 1 + chunk, s.grads.at[chunk], far)

    def third_done(*which):
        for chunk in which if ring else ():
            third_copy(chunk).wait_recv()
            s.grads[chunk] = s.g_own[chunk, z_high_at, z_low_at, x_at] + s.late_recv[chunk, 2]
            if chunk not in WO_AT:
                grad_result(chunk).start()

    def wo_grad_copy():
        return remote(s.grads.at[WO_AT[0] + 1 - ten], s.wo_grad_recv, s.wo_grad_sem, 0, y_peer)

    def wo_grad_done():
        wo_grad_copy().wait_recv()
        s.wo_grad[...] = s.grads[WO_AT[0] + ten] + s.wo_grad_recv[...]
        wo_grad_result().start()

    def wo_grad_result():
        return results(2 * blocks + 1 + WO_AT[0], s.wo_grad, far_attn_out_grad)

    def out_grad(c, b):
        return mm(s.top_t[b], s.active[b * RF : (b + 1) * RF, c * CW : (c + 1) * CW])

    def keep_in(c):
        keep(grad_chunk(s.normed2_t, s.grad_pre.at[:, c * CW : (c + 1) * CW]), IN_AT[c])

    def keep_wo(h):
        context = jnp.concatenate([s.ctx[h * pairs + p] for p in range(pairs)], axis=1)
        total = grad_chunk(s.grad_att_t, context)
        keep(total, WO_AT[h])

    for c in range(per):
        hold(out_grad(c, 0), c)
    feed(1)
    for i in range(blocks):
        out_copy(i).start()
    for c in range(2):
        keep_in(c)
        core_done(2 + c)
    for h in range(2):
        keep_wo(h)
        core_done(4 + h)
    for c in range(2):
        keep_in(2 + c)
        core_done(6 + c)

    s.grad_k[...] = jnp.zeros_like(s.grad_k)
    s.grad_v[...] = jnp.zeros_like(s.grad_v)
    s.grad_table[...] = jnp.zeros_like(s.grad_table)
    flip_row = lax.broadcasted_iota(jnp.int32, (2 * RB, 2 * RB), 0)
    flip_col = lax.broadcasted_iota(jnp.int32, (2 * RB, 2 * RB), 1)
    same_half = (flip_row < RB) == (flip_col < RB)
    local_row = lax.rem(flip_row, RB)
    local_col = lax.rem(flip_col, RB)
    flip = (same_half & (local_row + local_col == RB - 1)).astype(BF16)

    def attend_back(i):
        rows = pl.ds(i * RB, RB)
        grad_ctx_copy(i).wait_recv()

        def pair_step(p, carry):
            qs = stack(s.q[p, rows, :])
            cols = pl.ds(pl.multiple_of(p * 128, 128), 128)
            gs = stack((s.grad_ctx_own[rows, cols] + s.grad_ctx_recv[rows, cols]).astype(BF16))
            low = s.probs[p, i]
            s.grad_v[p] += mm_tn(low, gs)
            shares = low.astype(F32)
            grad_shares = mm_nt(gs, s.v[p])
            inner = jnp.sum(grad_shares * shares, axis=-1, keepdims=True)
            grad_scores = (shares * (grad_shares - inner)).astype(BF16)
            s.grad_k[p] += mm_tn(grad_scores, qs)
            grad_q = mm(grad_scores, s.k[p])
            flipped = mm(flip, grad_scores)
            wide = jnp.concatenate([flipped, jnp.zeros((2 * RB, RB), F32)], axis=1)
            spread = jnp.concatenate(
                [
                    pltpu.roll(wide[:RB], 0, 1, stride=1, stride_axis=0),
                    pltpu.roll(wide[RB:], 0, 1, stride=1, stride_axis=0),
                ],
                axis=0,
            ).astype(BF16)
            q_flipped = mm(flip, qs).astype(BF16)
            s.grad_table[table_rows_of(i), :] += mm_tn(spread, q_flipped)
            turned = mm(spread, s.table[table_rows_of(i), :])
            high = turned.astype(BF16)
            rest = (turned - high.astype(F32)).astype(BF16)
            grad_q = unstack(grad_q + (mm(flip, high) + mm(flip, rest))).astype(BF16)
            s.grad_pre[rows, cols] = (grad_q.astype(F32) * head_scale).astype(BF16)
            return carry

        lax.fori_loop(0, pairs, pair_step, 0)

    attend_back(0)
    core_done(8, 9)
    first_done(0, 1)
    attend_back(1)
    first_done(2, 4)
    attend_back(2)
    first_done(3, 5)
    attend_back(3)
    second_done(0, 1)

    for p in range(pairs):
        at = local + p * 128
        s.grad_pre[:, at : at + 128] = s.grad_k[p].astype(BF16)
        at += local
        s.grad_pre[:, at : at + 128] = s.grad_v[p].astype(BF16)
    def back_copy(i):
        rows = pl.ds(pl.multiple_of(i * RB, RB), RB)
        return remote(s.gn1_send.at[rows], s.gn1_recv.at[rows], s.gn1_sem, i, y_peer)

    def project_back(b, carry):
        start = pl.multiple_of(b * RF, RF)
        rows = pl.ds(start, RF)
        total = (
            mm_nt(s.grad_pre[rows, 0:local], attn_in[0])
            + mm_nt(s.grad_pre[rows, local : 2 * local], attn_in[1])
            + mm_nt(s.grad_pre[rows, 2 * local : 3 * local], attn_in[2])
        )
        unit, scale = norm_stats(hidden[rows, :].astype(F32))
        s.gn1_send[rows, :] = norm_back(total, unit, scale, gain1) + s.grad_middle[rows, :]
        s.n1[0:1, :] += col_sum(total * unit)
        s.n1[1:2, :] += col_sum(total)
        return carry

    lax.fori_loop(0, slots // RF, project_back, 0)

    def put(at, row):
        for j in range(row.shape[1] // 128):
            a, b, c, i = vec_place(at + j)
            s.vec[a, b, c, i : i + 1, :] = row[:, j * 128 : (j + 1) * 128]

    put(V_N1G, s.n1[0:1, :])
    put(V_N1B, s.n1[1:2, :])
    put(V_N2G, s.n2[0:1, :])
    put(V_N2B, s.n2[1:2, :])
    put(V_AOB, s.aob[...])
    put(V_FOB, s.fob[...])
    put(V_FIB, s.fib[...])
    put(V_AIB, col_sum(s.grad_pre[:, 0:local].astype(F32)))
    put(V_AIB + pairs, col_sum(s.grad_pre[:, 2 * local : 3 * local].astype(F32)))
    grad_rel = None
    rest = s.grad_table[...]
    for part in range(3):
        piece16 = rest.astype(BF16)
        term = mm_tn(pick, piece16)
        grad_rel = term if part == 0 else grad_rel + term
        rest = rest - piece16.astype(F32)
    grad_rel = grad_rel + pltpu.roll(grad_rel, HD, 1)
    fold = lax.broadcasted_iota(jnp.int32, (reach, 128), 1) < HD
    packed = jnp.where(fold, grad_rel[:reach], grad_rel[reach:])
    done = 0
    while done < reach:
        a, b, c, at = vec_place(V_REL + done)
        count = min(24 - at, reach - done)
        s.vec[a, b, c, at : at + count, :] = packed[done : done + count]
        done += count

    def vec_send(src, dst, at, peer):
        return remote(src, dst, s.vec_sem, at, peer)

    if ring:
        own_vec = s.vec.at[core, z_low_at, z_high_at]
        vec_core = vec_send(s.vec.at[1 - core], s.vec_half, 0, core_peer)
        vec_low = vec_send(s.vec.at[core, 1 - z_low_at], s.vec_quarter, 1, z_low)
        vec_high = vec_send(s.vec.at[core, z_low_at, 1 - z_high_at], s.vec_eighth.at[0], 2, z_high)
        vec_y = vec_send(own_vec.at[0:24], s.vec_eighth.at[1, 0:24], 3, y_peer)
        vec_x = vec_send(own_vec, s.vec_eighth.at[2], 4, x_peer)
        all_high, all_low, all_core = (
            vec_send(part, part, 5 + k, peer)
            for k, (part, peer) in enumerate(
                (
                    (s.vec_all.at[core, z_low_at, z_high_at], z_high),
                    (s.vec_all.at[core, z_low_at], z_low),
                    (s.vec_all.at[core], core_peer),
                )
            )
        )
        vec_core.start()
    else:
        vec_y = vec_send(s.vec.at[:, :, :, 0:24], s.vec_half, 0, y_peer)
        vec_y.start()
    back_copy(0).start()
    back_copy(1).start()

    for c in range(3):
        keep(grad_chunk(s.normed_t, s.grad_pre.at[:, c * local : (c + 1) * local]), QKV_AT[c])

    def finish_out(i, carry):
        start = pl.multiple_of(i * RB, RB)
        rows = pl.ds(start, RB)
        out_copy(i).wait_recv()
        branch = s.out_send[rows, :] + s.out_recv[rows, :]
        total = s.middle[rows, :] + (branch + out_bias2)
        output[rows, :] = (total * valid_rows(start, RB)).astype(BF16)
        results(i, output.at[rows], far_output.at[rows]).start()
        return carry

    def finish_hidden(i, carry):
        rows = pl.ds(pl.multiple_of(i * RB, RB), RB)
        back_copy(i).wait_recv()
        grad_hidden[rows, :] = (s.gn1_send[rows, :] + s.gn1_recv[rows, :]).astype(BF16)
        results(blocks + i, grad_hidden.at[rows], far_grad_hidden.at[rows]).start()
        return carry

    def sent():
        wo_y().wait_send()
        for i in range(blocks):
            for p in range(pairs):
                ctx_copy(i, p).wait_send()
            out_copy(i).wait_send()
            grad_ctx_copy(i).wait_send()
            rows = slice(i * RB, (i + 1) * RB)
            results(i, output.at[rows], far_output.at[rows]).wait()
        if ring:
            for copy in (wo_x(), wo_z(), wo_xz(), wo_core(True), wo_core(False), wo_grad_copy(), vec_core, vec_low, vec_high):
                copy.wait_send()
            wo_grad_result().wait()
            for c in range(chunks):
                if c >= chunks - SLOTS:
                    core_copy(c).wait_send()
                first_copy(c).wait_send()
                second_copy(c).wait_send()
                third_copy(c).wait_send()
                if c not in WO_AT:
                    grad_result(c).wait()

    vec_out = results(2 * blocks, s.vec_all if ring else s.vec, far_vec)
    if ring:
        first_done(6)
        second_done(2, 4)
        core_done(*QKV_AT)
        vec_core.wait_recv()
        s.vec[core] = s.vec[core] + s.vec_half[...]
        vec_low.start()
        first_done(7)
        second_done(3, 5)
        third_done(1)
        first_done(8)
        second_done(6)
        third_done(4)
        lax.fori_loop(0, blocks, finish_out, 0)
        vec_low.wait_recv()
        s.vec[core, z_low_at] = s.vec[core, z_low_at] + s.vec_quarter[...]
        vec_high.start()
        first_done(9)
        third_done(0)
        second_done(7)
        third_done(2, 5)
        second_done(8)
        third_done(6)
        vec_high.wait_recv()
        own_vec[...] = own_vec[...] + s.vec_eighth[0]
        vec_y.start()
        first_done(10)
        second_done(9)
        third_done(7)
        wo_grad_copy().start()
        back_copy(2).start()
        back_copy(3).start()
        third_done(8)
        vec_y.wait()
        own_vec[0:24] = own_vec[0:24] + s.vec_eighth[1, 0:24]
        vec_x.start()
        first_done(11)
        second_done(10)
        third_done(9)
        first_done(12)
        second_done(11)
        third_done(3)
        wo_grad_done()
        third_done(10)
        second_done(12)
        third_done(11)
        vec_x.wait()
        s.vec_all[core, z_low_at, z_high_at] = own_vec[...] + s.vec_eighth[2]
        all_high.start()
        third_done(12)
        all_high.wait_recv()
        all_low.start()
        sent()
        all_low.wait_recv()
        all_core.start()
        all_core.wait_recv()
    else:
        back_copy(2).start()
        back_copy(3).start()
        vec_y.wait()
        s.vec[:, :, :, 0:24] = s.vec[:, :, :, 0:24] + s.vec_half[...]
        lax.fori_loop(0, blocks, finish_out, 0)
        sent()
    vec_out.start()
    lax.fori_loop(0, blocks, finish_hidden, 0)
    for i in range(blocks):
        rows = slice(i * RB, (i + 1) * RB)
        back_copy(i).wait_send()
        results(blocks + i, grad_hidden.at[rows], far_grad_hidden.at[rows]).wait()
    vec_out.wait()
    if ring:
        for copy in (all_high, all_low, all_core):
            copy.wait_send()


def scratch_of(ring, slots, width, local, units, table_rows, chunks):
    pairs = local // 128
    blocks = slots // RB
    halves = slots // RF
    vm, dma = pltpu.VMEM, pltpu.SemaphoreType.DMA
    shapes = dict(
        hidden=vm((slots, width), BF16),
        attn_in=vm((3, width, local), BF16),
        attn_out=vm((local, width), BF16),
        ffn_in=vm((width, units), BF16),
        ffn_out=vm((units, width), BF16),
        cotangent=vm((slots, width), BF16),
        output=vm((slots, width), BF16),
        grad_hidden=vm((slots, width), BF16),
        in_s=dma((15,)),
        out_dma=dma((2 * blocks + 1 + chunks,)),
        normed_t=vm((halves, width, RF), BF16),
        q=vm((pairs, slots, 128), BF16),
        k=vm((pairs, slots, 128), BF16),
        v=vm((pairs, slots, 128), BF16),
        table=vm((2 * slots, 128), BF16),
        probs=vm((pairs, blocks, 2 * RB, slots), BF16),
        ctx=vm((2 * pairs, slots, 128), BF16),
        ctx_send=vm((pairs, slots, 128), F32),
        ctx_recv=vm((pairs, slots, 128), F32),
        wo=vm((2 * local, width), BF16),
        wo_stage=vm((local // 8, width) if ring else (local, width), F32),
        wo_recv=vm((2, 2, 2, local // 8, width) if ring else (local, width), F32),
        middle=vm((slots, width), F32),
        normed2_t=vm((halves, width, RF), BF16),
        top_t=vm((halves, width, RF), BF16),
        active=vm((slots, units), BF16),
        grad_pre=vm((slots, units), BF16),
        gn1_send=vm((slots, width), F32),
        gn1_recv=vm((slots, width), F32),
        out_send=vm((slots, width), F32),
        out_recv=vm((slots, width), F32),
        grad_middle=vm((slots, width), F32),
        grad_att_t=vm((halves, width, RF), BF16),
        grad_ctx_own=vm((slots, local), F32),
        grad_ctx_send=vm((slots, local), F32),
        grad_ctx_recv=vm((slots, local), F32),
        grad_k=vm((pairs, slots, 128), F32),
        grad_v=vm((pairs, slots, 128), F32),
        grad_table=vm((2 * slots, 128), F32),
        attn_in_bias=vm((2, local), BF16),
        rel_table_t=vm((HD, table_rows), BF16),
        attn_out_bias=vm((width // 128, 128), BF16),
        norm1_gain=vm((width // 128, 128), BF16),
        norm1_bias=vm((width // 128, 128), BF16),
        norm2_gain=vm((width // 128, 128), BF16),
        norm2_bias=vm((width // 128, 128), BF16),
        ffn_in_bias16=vm((units // 128, 128), BF16),
        ffn_out_bias=vm((width // 128, 128), BF16),
        vec=vm((2, 2, 2, 32, 128), F32),
        vec_half=vm((2, 2, 32, 128) if ring else (2, 2, 2, 24, 128), F32),
        fib=vm((1, units), F32),
        fob=vm((1, width), F32),
        aob=vm((1, width), F32),
        n1=vm((2, width), F32),
        n2=vm((2, width), F32),
        ffn_in_bias=vm((1, units), F32),
        free=pltpu.SemaphoreType.REGULAR((SLOTS,)),
        wo_sem=dma((2, 8)),
        ctx_sem=dma((2, blocks * pairs)),
        grad_ctx_sem=dma((2, blocks)),
        gn1_sem=dma((2, blocks)),
        out_sem=dma((2, blocks)),
        vec_sem=dma((2, 8)),
    )
    if ring:
        shapes.update(
            g_own=vm((chunks, 2, 2, 2, 48, CW), F32),
            g_send=vm((SLOTS, 2, 2, 2, 48, CW), F32),
            core_recv=vm((SLOTS, 2, 2, 2, 48, CW), F32),
            first_recv=vm((chunks, 2, 2, 48, CW), F32),
            late_recv=vm((chunks, 3, 48, CW), F32),
            grads=vm((chunks, 48, CW), F32),
            vec_quarter=vm((2, 32, 128), F32),
            vec_eighth=vm((3, 32, 128), F32),
            vec_all=vm((2, 2, 2, 32, 128), F32),
            wo_grad=vm((48, CW), F32),
            wo_grad_recv=vm((48, CW), F32),
            gc_sem=dma((2, chunks)),
            g1_sem=dma((2, chunks)),
            g2_sem=dma((2, chunks)),
            g3_sem=dma((2, chunks)),
            wo_grad_sem=dma((2, 1)),
        )
    return shapes


def place(*refs):
    ins, outs, held, small, sems = refs[:7], refs[7:22], refs[22:29], refs[29:38], refs[38]
    bring = [pltpu.make_async_copy(far, near, sems.at[k]) for k, (far, near) in enumerate(zip(ins, held))]
    write = [
        pltpu.make_async_copy(near, far, sems.at[7 + k]) for k, (near, far) in enumerate(zip(held[:6] + small, outs))
    ]
    for copy in bring[::-1]:
        copy.start()
    bring[6].wait()
    vec = held[6]
    g_attn_in_bias, g_rel_t = small[:2]
    for ref, at in zip(small[2:], (V_AOB, V_N1G, V_N1B, V_N2G, V_N2B, V_FIB, V_FOB)):
        ref[...] = jnp.concatenate(vec_rows(vec, at, ref.shape[0]), axis=0)
    count = g_attn_in_bias.shape[1] // 128
    for k in range(2):
        g_attn_in_bias[k : k + 1, :] = jnp.concatenate(vec_rows(vec, V_AIB + k * count, count), axis=1)
    reach = g_rel_t.shape[1] // 2
    turned = jnp.concatenate(vec_rows(vec, V_REL, reach), axis=0).T
    g_rel_t[...] = jnp.concatenate([turned[:HD], turned[HD:]], axis=1)
    for copy in write[6:]:
        copy.start()
    for k in range(6):
        bring[k].wait()
        write[k].start()
    for copy in write:
        copy.wait()


def on_device(
    ring,
    hidden, lengths, attn_in, attn_in_bias, rel_table, attn_out, attn_out_bias,
    norm1_gain, norm1_bias, norm2_gain, norm2_bias,
    ffn_in, ffn_in_bias, ffn_out, ffn_out_bias, cotangent,
):
    slots, width = hidden.shape
    local = attn_out.shape[0]
    units = ffn_in.shape[1]
    table_rows = rel_table.shape[0]
    chunks = 2 * units // CW + 5
    rows = width // 16
    shape = jax.ShapeDtypeStruct
    shapes = scratch_of(ring, slots, width, local, units, table_rows, chunks)
    names = tuple(shapes)
    outs = [
        shape((slots, width), BF16), shape((slots, width), BF16), shape((3, rows, local), F32), shape((rows, local), F32),
        shape((rows, units), F32), shape((rows, units), F32), shape((2, 2, 2, 32, 128), F32),
    ]
    far = pl.BlockSpec(memory_space=pl.ANY)
    near = pl.BlockSpec(memory_space=pltpu.VMEM)
    out_specs = [far] * 7
    if not ring:
        names = (FULL,) + names
        outs.append(shape((chunks, width, CW), F32))
        out_specs.append(near)

    def lanes(vector):
        return vector.reshape(vector.shape[0] // 128, 128)

    def unlanes(array):
        return array.reshape(array.shape[0] * 128)

    results = pl.pallas_call(
        partial(body, ring, names),
        out_shape=outs,
        in_specs=[pl.BlockSpec(memory_space=pltpu.SMEM)] + [far] * 15,
        out_specs=out_specs,
        scratch_shapes=list(shapes.values()),
        compiler_params=pltpu.CompilerParams(
            collective_id=0, has_side_effects=True, vmem_limit_bytes=64 * 1024 * 1024
        ),
    )(
        lengths, attn_in_bias, rel_table.T, lanes(attn_out_bias), lanes(norm1_gain), lanes(norm1_bias),
        lanes(norm2_gain), lanes(norm2_bias), lanes(ffn_in_bias), lanes(ffn_out_bias),
        hidden, attn_in, attn_out, ffn_in, ffn_out, cotangent,
    )
    if ring:
        vector = shape((width // 128, 128), F32)
        small = [
            shape((2, local), F32), shape((HD, table_rows), F32), vector, vector, vector, vector, vector,
            shape((units // 128, 128), F32), vector,
        ]
        placed = pl.pallas_call(
            place,
            out_shape=outs[:6] + small,
            in_specs=[far] * 7,
            out_specs=[far] * 15,
            scratch_shapes=[pltpu.VMEM(array.shape, array.dtype) for array in outs + small]
            + [pltpu.SemaphoreType.DMA((22,))],
        )(*results)
        (
            output, grad_hidden, g_attn_in, g_attn_out_t, g_ffn_in, g_ffn_out_t, g_attn_in_bias, g_rel_t,
            g_attn_out_bias, n1g, n1b, n2g, n2b, g_ffn_in_bias, g_ffn_out_bias,
        ) = placed
        return (
            output, grad_hidden, g_attn_in, g_attn_in_bias, g_rel_t.T, g_attn_out_t.T, unlanes(g_attn_out_bias),
            unlanes(n1g), unlanes(n1b), unlanes(n2g), unlanes(n2b),
            g_ffn_in, unlanes(g_ffn_in_bias), g_ffn_out_t.T, unlanes(g_ffn_out_bias),
        )
    output, grad_hidden, vec, full = results[0], results[1], results[6], results[7]

    def wide(which):
        return jnp.concatenate([full[c] for c in which], axis=1)

    def scatter(value, dim, axis="dp"):
        return lax.psum_scatter(value, axis, scatter_dimension=dim, tiled=True)

    g_ffn_out = scatter(wide(OUT_AT).T, 1)
    g_ffn_in = scatter(wide(IN_AT), 0)
    g_attn_out = scatter(scatter(full[WO_AT[0] : WO_AT[1] + 1], 0, "tensor")[0].T, 1)
    g_attn_in = scatter(full[QKV_AT[0] : QKV_AT[2] + 1], 1)
    vec = lax.psum(vec, "dp")

    def row(at, count=width):
        return unlanes(jnp.concatenate(vec_rows(vec, at, count // 128), axis=0))

    rel_pairs = jnp.concatenate(vec_rows(vec, V_REL, table_rows // 2), axis=0)
    grad_rel = jnp.concatenate([rel_pairs[:, :HD], rel_pairs[:, HD:]], axis=0)
    return (
        output, grad_hidden, g_attn_in,
        row(V_AIB, 2 * local).reshape(2, local), grad_rel, g_attn_out, row(V_AOB),
        row(V_N1G), row(V_N1B), row(V_N2G), row(V_N2B),
        g_ffn_in, row(V_FIB, units), g_ffn_out, row(V_FOB),
    )


def solution(mesh):
    ring = mesh.shape["dp"] == 16
    return jax.shard_map(
        partial(on_device, ring),
        mesh=mesh,
        in_specs=(
            P("dp", None), P("dp"), P(None, None, "tensor"), P(None, "tensor"), P(),
            P("tensor", None), P(), P(), P(), P(), P(),
            P(None, "tensor"), P("tensor"), P("tensor", None), P(), P("dp", None),
        ),
        out_specs=(
            P("dp", None), P("dp", None), P(None, "dp", "tensor"), P(None, "tensor"), P(),
            P("tensor", "dp"), P(), P(), P(), P(), P(),
            P("dp", "tensor"), P("tensor"), P("tensor", "dp"), P(),
        ),
        check_vma=False,
    )
```

```python
from functools import partial
from types import SimpleNamespace

import jax
import jax.numpy as jnp
from jax import lax
from jax.experimental import pallas as pl
from jax.experimental.pallas import tpu as pltpu
from jax.sharding import PartitionSpec as P

HD = 64
EPSILON = 1e-05
NEGATIVE = -1e30
SQRT_HALF = 0.7071067811865476
INV_SQRT_2PI = 0.3989422804014327
RB = 128
RF = 256
CW = 384
FULL = "g_full"
OUT_AT, IN_AT, WO_AT, QKV_AT = (0, 1, 2, 3), (4, 5, 8, 9), (6, 7), (10, 11, 12)
Z_FIRST = (0, 2, 3)
SLOTS = 4
MESH = pl.DeviceIdType.MESH
F32 = jnp.float32
BF16 = jnp.bfloat16


def mm(a, b):
    return jnp.dot(a, b, preferred_element_type=F32)


def mm_nt(a, b):
    return lax.dot_general(a, b, (((1,), (1,)), ((), ())), preferred_element_type=F32)


def mm_tn(a, b):
    return lax.dot_general(a, b, (((0,), (0,)), ((), ())), preferred_element_type=F32)


def norm_stats(value):
    mean = jnp.mean(value, axis=-1, keepdims=True)
    centred = value - mean
    scale = lax.rsqrt(jnp.mean(centred * centred, axis=-1, keepdims=True) + EPSILON)
    return centred * scale, scale


def norm_back(grad, unit, scale, gain):
    grad_unit = grad * gain
    inner = (
        grad_unit
        - jnp.mean(grad_unit, axis=-1, keepdims=True)
        - unit * jnp.mean(grad_unit * unit, axis=-1, keepdims=True)
    )
    return inner * scale


def col_sum(value):
    return jnp.sum(value, axis=0, keepdims=True)


def lanes_of(ref3, rows):
    return jnp.concatenate([ref3[p, rows, :] for p in range(ref3.shape[0])], axis=1)


V_N1G, V_N1B, V_AOB, V_N2G, V_N2B, V_REL, V_FOB, V_FIB, V_AIB = 0, 6, 12, 18, 24, 32, 192, 198, 210
YROWS, VROWS = 192, 216


def vec_place(row):
    part, at = (row // 24, row % 24) if row < YROWS else ((row - YROWS) // 3, 24 + (row - YROWS) % 3)
    return part // 4, part // 2 % 2, part % 2, at


def vec_rows(vec, first, count):
    found = []
    for row in range(first, first + count):
        a, b, c, at = vec_place(row)
        found.append(vec[a, b, c, at : at + 1, :])
    return found


def body(
    ring, names,
    lengths, far_attn_in_bias, far_rel_table_t, far_attn_out_bias, far_norm1_gain, far_norm1_bias, far_norm2_gain,
    far_norm2_bias, far_ffn_in_bias, far_ffn_out_bias, far_hidden, far_attn_in, far_attn_out, far_ffn_in, far_ffn_out, far_cotangent,
    far_output, far_grad_hidden, far_attn_in_grad, far_attn_out_grad, far_ffn_in_grad, far_ffn_out_grad, far_vec,
    *scratch,
):
    s = SimpleNamespace(**dict(zip(names, scratch)))

    def bring(at, near, far):
        copy = pltpu.make_async_copy(far, near, s.in_s.at[at])
        copy.start()
        return copy

    bring_attn_out = bring(0, s.attn_out, far_attn_out)
    bring_hidden = bring(1, s.hidden, far_hidden)
    bring_attn_in = bring(2, s.attn_in, far_attn_in)
    small = (
        (s.attn_in_bias, far_attn_in_bias), (s.rel_table_t, far_rel_table_t), (s.attn_out_bias, far_attn_out_bias),
        (s.norm1_gain, far_norm1_gain), (s.norm1_bias, far_norm1_bias), (s.norm2_gain, far_norm2_gain),
        (s.norm2_bias, far_norm2_bias), (s.ffn_in_bias16, far_ffn_in_bias), (s.ffn_out_bias, far_ffn_out_bias),
    )
    bring_small = [bring(6 + k, near, far) for k, (near, far) in enumerate(small)]
    hidden, attn_in, attn_out = s.hidden, s.attn_in, s.attn_out
    cotangent, ffn_in, ffn_out = s.cotangent, s.ffn_in, s.ffn_out
    output, grad_hidden = s.output, s.grad_hidden
    slots, width = hidden.shape
    local = attn_out.shape[0]
    pairs = local // 128
    units = ffn_in.shape[1]
    table_rows = s.rel_table_t.shape[1]
    reach = table_rows // 2
    blocks = slots // RB
    ext = slots + RB
    head_scale = HD ** (-0.5)

    dp = lax.axis_index("dp")
    ten = lax.axis_index("tensor")
    y_peer = (dp, 1 - ten)
    if ring:
        core = lax.rem(dp, 2)
        x_at = lax.rem(lax.div(dp, 2), 2)
        z_low_at = lax.rem(lax.div(dp, 4), 2)
        z_high_at = lax.div(dp, 8)
        core_peer = (dp + 1 - 2 * core, ten)
        x_peer = (dp + 2 - 4 * x_at, ten)
        z_low = (dp + 4 - 8 * z_low_at, ten)
        z_high = (dp + 8 - 16 * z_high_at, ten)
        greet = [y_peer, core_peer, x_peer, z_low, z_high]
    else:
        greet = [y_peer]

    barrier = pltpu.get_barrier_semaphore()
    for peer in greet:
        pl.semaphore_signal(barrier, inc=1, device_id=peer, device_id_type=MESH)

    def remote(src, dst, sems, at, peer):
        return pltpu.make_async_remote_copy(
            src_ref=src, dst_ref=dst, send_sem=sems.at[0, at], recv_sem=sems.at[1, at],
            device_id=peer, device_id_type=MESH,
        )

    bring_attn_out.wait()
    if ring:
        piece = local // 8
        mine = (2 * z_low_at + x_at) * 2 + core
        s.wo_stage[...] = attn_out[pl.ds(pl.multiple_of(mine * piece, 16), piece), :].astype(F32)

        def wo_y():
            return remote(s.wo_stage, s.wo_recv.at[z_low_at, x_at, core], s.wo_sem, 0, y_peer)

        def wo_pass(part, at, peer):
            return remote(part, part, s.wo_sem, at, peer)

        def wo_x():
            return wo_pass(s.wo_recv.at[z_low_at, x_at, core], 1, x_peer)

        def wo_z():
            return wo_pass(s.wo_recv.at[z_low_at, x_at, core], 2, z_low)

        def wo_xz():
            return wo_pass(s.wo_recv.at[z_low_at, 1 - x_at, core], 3, z_low)

        def wo_core(near):
            return wo_pass(s.wo_recv.at[z_low_at if near else 1 - z_low_at, :, core], 4 if near else 5, core_peer)
    else:
        s.wo_stage[...] = attn_out[...].astype(F32)

        def wo_y():
            return remote(s.wo_stage, s.wo_recv, s.wo_sem, 0, y_peer)

    pl.semaphore_wait(barrier, len(greet))
    wo_y().start()

    def flat(ref):
        value = ref[...].astype(F32)
        return jnp.concatenate([value[j : j + 1] for j in range(value.shape[0])], axis=1)

    for copy in bring_small:
        copy.wait()
    bias_q = s.attn_in_bias[0:1, :].astype(F32)
    bias_v = s.attn_in_bias[1:2, :].astype(F32)
    gain1, offset1 = flat(s.norm1_gain), flat(s.norm1_bias)
    gain2, offset2 = flat(s.norm2_gain), flat(s.norm2_bias)
    out_bias1, out_bias2 = flat(s.attn_out_bias), flat(s.ffn_out_bias)
    s.ffn_in_bias[...] = flat(s.ffn_in_bias16)
    seq_len = lengths[0]

    ext_rows = 2 * slots
    distance = slots - 1 - lax.broadcasted_iota(jnp.int32, (ext_rows, table_rows), 0)
    bucket = jnp.clip(distance, -reach, reach - 1) + reach
    pick = (bucket == lax.broadcasted_iota(jnp.int32, (ext_rows, table_rows), 1)).astype(BF16)
    rel_t = s.rel_table_t[...]
    s.table[...] = mm_nt(pick, jnp.concatenate([rel_t, rel_t], axis=0)).astype(BF16)

    def project(i, carry):
        rows = pl.ds(pl.multiple_of(i * RF, RF), RF)
        unit, unused = norm_stats(hidden[rows, :].astype(F32))
        normed = (unit * gain1 + offset1).astype(BF16)
        s.normed_t[i] = normed.T
        q = ((mm(normed, attn_in[0]) + bias_q) * head_scale).astype(BF16)
        k = mm(normed, attn_in[1]).astype(BF16)
        v = (mm(normed, attn_in[2]) + bias_v).astype(BF16)
        for p in range(pairs):
            s.q[p, rows, :] = q[:, p * 128 : (p + 1) * 128]
            s.k[p, rows, :] = k[:, p * 128 : (p + 1) * 128]
            s.v[p, rows, :] = v[:, p * 128 : (p + 1) * 128]
        return carry

    bring_hidden.wait()
    bring_attn_in.wait()
    bring_cotangent = bring(3, s.cotangent, far_cotangent)
    bring_ffn_in = bring(4, s.ffn_in, far_ffn_in)
    bring_ffn_out = bring(5, s.ffn_out, far_ffn_out)
    lax.fori_loop(0, slots // RF, project, 0)

    low_lanes = lax.broadcasted_iota(jnp.int32, (RB, 128), 1) < HD
    key_ok = lax.broadcasted_iota(jnp.int32, (1, slots), 1) < seq_len

    def stack(both):
        zero = jnp.zeros_like(both)
        return jnp.concatenate([jnp.where(low_lanes, both, zero), jnp.where(low_lanes, zero, both)], axis=0)

    def unstack(tall):
        return jnp.where(low_lanes, tall[:RB], tall[RB:])

    def table_rows_of(i):
        return pl.ds(pl.multiple_of(slots - RB - i * RB, RB), ext)

    def ctx_copy(i, p):
        rows = pl.ds(pl.multiple_of(i * RB, RB), RB)
        return remote(s.ctx_send.at[p, rows], s.ctx_recv.at[p, rows], s.ctx_sem, i * pairs + p, y_peer)

    def attend(i):
        rows = pl.ds(pl.multiple_of(i * RB, RB), RB)

        def pair_step(p, carry):
            qs = stack(s.q[p, rows, :])
            spread = mm_nt(qs, s.table[table_rows_of(i), :])
            shift = ext - RB + 1
            bias = jnp.concatenate(
                [
                    pltpu.roll(spread[:RB], shift, 1, stride=1, stride_axis=0)[:, :slots],
                    pltpu.roll(spread[RB:], shift, 1, stride=1, stride_axis=0)[:, :slots],
                ],
                axis=0,
            )
            scores = jnp.where(key_ok, mm_nt(qs, s.k[p]) + bias, NEGATIVE)
            expon = jnp.exp(scores - jnp.max(scores, axis=-1, keepdims=True))
            shares = (expon * (1.0 / jnp.sum(expon, axis=-1, keepdims=True))).astype(BF16)
            s.probs[p, i] = shares
            context = unstack(mm(shares, s.v[p])).astype(BF16)
            s.ctx[ten * pairs + p, rows, :] = context
            s.ctx_send[p, rows, :] = context.astype(F32)
            ctx_copy(i, p).start()
            return carry

        lax.fori_loop(0, pairs, pair_step, 0)

    half = pl.ds(pl.multiple_of(ten * local, 128), local)
    far_half = pl.ds(pl.multiple_of((1 - ten) * local, 128), local)
    s.wo[half, :] = attn_out[...]
    attend(0)
    if ring:
        wo_y().wait_recv()
        wo_x().start()
        wo_z().start()
    attend(1)
    if ring:
        wo_x().wait_recv()
        wo_xz().start()
        wo_core(True).start()
    attend(2)
    attend(3)

    if ring:
        wo_z().wait_recv()
        wo_xz().wait_recv()
        wo_core(False).start()
        wo_core(True).wait_recv()
        wo_core(False).wait_recv()
        s.wo[far_half, :] = s.wo_recv[...].reshape(local, width).astype(BF16)
    else:
        wo_y().wait_recv()
        s.wo[far_half, :] = s.wo_recv[...].astype(BF16)
    bring_cotangent.wait()
    bring_ffn_in.wait()
    bring_ffn_out.wait()

    def valid_rows(start, count):
        return (lax.broadcasted_iota(jnp.int32, (count, 1), 0) + start < seq_len).astype(F32)

    def grad_ctx_copy(i):
        rows = pl.ds(i * RB, RB)
        return remote(s.grad_ctx_send.at[rows], s.grad_ctx_recv.at[rows], s.grad_ctx_sem, i, y_peer)

    def out_copy(i):
        rows = pl.ds(pl.multiple_of(i * RB, RB), RB)
        return remote(s.out_send.at[rows], s.out_recv.at[rows], s.out_sem, i, y_peer)

    s.vec[...] = jnp.zeros_like(s.vec)
    s.fib[...] = jnp.zeros_like(s.fib)
    s.fob[...] = jnp.zeros_like(s.fob)
    s.aob[...] = jnp.zeros_like(s.aob)
    s.n1[...] = jnp.zeros_like(s.n1)
    s.n2[...] = jnp.zeros_like(s.n2)

    step_units = 512

    def feed(b):
        start = b * RF
        rows = slice(start, start + RF)
        for j in range(RF // RB):
            for p in range(pairs):
                ctx_copy(b * (RF // RB) + j, p).wait_recv()
        for p in range(pairs):
            s.ctx[(1 - ten) * pairs + p, rows, :] = s.ctx_recv[p, rows, :].astype(BF16)
        attended = mm(lanes_of(s.ctx, rows), s.wo[...]) + out_bias1
        middle = hidden[rows, :].astype(F32) + attended
        s.middle[rows, :] = middle
        unit, scale = norm_stats(middle)
        normed = (unit * gain2 + offset2).astype(BF16)
        s.normed2_t[b] = normed.T
        top = cotangent[rows, :].astype(F32) * valid_rows(start, RF)
        s.fob[...] += col_sum(top)
        half_top = 0.5 * top
        top = top.astype(BF16)
        s.top_t[b] = top.T
        for c in range(units // step_units):
            cols = slice(c * step_units, (c + 1) * step_units)
            pre = mm(normed, ffn_in[:, cols]) + s.ffn_in_bias[:, cols]
            share = 0.5 + 0.5 * lax.erf(pre * SQRT_HALF)
            active = (pre * share).astype(BF16)
            s.active[rows, cols] = active
            slope = share + pre * (jnp.exp(-0.5 * pre * pre) * INV_SQRT_2PI)
            grad_pre = (mm_nt(top, ffn_out[cols, :]) * slope).astype(BF16)
            s.grad_pre[rows, cols] = grad_pre
            s.fib[:, cols] += col_sum(grad_pre.astype(F32))
            back = mm_nt(grad_pre, ffn_in[:, cols])
            onward = mm(active, ffn_out[cols, :])
            if c == 0:
                s.gn1_send[rows, :] = back
                s.out_send[rows, :] = onward
            else:
                s.gn1_send[rows, :] += back
                s.out_send[rows, :] += onward
            if b == 1:
                for chunk in range(per):
                    if c * step_units < (chunk + 1) * CW <= (c + 1) * step_units:
                        keep(out_grad(chunk, 1), chunk, True)
                if c > 0:
                    core_done(c - 1)
        back = s.gn1_send[rows, :]
        s.n2[0:1, :] += col_sum(back * unit)
        s.n2[1:2, :] += col_sum(back)
        grad_middle = half_top + norm_back(back, unit, scale, gain2)
        s.grad_middle[rows, :] = grad_middle
        grad_attended = grad_middle.astype(BF16)
        s.grad_ctx_send[rows, :] = mm_nt(grad_attended, s.wo[far_half, :])
        for j in range(RF // RB):
            grad_ctx_copy(b * (RF // RB) + j).start()
        s.grad_ctx_own[rows, :] = mm_nt(grad_attended, attn_out[...])
        s.aob[...] += col_sum(grad_attended.astype(F32))
        s.grad_att_t[b] = grad_attended.T

    feed(0)

    def grad_chunk(left_t, right):
        total = mm(left_t[0], right[0:RF])
        for b in range(1, slots // RF):
            total += mm(left_t[b], right[b * RF : (b + 1) * RF])
        return total

    per = units // CW
    chunks = 2 * per + 5

    def hold(total, chunk, begun=False):
        if not ring:
            s.g_full[chunk] = s.g_full[chunk] + total if begun else total
            return
        slot = chunk % SLOTS
        parts = total.reshape(8, 2, 48, CW)
        even, odd = parts[:, 0], parts[:, 1]
        near = jnp.where(core == 0, even, odd).reshape(2, 2, 2, 48, CW)
        far = jnp.where(core == 0, odd, even).reshape(2, 2, 2, 48, CW)
        s.g_own[chunk] = s.g_own[chunk] + near if begun else near
        s.g_send[slot] = s.g_send[slot] + far if begun else far

    def keep(total, chunk, begun=False):
        if ring and chunk >= SLOTS:
            core_copy(chunk - SLOTS).wait_send()
            pl.semaphore_wait(s.free.at[chunk % SLOTS], 1)
        hold(total, chunk, begun)
        if ring:
            core_copy(chunk).start()

    def core_copy(chunk):
        slot = chunk % SLOTS
        return remote(s.g_send.at[slot], s.core_recv.at[slot], s.gc_sem, chunk, core_peer)

    def first_copy(chunk):
        own = s.g_own.at[chunk]
        if chunk in Z_FIRST:
            return remote(own.at[:, 1 - z_low_at], s.first_recv.at[chunk], s.g1_sem, chunk, z_low)
        return remote(own.at[:, :, 1 - x_at], s.first_recv.at[chunk], s.g1_sem, chunk, x_peer)

    def second_copy(chunk):
        own = s.g_own.at[chunk]
        into = s.late_recv.at[chunk, 0:2]
        if chunk in Z_FIRST:
            return remote(own.at[1 - z_high_at, z_low_at], into, s.g2_sem, chunk, z_high)
        return remote(own.at[:, 1 - z_low_at, x_at], into, s.g2_sem, chunk, z_low)

    def third_copy(chunk):
        own = s.g_own.at[chunk]
        into = s.late_recv.at[chunk, 2]
        if chunk in Z_FIRST:
            return remote(own.at[z_high_at, z_low_at, 1 - x_at], into, s.g3_sem, chunk, x_peer)
        return remote(own.at[1 - z_high_at, z_low_at, x_at], into, s.g3_sem, chunk, z_high)

    def core_done(*which):
        for chunk in which if ring else ():
            core_copy(chunk).wait_recv()
            s.g_own[chunk] = s.g_own[chunk] + s.core_recv[chunk % SLOTS]
            if chunk + SLOTS < chunks:
                pl.semaphore_signal(s.free.at[chunk % SLOTS], inc=1, device_id=core_peer, device_id_type=MESH)
            first_copy(chunk).start()

    def first_done(*which):
        for chunk in which if ring else ():
            first_copy(chunk).wait_recv()
            if chunk in Z_FIRST:
                s.g_own[chunk, :, z_low_at] = s.g_own[chunk, :, z_low_at] + s.first_recv[chunk]
            else:
                s.g_own[chunk, :, :, x_at] = s.g_own[chunk, :, :, x_at] + s.first_recv[chunk]
            second_copy(chunk).start()

    def second_done(*which):
        for chunk in which if ring else ():
            second_copy(chunk).wait_recv()
            if chunk in Z_FIRST:
                s.g_own[chunk, z_high_at, z_low_at] = s.g_own[chunk, z_high_at, z_low_at] + s.late_recv[chunk, 0:2]
            else:
                s.g_own[chunk, :, z_low_at, x_at] = s.g_own[chunk, :, z_low_at, x_at] + s.late_recv[chunk, 0:2]
            third_copy(chunk).start()

    def results(at, near, far):
        return pltpu.make_async_copy(near, far, s.out_dma.at[at])

    def grad_result(chunk):
        if chunk in OUT_AT:
            c = OUT_AT.index(chunk)
            far = far_ffn_out_grad.at[:, c * CW : (c + 1) * CW]
        elif chunk in IN_AT:
            c = IN_AT.index(chunk)
            far = far_ffn_in_grad.at[:, c * CW : (c + 1) * CW]
        else:
            far = far_attn_in_grad.at[QKV_AT.index(chunk)]
        return results(2 * blocks + 1 + chunk, s.grads.at[chunk], far)

    def third_done(*which):
        for chunk in which if ring else ():
            third_copy(chunk).wait_recv()
            s.grads[chunk] = s.g_own[chunk, z_high_at, z_low_at, x_at] + s.late_recv[chunk, 2]
            if chunk not in WO_AT:
                grad_result(chunk).start()

    def wo_grad_copy():
        return remote(s.grads.at[WO_AT[0] + 1 - ten], s.wo_grad_recv, s.wo_grad_sem, 0, y_peer)

    def wo_grad_done():
        wo_grad_copy().wait_recv()
        s.wo_grad[...] = s.grads[WO_AT[0] + ten] + s.wo_grad_recv[...]
        wo_grad_result().start()

    def wo_grad_result():
        return results(2 * blocks + 1 + WO_AT[0], s.wo_grad, far_attn_out_grad)

    def out_grad(c, b):
        return mm(s.top_t[b], s.active[b * RF : (b + 1) * RF, c * CW : (c + 1) * CW])

    def keep_in(c):
        keep(grad_chunk(s.normed2_t, s.grad_pre.at[:, c * CW : (c + 1) * CW]), IN_AT[c])

    def keep_wo(h):
        context = jnp.concatenate([s.ctx[h * pairs + p] for p in range(pairs)], axis=1)
        total = grad_chunk(s.grad_att_t, context)
        keep(total, WO_AT[h])

    for c in range(per):
        hold(out_grad(c, 0), c)
    feed(1)
    for i in range(blocks):
        out_copy(i).start()
    for c in range(2):
        keep_in(c)
        core_done(2 + c)
    for h in range(2):
        keep_wo(h)
        core_done(4 + h)
    for c in range(2):
        keep_in(2 + c)
        core_done(6 + c)

    s.grad_k[...] = jnp.zeros_like(s.grad_k)
    s.grad_v[...] = jnp.zeros_like(s.grad_v)
    s.grad_table[...] = jnp.zeros_like(s.grad_table)
    flip_row = lax.broadcasted_iota(jnp.int32, (2 * RB, 2 * RB), 0)
    flip_col = lax.broadcasted_iota(jnp.int32, (2 * RB, 2 * RB), 1)
    same_half = (flip_row < RB) == (flip_col < RB)
    local_row = lax.rem(flip_row, RB)
    local_col = lax.rem(flip_col, RB)
    flip = (same_half & (local_row + local_col == RB - 1)).astype(BF16)

    def attend_back(i):
        rows = pl.ds(i * RB, RB)
        grad_ctx_copy(i).wait_recv()

        def pair_step(p, carry):
            qs = stack(s.q[p, rows, :])
            cols = pl.ds(pl.multiple_of(p * 128, 128), 128)
            gs = stack((s.grad_ctx_own[rows, cols] + s.grad_ctx_recv[rows, cols]).astype(BF16))
            low = s.probs[p, i]
            s.grad_v[p] += mm_tn(low, gs)
            shares = low.astype(F32)
            grad_shares = mm_nt(gs, s.v[p])
            inner = jnp.sum(grad_shares * shares, axis=-1, keepdims=True)
            grad_scores = (shares * (grad_shares - inner)).astype(BF16)
            s.grad_k[p] += mm_tn(grad_scores, qs)
            grad_q = mm(grad_scores, s.k[p])
            flipped = mm(flip, grad_scores)
            wide = jnp.concatenate([flipped, jnp.zeros((2 * RB, RB), F32)], axis=1)
            spread = jnp.concatenate(
                [
                    pltpu.roll(wide[:RB], 0, 1, stride=1, stride_axis=0),
                    pltpu.roll(wide[RB:], 0, 1, stride=1, stride_axis=0),
                ],
                axis=0,
            ).astype(BF16)
            q_flipped = mm(flip, qs).astype(BF16)
            s.grad_table[table_rows_of(i), :] += mm_tn(spread, q_flipped)
            turned = mm(spread, s.table[table_rows_of(i), :])
            high = turned.astype(BF16)
            rest = (turned - high.astype(F32)).astype(BF16)
            grad_q = unstack(grad_q + (mm(flip, high) + mm(flip, rest))).astype(BF16)
            s.grad_pre[rows, cols] = (grad_q.astype(F32) * head_scale).astype(BF16)
            return carry

        lax.fori_loop(0, pairs, pair_step, 0)

    attend_back(0)
    core_done(8, 9)
    first_done(0, 1)
    attend_back(1)
    first_done(2, 4)
    attend_back(2)
    first_done(3, 5)
    attend_back(3)
    second_done(0, 1)

    for p in range(pairs):
        at = local + p * 128
        s.grad_pre[:, at : at + 128] = s.grad_k[p].astype(BF16)
        at += local
        s.grad_pre[:, at : at + 128] = s.grad_v[p].astype(BF16)
    def back_copy(i):
        rows = pl.ds(pl.multiple_of(i * RB, RB), RB)
        return remote(s.gn1_send.at[rows], s.gn1_recv.at[rows], s.gn1_sem, i, y_peer)

    def project_back(b, carry):
        start = pl.multiple_of(b * RF, RF)
        rows = pl.ds(start, RF)
        total = (
            mm_nt(s.grad_pre[rows, 0:local], attn_in[0])
            + mm_nt(s.grad_pre[rows, local : 2 * local], attn_in[1])
            + mm_nt(s.grad_pre[rows, 2 * local : 3 * local], attn_in[2])
        )
        unit, scale = norm_stats(hidden[rows, :].astype(F32))
        s.gn1_send[rows, :] = norm_back(total, unit, scale, gain1) + s.grad_middle[rows, :]
        s.n1[0:1, :] += col_sum(total * unit)
        s.n1[1:2, :] += col_sum(total)
        return carry

    lax.fori_loop(0, slots // RF, project_back, 0)

    def put(at, row):
        for j in range(row.shape[1] // 128):
            a, b, c, i = vec_place(at + j)
            s.vec[a, b, c, i : i + 1, :] = row[:, j * 128 : (j + 1) * 128]

    put(V_N1G, s.n1[0:1, :])
    put(V_N1B, s.n1[1:2, :])
    put(V_N2G, s.n2[0:1, :])
    put(V_N2B, s.n2[1:2, :])
    put(V_AOB, s.aob[...])
    put(V_FOB, s.fob[...])
    put(V_FIB, s.fib[...])
    put(V_AIB, col_sum(s.grad_pre[:, 0:local].astype(F32)))
    put(V_AIB + pairs, col_sum(s.grad_pre[:, 2 * local : 3 * local].astype(F32)))
    grad_rel = None
    rest = s.grad_table[...]
    for part in range(3):
        piece16 = rest.astype(BF16)
        term = mm_tn(pick, piece16)
        grad_rel = term if part == 0 else grad_rel + term
        rest = rest - piece16.astype(F32)
    grad_rel = grad_rel + pltpu.roll(grad_rel, HD, 1)
    fold = lax.broadcasted_iota(jnp.int32, (reach, 128), 1) < HD
    packed = jnp.where(fold, grad_rel[:reach], grad_rel[reach:])
    done = 0
    while done < reach:
        a, b, c, at = vec_place(V_REL + done)
        count = min(24 - at, reach - done)
        s.vec[a, b, c, at : at + count, :] = packed[done : done + count]
        done += count

    def vec_send(src, dst, at, peer):
        return remote(src, dst, s.vec_sem, at, peer)

    if ring:
        own_vec = s.vec.at[core, z_low_at, z_high_at]
        vec_core = vec_send(s.vec.at[1 - core], s.vec_half, 0, core_peer)
        vec_low = vec_send(s.vec.at[core, 1 - z_low_at], s.vec_quarter, 1, z_low)
        vec_high = vec_send(s.vec.at[core, z_low_at, 1 - z_high_at], s.vec_eighth, 2, z_high)
        vec_y = vec_send(s.vec.at[core, :, :, 0:24], s.vec_y_recv, 3, y_peer)
        vec_x = vec_send(s.vec.at[core], s.vec_x_recv, 4, x_peer)
        all_high, all_low, all_core = (
            vec_send(part, part, 5 + k, peer)
            for k, (part, peer) in enumerate(
                (
                    (s.vec_all.at[core, z_low_at, z_high_at], z_high),
                    (s.vec_all.at[core, z_low_at], z_low),
                    (s.vec_all.at[core], core_peer),
                )
            )
        )
        vec_core.start()
    else:
        vec_y = vec_send(s.vec.at[:, :, :, 0:24], s.vec_half, 0, y_peer)
        vec_y.start()
    for i in range(blocks - 2):
        back_copy(i).start()

    for c in range(3):
        keep(grad_chunk(s.normed_t, s.grad_pre.at[:, c * local : (c + 1) * local]), QKV_AT[c])

    def finish_out(i, carry):
        start = pl.multiple_of(i * RB, RB)
        rows = pl.ds(start, RB)
        out_copy(i).wait_recv()
        branch = s.out_send[rows, :] + s.out_recv[rows, :]
        total = s.middle[rows, :] + (branch + out_bias2)
        output[rows, :] = (total * valid_rows(start, RB)).astype(BF16)
        results(i, output.at[rows], far_output.at[rows]).start()
        return carry

    def finish_hidden(i, carry):
        rows = pl.ds(pl.multiple_of(i * RB, RB), RB)
        back_copy(i).wait_recv()
        grad_hidden[rows, :] = (s.gn1_send[rows, :] + s.gn1_recv[rows, :]).astype(BF16)
        results(blocks + i, grad_hidden.at[rows], far_grad_hidden.at[rows]).start()
        return carry

    def sent():
        wo_y().wait_send()
        for i in range(blocks):
            for p in range(pairs):
                ctx_copy(i, p).wait_send()
            out_copy(i).wait_send()
            grad_ctx_copy(i).wait_send()
            rows = slice(i * RB, (i + 1) * RB)
            results(i, output.at[rows], far_output.at[rows]).wait()
        if ring:
            for copy in (wo_x(), wo_z(), wo_xz(), wo_core(True), wo_core(False), vec_core, vec_low):
                copy.wait_send()
            for c in range(chunks):
                if c >= chunks - SLOTS:
                    core_copy(c).wait_send()
                first_copy(c).wait_send()

    def sent_late(*which):
        for c in which:
            second_copy(c).wait_send()
            third_copy(c).wait_send()
            if c not in WO_AT:
                grad_result(c).wait()

    vec_out = results(2 * blocks, s.vec_all if ring else s.vec, far_vec)
    if ring:
        first_done(6)
        second_done(2, 4)
        vec_core.wait_recv()
        s.vec[core] = s.vec[core] + s.vec_half[...]
        vec_x.start()
        core_done(*QKV_AT)
        first_done(7)
        second_done(3, 5)
        third_done(1)
        first_done(8)
        second_done(6)
        third_done(4)
        lax.fori_loop(0, blocks, finish_out, 0)
        first_done(9)
        vec_x.wait()
        s.vec[core] = s.vec[core] + s.vec_x_recv[...]
        vec_y.start()
        back_copy(blocks - 2).start()
        third_done(0)
        second_done(7)
        third_done(2, 5)
        second_done(8)
        third_done(6)
        first_done(10)
        second_done(9)
        third_done(7)
        wo_grad_copy().start()
        back_copy(blocks - 1).start()
        vec_y.wait()
        s.vec[core, :, :, 0:24] = s.vec[core, :, :, 0:24] + s.vec_y_recv[...]
        vec_low.start()
        third_done(8)
        first_done(11)
        second_done(10)
        third_done(9)
        vec_low.wait_recv()
        s.vec[core, z_low_at] = s.vec[core, z_low_at] + s.vec_quarter[...]
        vec_high.start()
        first_done(12)
        finish_hidden(0, 0)
        finish_hidden(1, 0)
        second_done(11)
        third_done(3)
        vec_high.wait_recv()
        s.vec_all[core, z_low_at, z_high_at] = own_vec[...] + s.vec_eighth[...]
        all_high.start()
        wo_grad_done()
        third_done(10)
        second_done(12)
        third_done(11)
        sent()
        all_high.wait_recv()
        all_low.start()
        sent_late(*range(chunks - 1))
        third_done(12)
        all_low.wait_recv()
        all_core.start()
        wo_grad_copy().wait_send()
        vec_high.wait_send()
        finish_hidden(2, 0)
        all_core.wait_recv()
        vec_out.start()
        finish_hidden(3, 0)
        sent_late(12)
        wo_grad_result().wait()
    else:
        back_copy(blocks - 2).start()
        back_copy(blocks - 1).start()
        vec_y.wait()
        s.vec[:, :, :, 0:24] = s.vec[:, :, :, 0:24] + s.vec_half[...]
        lax.fori_loop(0, blocks, finish_out, 0)
        vec_out.start()
        sent()
        lax.fori_loop(0, blocks, finish_hidden, 0)
    for i in range(blocks):
        rows = slice(i * RB, (i + 1) * RB)
        back_copy(i).wait_send()
        results(blocks + i, grad_hidden.at[rows], far_grad_hidden.at[rows]).wait()
    vec_out.wait()
    if ring:
        for copy in (all_high, all_low, all_core):
            copy.wait_send()


def scratch_of(ring, slots, width, local, units, table_rows, chunks):
    pairs = local // 128
    blocks = slots // RB
    halves = slots // RF
    vm, dma = pltpu.VMEM, pltpu.SemaphoreType.DMA
    shapes = dict(
        hidden=vm((slots, width), BF16),
        attn_in=vm((3, width, local), BF16),
        attn_out=vm((local, width), BF16),
        ffn_in=vm((width, units), BF16),
        ffn_out=vm((units, width), BF16),
        cotangent=vm((slots, width), BF16),
        output=vm((slots, width), BF16),
        grad_hidden=vm((slots, width), BF16),
        in_s=dma((15,)),
        out_dma=dma((2 * blocks + 1 + chunks,)),
        normed_t=vm((halves, width, RF), BF16),
        q=vm((pairs, slots, 128), BF16),
        k=vm((pairs, slots, 128), BF16),
        v=vm((pairs, slots, 128), BF16),
        table=vm((2 * slots, 128), BF16),
        probs=vm((pairs, blocks, 2 * RB, slots), BF16),
        ctx=vm((2 * pairs, slots, 128), BF16),
        ctx_send=vm((pairs, slots, 128), F32),
        ctx_recv=vm((pairs, slots, 128), F32),
        wo=vm((2 * local, width), BF16),
        wo_stage=vm((local // 8, width) if ring else (local, width), F32),
        wo_recv=vm((2, 2, 2, local // 8, width) if ring else (local, width), F32),
        middle=vm((slots, width), F32),
        normed2_t=vm((halves, width, RF), BF16),
        top_t=vm((halves, width, RF), BF16),
        active=vm((slots, units), BF16),
        grad_pre=vm((slots, units), BF16),
        gn1_send=vm((slots, width), F32),
        gn1_recv=vm((slots, width), F32),
        out_send=vm((slots, width), F32),
        out_recv=vm((slots, width), F32),
        grad_middle=vm((slots, width), F32),
        grad_att_t=vm((halves, width, RF), BF16),
        grad_ctx_own=vm((slots, local), F32),
        grad_ctx_send=vm((slots, local), F32),
        grad_ctx_recv=vm((slots, local), F32),
        grad_k=vm((pairs, slots, 128), F32),
        grad_v=vm((pairs, slots, 128), F32),
        grad_table=vm((2 * slots, 128), F32),
        attn_in_bias=vm((2, local), BF16),
        rel_table_t=vm((HD, table_rows), BF16),
        attn_out_bias=vm((width // 128, 128), BF16),
        norm1_gain=vm((width // 128, 128), BF16),
        norm1_bias=vm((width // 128, 128), BF16),
        norm2_gain=vm((width // 128, 128), BF16),
        norm2_bias=vm((width // 128, 128), BF16),
        ffn_in_bias16=vm((units // 128, 128), BF16),
        ffn_out_bias=vm((width // 128, 128), BF16),
        vec=vm((2, 2, 2, 32, 128), F32),
        vec_half=vm((2, 2, 32, 128) if ring else (2, 2, 2, 24, 128), F32),
        fib=vm((1, units), F32),
        fob=vm((1, width), F32),
        aob=vm((1, width), F32),
        n1=vm((2, width), F32),
        n2=vm((2, width), F32),
        ffn_in_bias=vm((1, units), F32),
        free=pltpu.SemaphoreType.REGULAR((SLOTS,)),
        wo_sem=dma((2, 8)),
        ctx_sem=dma((2, blocks * pairs)),
        grad_ctx_sem=dma((2, blocks)),
        gn1_sem=dma((2, blocks)),
        out_sem=dma((2, blocks)),
        vec_sem=dma((2, 8)),
    )
    if ring:
        shapes.update(
            g_own=vm((chunks, 2, 2, 2, 48, CW), F32),
            g_send=vm((SLOTS, 2, 2, 2, 48, CW), F32),
            core_recv=vm((SLOTS, 2, 2, 2, 48, CW), F32),
            first_recv=vm((chunks, 2, 2, 48, CW), F32),
            late_recv=vm((chunks, 3, 48, CW), F32),
            grads=vm((chunks, 48, CW), F32),
            vec_quarter=vm((2, 32, 128), F32),
            vec_x_recv=vm((2, 2, 32, 128), F32),
            vec_y_recv=vm((2, 2, 24, 128), F32),
            vec_eighth=vm((32, 128), F32),
            vec_all=vm((2, 2, 2, 32, 128), F32),
            wo_grad=vm((48, CW), F32),
            wo_grad_recv=vm((48, CW), F32),
            gc_sem=dma((2, chunks)),
            g1_sem=dma((2, chunks)),
            g2_sem=dma((2, chunks)),
            g3_sem=dma((2, chunks)),
            wo_grad_sem=dma((2, 1)),
        )
    return shapes


def place(*refs):
    ins, outs, held, small, sems = refs[:7], refs[7:22], refs[22:29], refs[29:38], refs[38]
    bring = [pltpu.make_async_copy(far, near, sems.at[k]) for k, (far, near) in enumerate(zip(ins, held))]
    write = [
        pltpu.make_async_copy(near, far, sems.at[7 + k]) for k, (near, far) in enumerate(zip(held[:6] + small, outs))
    ]
    for copy in bring[::-1]:
        copy.start()
    bring[6].wait()
    vec = held[6]
    g_attn_in_bias, g_rel_t = small[:2]
    for ref, at in zip(small[2:], (V_AOB, V_N1G, V_N1B, V_N2G, V_N2B, V_FIB, V_FOB)):
        ref[...] = jnp.concatenate(vec_rows(vec, at, ref.shape[0]), axis=0)
    count = g_attn_in_bias.shape[1] // 128
    for k in range(2):
        g_attn_in_bias[k : k + 1, :] = jnp.concatenate(vec_rows(vec, V_AIB + k * count, count), axis=1)
    reach = g_rel_t.shape[1] // 2
    turned = jnp.concatenate(vec_rows(vec, V_REL, reach), axis=0).T
    g_rel_t[...] = jnp.concatenate([turned[:HD], turned[HD:]], axis=1)
    for copy in write[6:]:
        copy.start()
    for k in range(6):
        bring[k].wait()
        write[k].start()
    for copy in write:
        copy.wait()


def on_device(
    ring,
    hidden, lengths, attn_in, attn_in_bias, rel_table, attn_out, attn_out_bias,
    norm1_gain, norm1_bias, norm2_gain, norm2_bias,
    ffn_in, ffn_in_bias, ffn_out, ffn_out_bias, cotangent,
):
    slots, width = hidden.shape
    local = attn_out.shape[0]
    units = ffn_in.shape[1]
    table_rows = rel_table.shape[0]
    chunks = 2 * units // CW + 5
    rows = width // 16
    shape = jax.ShapeDtypeStruct
    shapes = scratch_of(ring, slots, width, local, units, table_rows, chunks)
    names = tuple(shapes)
    outs = [
        shape((slots, width), BF16), shape((slots, width), BF16), shape((3, rows, local), F32), shape((rows, local), F32),
        shape((rows, units), F32), shape((rows, units), F32), shape((2, 2, 2, 32, 128), F32),
    ]
    far = pl.BlockSpec(memory_space=pl.ANY)
    near = pl.BlockSpec(memory_space=pltpu.VMEM)
    out_specs = [far] * 7
    if not ring:
        names = (FULL,) + names
        outs.append(shape((chunks, width, CW), F32))
        out_specs.append(near)

    def lanes(vector):
        return vector.reshape(vector.shape[0] // 128, 128)

    def unlanes(array):
        return array.reshape(array.shape[0] * 128)

    results = pl.pallas_call(
        partial(body, ring, names),
        out_shape=outs,
        in_specs=[pl.BlockSpec(memory_space=pltpu.SMEM)] + [far] * 15,
        out_specs=out_specs,
        scratch_shapes=list(shapes.values()),
        compiler_params=pltpu.CompilerParams(
            collective_id=0, has_side_effects=True, vmem_limit_bytes=64 * 1024 * 1024
        ),
    )(
        lengths, attn_in_bias, rel_table.T, lanes(attn_out_bias), lanes(norm1_gain), lanes(norm1_bias),
        lanes(norm2_gain), lanes(norm2_bias), lanes(ffn_in_bias), lanes(ffn_out_bias),
        hidden, attn_in, attn_out, ffn_in, ffn_out, cotangent,
    )
    if ring:
        vector = shape((width // 128, 128), F32)
        small = [
            shape((2, local), F32), shape((HD, table_rows), F32), vector, vector, vector, vector, vector,
            shape((units // 128, 128), F32), vector,
        ]
        placed = pl.pallas_call(
            place,
            out_shape=outs[:6] + small,
            in_specs=[far] * 7,
            out_specs=[far] * 15,
            scratch_shapes=[pltpu.VMEM(array.shape, array.dtype) for array in outs + small]
            + [pltpu.SemaphoreType.DMA((22,))],
        )(*results)
        (
            output, grad_hidden, g_attn_in, g_attn_out_t, g_ffn_in, g_ffn_out_t, g_attn_in_bias, g_rel_t,
            g_attn_out_bias, n1g, n1b, n2g, n2b, g_ffn_in_bias, g_ffn_out_bias,
        ) = placed
        return (
            output, grad_hidden, g_attn_in, g_attn_in_bias, g_rel_t.T, g_attn_out_t.T, unlanes(g_attn_out_bias),
            unlanes(n1g), unlanes(n1b), unlanes(n2g), unlanes(n2b),
            g_ffn_in, unlanes(g_ffn_in_bias), g_ffn_out_t.T, unlanes(g_ffn_out_bias),
        )
    output, grad_hidden, vec, full = results[0], results[1], results[6], results[7]

    def wide(which):
        return jnp.concatenate([full[c] for c in which], axis=1)

    def scatter(value, dim, axis="dp"):
        return lax.psum_scatter(value, axis, scatter_dimension=dim, tiled=True)

    g_ffn_out = scatter(wide(OUT_AT).T, 1)
    g_ffn_in = scatter(wide(IN_AT), 0)
    g_attn_out = scatter(scatter(full[WO_AT[0] : WO_AT[1] + 1], 0, "tensor")[0].T, 1)
    g_attn_in = scatter(full[QKV_AT[0] : QKV_AT[2] + 1], 1)
    vec = lax.psum(vec, "dp")

    def row(at, count=width):
        return unlanes(jnp.concatenate(vec_rows(vec, at, count // 128), axis=0))

    rel_pairs = jnp.concatenate(vec_rows(vec, V_REL, table_rows // 2), axis=0)
    grad_rel = jnp.concatenate([rel_pairs[:, :HD], rel_pairs[:, HD:]], axis=0)
    return (
        output, grad_hidden, g_attn_in,
        row(V_AIB, 2 * local).reshape(2, local), grad_rel, g_attn_out, row(V_AOB),
        row(V_N1G), row(V_N1B), row(V_N2G), row(V_N2B),
        g_ffn_in, row(V_FIB, units), g_ffn_out, row(V_FOB),
    )


def solution(mesh):
    ring = mesh.shape["dp"] == 16
    return jax.shard_map(
        partial(on_device, ring),
        mesh=mesh,
        in_specs=(
            P("dp", None), P("dp"), P(None, None, "tensor"), P(None, "tensor"), P(),
            P("tensor", None), P(), P(), P(), P(), P(),
            P(None, "tensor"), P("tensor"), P("tensor", None), P(), P("dp", None),
        ),
        out_specs=(
            P("dp", None), P("dp", None), P(None, "dp", "tensor"), P(None, "tensor"), P(),
            P("tensor", "dp"), P(), P(), P(), P(), P(),
            P("dp", "tensor"), P("tensor"), P("tensor", "dp"), P(),
        ),
        check_vma=False,
    )
```
